32 devices in a mesh: dp: 8 (over y, x, core), seq: 4 (over z).
Axes of the slice: x: 2, y: 2, z: 4, core: 2. Of those that a mesh axis runs over, the one named last changes fastest.
Arguments:
- tokens: bfloat16 [16, 1024, 1536], P('dp', 'seq'), may hold values from -6 to 6
- lengths: int32 [16], P('dp'), may hold values from 1 to 1024, as said below
- in_weight: bfloat16 [1536, 6448], P(('dp', 'seq')), may hold values from -0.15625 to 0.15625
- conv_weight: bfloat16 [3328, 4], P(('dp', 'seq')), may hold values from -3 to 3
- conv_bias: bfloat16 [3328], P(('dp', 'seq')), may hold values from -1.5 to 1.5
- decay_log: float32 [48], replicated, may hold values from -6 to 1
- step_bias: float32 [48], replicated, may hold values from -4.5 to -2.5
- skip_gain: float32 [48], replicated, may hold values from 0.5 to 2
- norm_gain: bfloat16 [1536], P(('dp', 'seq')), may hold values from 0.5 to 1.5
- gate_gain: bfloat16 [3072], P(('dp', 'seq')), may hold values from 0.5 to 1.5
- out_weight: bfloat16 [3072, 1536], P(('dp', 'seq')), may hold values from -0.109375 to 0.109375
- cotangent: bfloat16 [16, 1024, 1536], P('dp', 'seq'), may hold values from -6 to 6
Outputs:
- output: bfloat16 [16, 1024, 1536], P('dp', 'seq')
- token_grad: bfloat16 [16, 1024, 1536], P('dp', 'seq')
- in_weight_grad: float32 [1536, 6448], P(('dp', 'seq'))
- conv_weight_grad: float32 [3328, 4], P(('dp', 'seq'))
- conv_bias_grad: float32 [3328], P(('dp', 'seq'))
- decay_log_grad: float32 [48], replicated
- step_bias_grad: float32 [48], replicated
- skip_gain_grad: float32 [48], replicated
- norm_gain_grad: float32 [1536], P(('dp', 'seq'))
- gate_gain_grad: float32 [3072], P(('dp', 'seq'))
- out_weight_grad: float32 [3072, 1536], P(('dp', 'seq'))
The draws below stay inside these ranges and needn't reach their ends.
Inputs may be any that keep to these rules, and one draw needn't show every extreme that they name: `lengths`: among the 2 sequences of each dp index one, drawn from the seed, has length 1024.
All inputs are finite; a program needn't handle non-finite values.
Results may differ from the reference program's by a relative error of at most 0.0084.
Values may be sent and summed in bfloat16 or wider, within the bound.
A program may use at most 184 MiB of HBM per device.

```python
import jax
import jax.numpy as jnp
from jax import lax

D = 1536
DI = 3072
HEADS = 48
HDIM = 64
STATE = 128
CONV = 4
SEG = 256
SEQ_DEV = 2
PROJ = 6448
CONV_CH = 3328
SEQS = 16
LEN = 1024


def draw_lengths(key, part):
    key = jax.random.fold_in(key, 11)
    first, second = jax.random.split(key)
    ragged = jax.random.randint(first, (SEQS,), 1, LEN + 1)
    chosen = jax.random.randint(second, (SEQS // SEQ_DEV,), 0, SEQ_DEV)
    slots = jnp.arange(SEQS) % SEQ_DEV
    full = jnp.repeat(chosen, SEQ_DEV) == slots
    return jnp.where(full, LEN, ragged).astype(jnp.int32)


def draw_decay_log(key, part):
    key = jax.random.fold_in(key, 23)
    values = jax.random.uniform(key, (HEADS,), jnp.float32, -6.0, 1.0)
    return values


def steps_of(own_key, extent, cuts, least, top_value):
    gain = 1.0
    for dim, parts in cuts:
        heights = jax.random.uniform(jax.random.fold_in(jax.random.fold_in(own_key, 6), dim), (parts,), jnp.float32, least / len(cuts), top_value / len(cuts))
        gain = gain * jnp.repeat(jnp.exp(heights), extent[dim] // parts).reshape((-1,) + (1,) * (len(extent) - 1 - dim))
    return gain


def scatter_about(rng, dims, width, most, cuts=(), kind=jnp.bfloat16):
    drawn = jax.random.normal(rng, dims, jnp.float32) * width
    if len(cuts) > 0:
        drawn = steps_of(rng, dims, cuts, -0.22, 0.18) * drawn
    return jnp.clip(drawn, min=-most, max=most).astype(kind)


def setup_inputs(seed: int = 0) -> dict:
    key_list = jax.random.split(jax.random.key(seed), 13)
    return {
        "tokens": scatter_about(key_list[0], (SEQS, LEN, D), 1.0, 6.0, ((0, 8), (1, 4))),
        "lengths": draw_lengths(jax.random.fold_in(key_list[12], 71), 0),
        "in_weight": scatter_about(key_list[2], (D, PROJ), D ** -0.5, 0.15625, ((0, 32),)),
        "conv_weight": scatter_about(key_list[3], (CONV_CH, CONV), CONV ** -0.5, 3.0, ((0, 32),)),
        "conv_bias": scatter_about(key_list[4], (CONV_CH,), 0.3, 1.5, ((0, 32),)),
        "decay_log": draw_decay_log(jax.random.fold_in(key_list[12], 71), 0),
        "step_bias": jnp.clip(jax.random.uniform(key_list[6], (HEADS,), jnp.float32, -4.5, -2.5), -4.5, -2.5),
        "skip_gain": jnp.clip(jax.random.uniform(key_list[7], (HEADS,), jnp.float32, 0.5, 2.0), 0.5, 2.0),
        "norm_gain": jnp.clip(1.0 + 0.1 * jax.random.normal(key_list[8], (D,), jnp.float32), 0.5, 1.5).astype(jnp.bfloat16),
        "gate_gain": jnp.clip(1.0 + 0.1 * jax.random.normal(key_list[9], (DI,), jnp.float32), 0.5, 1.5).astype(jnp.bfloat16),
        "out_weight": scatter_about(key_list[10], (DI, D), DI ** -0.5, 0.109375, ((0, 32),)),
        "cotangent": scatter_about(key_list[11], (SEQS, LEN, D), 1.0, 6.0, ((0, 8), (1, 4))),
    }


epsilon = 1e-05
highest = lax.Precision.HIGHEST

@jax.custom_vjp
def low(v):
    return lax.optimization_barrier(v.astype(jnp.bfloat16)).astype(jnp.float32)

@jax.custom_vjp
def low_back(v):
    return v

def low_keep(v):
    return (low(v), None)

def low_pass(kept, grad):
    return (grad,)

def back_keep(v):
    return (v, None)

def back_low(kept, grad):
    return (low(grad),)
low.defvjp(low_keep, low_pass)
low_back.defvjp(back_keep, back_low)

def rms_scale(values):
    return lax.rsqrt(lax.optimization_barrier(jnp.mean(values * values, axis=-1, keepdims=True)) + epsilon)

def group_terms(state, values_h, keys_b, reads_c, steps, rates):
    log_decay = jnp.cumsum(steps * rates[None, :], axis=0)
    count = log_decay.shape[0]
    causal = (jnp.arange(count)[:, None] >= jnp.arange(count)[None, :])[:, :, None]
    gaps = jnp.where(causal, log_decay[:, None, :] - log_decay[None, :, :], -1e+30)
    fades = jnp.exp(gaps)
    intersection = jnp.dot(reads_c, keys_b.T, precision=highest)
    scaled = values_h * steps[:, :, None]
    inside = jnp.einsum('ijh,ij,jhp->ihp', fades, intersection, scaled, precision=highest)
    carried = jnp.exp(log_decay)[:, :, None] * jnp.einsum('hpn,in->ihp', state, reads_c, precision=highest)
    tail_fade = jnp.exp(log_decay[-1][None, :] - log_decay)
    new_state = jnp.exp(log_decay[-1])[:, None, None] * state + jnp.einsum('jh,jhp,jn->hpn', tail_fade, scaled, keys_b, precision=highest)
    return (new_state, inside + carried)

def mixer(inputs, in_weight, conv_weight, conv_bias, decay_log, step_bias, skip_gain, norm_gain, gate_gain, out_weight, live):
    count = inputs.shape[0]
    normed = low(inputs * rms_scale(inputs) * norm_gain)
    projected = low_back(jnp.dot(normed, in_weight, precision=highest))
    gate_z = projected[:, :DI]
    conv_in = low(projected[:, DI:2 * DI + 2 * STATE])
    step_raw = projected[:, 2 * DI + 2 * STATE:]
    padded = jnp.concatenate([jnp.zeros((CONV - 1, conv_in.shape[1]), conv_in.dtype), conv_in], axis=0)
    mixed = conv_bias[None, :] + jnp.zeros_like(conv_in)
    for offset in range(CONV):
        mixed = mixed + conv_weight[:, offset][None, :] * padded[offset:offset + count]
    active = jax.nn.silu(mixed)
    values_h = active[:, :DI].reshape(count, HEADS, HDIM)
    keys_b = active[:, DI:DI + STATE]
    reads_c = active[:, DI + STATE:]
    steps = jax.nn.softplus(step_raw + step_bias[None, :])
    rates = -jnp.exp(decay_log)
    blocks = count // SEG

    def advance(state, pieces):
        return group_terms(state, pieces[0], pieces[1], pieces[2], pieces[3], rates)
    start = jnp.zeros((HEADS, HDIM, STATE), jnp.float32)
    final_state, outputs = lax.scan(jax.checkpoint(advance), start, (values_h.reshape(blocks, SEG, HEADS, HDIM), keys_b.reshape(blocks, SEG, STATE), reads_c.reshape(blocks, SEG, STATE), steps.reshape(blocks, SEG, HEADS)))
    mixed_y = outputs.reshape(count, HEADS, HDIM) + skip_gain[None, :, None] * values_h
    gated = mixed_y.reshape(count, DI) * jax.nn.silu(gate_z)
    normed_y = low(gated * rms_scale(gated) * gate_gain)
    branch = jnp.dot(normed_y, out_weight, precision=highest)
    return inputs + live[:, None] * branch

def reference(tokens, lengths, in_weight, conv_weight, conv_bias, decay_log, step_bias, skip_gain, norm_gain, gate_gain, out_weight, cotangent):
    params = (in_weight.astype(jnp.float32), conv_weight.astype(jnp.float32), conv_bias.astype(jnp.float32), decay_log.astype(jnp.float32), step_bias.astype(jnp.float32), skip_gain.astype(jnp.float32), norm_gain.astype(jnp.float32), gate_gain.astype(jnp.float32), out_weight.astype(jnp.float32))
    positions = jnp.arange(LEN)

    def per_sequence(totals, items):
        sequence, length_one, upstream = items
        live = (positions < length_one).astype(jnp.float32)

        def layer(inputs, weights):
            return mixer(inputs, weights[0], weights[1], weights[2], weights[3], weights[4], weights[5], weights[6], weights[7], weights[8], live)
        result, pullback = jax.vjp(layer, sequence.astype(jnp.float32), params)
        input_grad, weight_grads = pullback(upstream.astype(jnp.float32))
        totals = jax.tree.map(jnp.add, totals, weight_grads)
        return (totals, (result.astype(jnp.bfloat16), input_grad.astype(jnp.bfloat16)))
    zeros = jax.tree.map(jnp.zeros_like, params)
    totals, (output, token_grad) = lax.scan(per_sequence, zeros, (tokens, lengths, cotangent))
    return (output, token_grad, totals[0], totals[1], totals[2], totals[3], totals[4], totals[5], totals[6], totals[7], totals[8])
```

```python
import functools
import jax
import jax.numpy as jnp
from jax import lax
from jax.experimental import pallas as pl
from jax.experimental.pallas import tpu as pltpu
from jax.sharding import PartitionSpec as P

D = 1536
DI = 3072
HEADS = 48
HDIM = 64
STATE = 128
CONV = 4
PROJ = 6448
CONV_CH = 3328
CW = 384
GROUPS = DI // CW
GH = CW // HDIM
NI = 1 + 2 * GROUPS
NO = D // CW
MID = 2 + GROUPS
GATE = MID + NO // 2
LATE = GATE + GROUPS
HALO = 16
EPS = 1e-05
MESH = pl.DeviceIdType.MESH
HIGH = lax.Precision.HIGHEST
f32 = jnp.float32
bf16 = jnp.bfloat16
AXES = ("dp", "seq")
LAG = 2
AHEAD = 4


def flip(p, w):
    return p + w * (1 - 2 * lax.rem(lax.div(p, w), 2))


class Place:
    def __init__(self, S, PL):
        self.S, self.PL, self.m = S, PL, PL.bit_length() - 1
        self.d = lax.axis_index("dp")
        self.z = lax.axis_index("seq")
        self.p = lax.div(self.d, 2)
        self.c = lax.rem(self.d, 2)
        self.sib = self.d + 1 - 2 * self.c

    def weight(self, j, h):
        return 2 ** ((j + h) % self.m)

    def held(self, h, j):
        out = [self.p]
        for i in range(j):
            out = out + [flip(q, self.weight(i, h)) for q in out]
        return out

    def across(self, j, h):
        return (2 * flip(self.p, self.weight(j, h)) + self.c, self.z)

    def along(self, o):
        return (self.d, lax.rem(self.z + o, self.S))

    def behind(self, o):
        return lax.rem(self.z - o + self.S, self.S)

    def barrier(self):
        peers = [self.along(o) for o in range(1, self.S)]
        peers += [self.across(j, 0) for j in range(self.m)]
        peers += [(self.sib, self.z)]
        bar = pltpu.get_barrier_semaphore()
        for q in peers:
            pl.semaphore_signal(bar, inc=1, device_id=q, device_id_type=MESH)
        pl.semaphore_wait(bar, len(peers))


def remote(src, dst, ss, rs, to):
    return pltpu.make_async_remote_copy(
        src_ref=src, dst_ref=dst, send_sem=ss, recv_sem=rs, device_id=to, device_id_type=MESH
    )


def picks(rows, R, padded):
    i = lax.broadcasted_iota(jnp.int32, (rows, rows // R * padded), 0)
    j = lax.broadcasted_iota(jnp.int32, (rows, rows // R * padded), 1)
    out = jnp.zeros(i.shape, jnp.bool_)
    for b in range(rows // R):
        inside = (i >= b * R) & (i < b * R + R)
        out = out | (inside & (j - b * padded == i - b * R))
    return jnp.where(out, 1.0, 0.0).astype(bf16)


class Gather:
    def __init__(self, at, sems, arrays):
        self.at = at
        self.zs, self.zr, self.xs, self.xr, self.cs, self.cr = sems
        self.arrays = arrays

    def each(self, k, f):
        for among, fn, land, R in self.arrays:
            if isinstance(k, int):
                if among(k):
                    f(fn(k), R, land and land(k))
            else:
                @pl.when(among(k))
                def _():
                    f(fn(k), R, land and land(k))

    def zcopy(self, ref, R, land, k, o, recv=False):
        at = self.at
        src = at.behind(o) if recv else at.z
        blk = ref.at[pl.ds((at.d * at.S + src) * R, R)] if land is None else land.at[src]
        return remote(blk, blk, self.zs.at[k, o - 1], self.zr.at[k, o - 1], at.along(o))

    def half(self, ref, R, q, c, h):
        n = self.at.S * R // 2
        return ref.at[pl.ds((q * 2 + c) * self.at.S * R + h * n, n)]

    def xcopy(self, ref, R, k, j, i, h, recv=False):
        at = self.at
        q = at.held(h, j)[i]
        if recv:
            q = flip(q, at.weight(j, h))
        blk = self.half(ref, R, q, at.c, h)
        n = (2**j - 1 + i) * 2 + h
        return remote(blk, blk, self.xs.at[k, n], self.xr.at[k, n], at.across(j, h))

    def ccopy(self, ref, R, k, n, h, recv=False):
        at = self.at
        q = at.held(h, at.m)[n]
        blk = self.half(ref, R, q, 1 - at.c if recv else at.c, h)
        return remote(blk, blk, self.cs.at[k, n * 2 + h], self.cr.at[k, n * 2 + h], (at.sib, at.z))

    def send_z(self, k):
        def f(ref, R, land):
            for o in range(1, self.at.S):
                self.zcopy(ref, R, land, k, o).start()

        self.each(k, f)

    def stage(self, k, j):
        def f(ref, R, land):
            if j == 0:
                for o in range(1, self.at.S):
                    self.zcopy(ref, R, land, k, o, True).wait_recv()
                if land is not None:
                    rows = self.at.S * R
                    own = ref.at[pl.ds(pl.multiple_of(self.at.d * rows, 16), rows)]
                    own[...] = dot(picks(rows, R, land.shape[1]), land[...].reshape(-1, land.shape[2])).astype(bf16)
            else:
                for h in range(2):
                    for i in range(2 ** (j - 1)):
                        self.xcopy(ref, R, k, j - 1, i, h, True).wait_recv()
            if j < self.at.m:
                for h in range(2):
                    for i in range(2**j):
                        self.xcopy(ref, R, k, j, i, h).start()
            for h in range(2):
                for n in range(0 if j == 0 else 2 ** (j - 1), 2**j):
                    self.ccopy(ref, R, k, n, h).start()

        self.each(k, f)

    def arrived(self, k):
        def f(ref, R, land):
            for n in range(self.at.PL):
                for h in range(2):
                    self.ccopy(ref, R, k, n, h, True).wait_recv()

        self.each(k, f)

    def sent(self, k):
        def f(ref, R, land):
            for o in range(1, self.at.S):
                self.zcopy(ref, R, land, k, o).wait_send()
            for h in range(2):
                for j in range(self.at.m):
                    for i in range(2**j):
                        self.xcopy(ref, R, k, j, i, h).wait_send()
                for n in range(self.at.PL):
                    self.ccopy(ref, R, k, n, h).wait_send()

        self.each(k, f)


def lanes128(r):
    return jnp.concatenate([r, jnp.zeros((r.shape[0], 128 - r.shape[1]), r.dtype)], axis=1)


def set_heads(heads, decay, bias, skips):
    rows = [bias[...], -jnp.exp(decay[...]), skips[...]]
    heads[...] = jnp.concatenate([lanes128(r) for r in rows] + [jnp.zeros((5, 128), f32)], axis=0)


def sigmoid(v):
    return 1.0 / (1.0 + jnp.exp(-v))


NT = ((1,), (1,))
TN = ((0,), (0,))


def dot(a, b, dims=((1,), (0,)), precision=None):
    return lax.dot_general(a, b, (dims, ((), ())), precision=precision, preferred_element_type=f32)


def halves(v):
    hi = v.astype(bf16)
    return hi, (v - hi.astype(f32)).astype(bf16)


def spread(cols, g6):
    T = cols.shape[0]
    low = lax.broadcasted_iota(jnp.int32, (T, 128), 1) < HDIM
    return jnp.concatenate(
        [
            jnp.where(
                low,
                jnp.broadcast_to(cols[:, 2 * q : 2 * q + 1], (T, 128)),
                jnp.broadcast_to(cols[:, 2 * q + 1 : 2 * q + 2], (T, 128)),
            )
            for q in range(GH // 2)
        ],
        axis=1,
    )


def turned(x, g):
    return pltpu.roll(x, lax.rem(128 - GH * g, 128), 1)


def convolve(x, cp):
    T = x.shape[0] - HALO
    mixed = cp[4:5] + cp[3:4] * x[HALO:]
    for k in range(CONV - 1):
        mixed = mixed + cp[k : k + 1] * pltpu.roll(x, CONV - 1 - k, 0)[HALO:]
    return mixed


def columns(count, first):
    ch = (lax.broadcasted_iota(jnp.int32, (1, CW), 1) + first).astype(f32)
    place = ch - count * jnp.floor((ch + 0.5) / count)
    return jnp.where(lax.broadcasted_iota(jnp.int32, (128, CW), 0).astype(f32) == place, 1.0, 0.0)


def prepare(s, raw, x, heads, cp, ld, ldT, gram):
    T = raw.shape[0]
    steps = jax.nn.softplus(raw + heads[0:1])
    tri = lax.broadcasted_iota(jnp.int32, (T, T), 0) >= lax.broadcasted_iota(jnp.int32, (T, T), 1)
    log_decay = dot(jnp.where(tri, 1.0, 0.0), steps * heads[1:2], precision=HIGH)
    ld[0, s] = log_decay
    ld[1, s] = steps
    turned_ld = log_decay.T
    for g in range(GROUPS):
        ldT[s, g, 0:GH] = turned_ld[g * GH : (g + 1) * GH]
    mixed = convolve(x, cp)[:, : 2 * STATE]
    act = mixed * sigmoid(mixed)
    keys, reads = act[:, :STATE], act[:, STATE:]
    gram[s] = dot(reads, keys, ((1,), (1,)), HIGH)
    return keys, reads, mixed


def fade(ldc, ldr, h, lo, n, m):
    gap = ldc[lo : lo + n, h : h + 1] - ldr[h : h + 1, :m]
    i = lax.broadcasted_iota(jnp.int32, (n, m), 0) + lo
    j = lax.broadcasted_iota(jnp.int32, (n, m), 1)
    return jnp.exp(jnp.where(i >= j, gap, -1e30))


def forward_kernel(S, PL, lengths, tok, win, cw, cb, ng_in, gg_in, decay, bias, skips, wout, cot,
                   out, owin, onormed, opc, oraw, oz, oy, ohin, ony, oconv, ogain, ossq, ong, odny, otsum, old, oldT, ogram, okeys2, oreadsT,
                   wi, wo, sm, zi, zo, halo, normed, ybuf, nyb, loc, hin, hout, dlast, gram, keysT, reads2, keys2, readsT,
                   ld, ldT, convp, gain, ngain, ssq, tsum, heads, pcs, zst, yst,
                   lsem, osem, hsem, ssem, pcsem, zsem, ysem, esem, nsem, cotsem, *sems):
    at = Place(S, PL)
    me = at.d * S + at.z
    seqs, T, _ = tok.shape
    rows = seqs * T
    n = 1 + NI + NO
    nd = S * PL * 2
    RI, RO = D // nd, DI // nd
    packed_i, packed_o = RI % 16 > 0, RO % 16 > 0

    def in_i(k):
        return (k >= 1) & (k < LATE) & ((k < MID) | (k >= GATE))

    def in_o(k):
        return ((k >= MID) & (k < GATE)) | ((k >= LATE) & (k < n))

    def chunk_i(k):
        return k - 1 - (NO // 2) * lax.div(k, GATE)

    def chunk_o(k):
        return k - MID - GROUPS * lax.div(k, LATE)

    ga = Gather(at, sems, [
        (lambda k: k == 0, lambda k: sm, None, 16),
        (in_i, lambda k: wi.at[chunk_i(k)], (lambda k: zi.at[chunk_i(k)]) if packed_i else None, RI),
        (in_o, lambda k: wo.at[chunk_o(k)], (lambda k: zo.at[chunk_o(k)]) if packed_o else None, RO),
    ])

    def local(c):
        return pltpu.make_async_copy(
            wout.at[:, pl.ds(c * CW, CW)], zo.at[c, at.z] if packed_o else wo.at[c, pl.ds(me * RO, RO)], lsem.at[c])

    for c in range(NO):
        local(c).start()
    for j in range(NI):
        lane = 2 * DI if j == 0 else DI + (j - 1) * CW if j <= GROUPS else (j - 1 - GROUPS) * CW
        part = win[:, lane:] if j == 0 else win[:, lane : lane + CW]
        if j == 0:
            part = jnp.concatenate([part, jnp.zeros((part.shape[0], CW - part.shape[1]), bf16)], axis=1)
        if packed_i:
            zi[j, at.z] = part
        else:
            wi[j, pl.ds(pl.multiple_of(me * RI, 16), RI)] = part
    own = [lanes128(r[...].astype(f32)) for r in (cw, cb, ng_in, gg_in)] + [jnp.zeros((9, 128), f32)]
    sm[pl.ds(pl.multiple_of(me * 16, 16), 16)] = jnp.concatenate(own, axis=0).astype(bf16)
    set_heads(heads, decay, bias, skips)
    at.barrier()
    for c in range(NO):
        local(c).wait()
    for k in range(AHEAD):
        ga.send_z(k)

    def halo_copy():
        return remote(tok.at[:, pl.ds(T - HALO, HALO)], halo, hsem.at[0], hsem.at[1], at.along(1))

    @pl.when(at.z < S - 1)
    def _():
        halo_copy().start()

    @pl.when(at.z == 0)
    def _():
        halo[...] = jnp.zeros_like(halo)
        hin[...] = jnp.zeros_like(hin)

    @pl.when(at.z > 0)
    def _():
        halo_copy().wait_recv()

    ssq[...] = jnp.zeros_like(ssq)

    def chain(g):
        return remote(hout.at[g], hin.at[g], ssem.at[0, g], ssem.at[1, g], at.along(1))

    def normed_copies():
        return [pltpu.make_async_copy(normed.at[s, pl.ds(HALO, T), pl.ds(c * CW, CW)],
                                      onormed.at[c, pl.ds(s * T, T)], nsem.at[c, s])
                for c in range(D // CW) for s in range(seqs)]

    def unpack():
        gathered = sm[...]

        def rows_of(count, first):
            wide = dot(gathered, columns(count, first).astype(bf16)).reshape(nd, 16, CW)
            who = lax.broadcasted_iota(jnp.int32, (nd, 1, CW), 0) * count
            at_lane = lax.broadcasted_iota(jnp.int32, (nd, 1, CW), 2) + first
            wide = jnp.where((at_lane >= who) & (at_lane < who + count), wide, 0.0)
            return jnp.sum(wide, axis=0)[:8]

        def group(g, carry):
            convp[1 + g] = rows_of(CONV_CH // nd, g * CW)
            gain[g] = rows_of(DI // nd, g * CW)
            return carry

        lax.fori_loop(0, GROUPS, group, 0)
        convp[0] = rows_of(CONV_CH // nd, DI)
        ng = jnp.concatenate([rows_of(D // nd, g * CW)[5:6] for g in range(D // CW)], axis=1)
        ngain[...] = jnp.broadcast_to(ng, (8, D))
        pltpu.make_async_copy(ngain, ong, esem.at[4 + seqs]).start()
        for s in range(seqs):
            u = halo[s].astype(f32)
            r = lax.rsqrt(jnp.sum(u * u, axis=1, keepdims=True) * (1.0 / D) + EPS)
            normed[s, 0:HALO] = (u * r * ng).astype(bf16)
            for i in range(0, T, 64):
                u = tok[s, i : i + 64].astype(f32)
                r = lax.rsqrt(jnp.sum(u * u, axis=1, keepdims=True) * (1.0 / D) + EPS)
                normed[s, HALO + i : HALO + i + 64] = (u * r * ng).astype(bf16)
        for c in normed_copies():
            c.start()
        pltpu.make_async_copy(convp, oconv, esem.at[2 + seqs]).start()
        pltpu.make_async_copy(gain, ogain, esem.at[3 + seqs]).start()

    def project(w, first):
        x = normed[...] if first == 0 else normed[:, first:]
        return dot(x.reshape(seqs * x.shape[1], D), w).reshape(seqs, x.shape[1], CW)

    def keep_pc(pc, k, slot):
        pcs[slot] = pc
        pltpu.make_async_copy(pcs.at[slot], opc.at[k], pcsem.at[slot]).start()

    def prepared():
        pairs = ((ld, old), (ldT, oldT), (gram, ogram), (keys2, okeys2), (readsT, oreadsT))
        return [pltpu.make_async_copy(a, b, esem.at[seqs + 6 + i]) for i, (a, b) in enumerate(pairs)]

    def first_chunk():
        proj = project(wi[0], 0)
        pc = proj.astype(bf16)
        keep_pc(pc, 0, 0)
        raw = proj[:, HALO:, 2 * STATE :]
        zst[0, :, :, :128] = raw
        pltpu.make_async_copy(zst.at[0, :, :, pl.ds(0, 128)], oraw, zsem.at[0]).start()
        for s in range(seqs):
            keys, reads = prepare(s, raw[s], pc[s].astype(f32), heads, convp[0], ld, ldT, gram)[:2]
            keysT[s] = keys.T
            readsT[s] = reads.T
            reads2[s] = jnp.concatenate(halves(reads), axis=1)
            keys2[s] = jnp.concatenate(halves(keys), axis=1)
        for c in prepared():
            c.start()
        pltpu.make_async_copy(zst.at[0, :, :, pl.ds(0, 128)], oraw, zsem.at[0]).wait()

    def values_chunk(g, k):
        slot = lax.rem(k, 2)

        @pl.when(k >= 2)
        def _():
            pltpu.make_async_copy(pcs.at[slot], opc.at[k - 2], pcsem.at[slot]).wait()

        pc = project(wi[k], 0).astype(bf16)
        keep_pc(pc, k, slot)
        cp = convp[k]
        low = lax.broadcasted_iota(jnp.int32, (T // 2, 128), 1) < HDIM
        skip = spread(turned(jnp.broadcast_to(heads[2:3], (8, 128)), g), 0)[0:1]

        def sequence(s, carry):
            mixed = convolve(pcs[slot, s].astype(f32), cp)
            V = mixed * sigmoid(mixed)
            ldc = turned(ld[0, s], g)
            ldr = ldT[s, g]
            X = V * spread(turned(ld[1, s], g), g)
            lde = spread(ldc, g)
            last = lde[T - 1 : T]
            dlast[g, s] = jnp.broadcast_to(jnp.exp(last), (8, CW))
            loc[g, s] = dot(keysT[s], X * jnp.exp(last - lde), precision=HIGH)
            hi, lo = halves(X)
            H = T // 2
            for q in range(GH // 2):
                sl = slice(q * 128, q * 128 + 128)
                xs = jnp.concatenate([hi[:, sl], lo[:, sl]], axis=1)
                top, bot = [], []
                for h in (2 * q, 2 * q + 1):
                    mt = (gram[s, :H, :H] * fade(ldc, ldr, h, 0, H, H)).astype(bf16)
                    mb = (gram[s, H:, :] * fade(ldc, ldr, h, H, H, T)).astype(bf16)
                    r = dot(mt, xs[:H])
                    top.append(r[:, :128] + r[:, 128:])
                    r = dot(mb, xs)
                    bot.append(r[:, :128] + r[:, 128:])
                ybuf[g, s, :H, sl] = jnp.where(low, top[0], top[1]) + skip[:, sl] * V[:H, sl]
                ybuf[g, s, H:, sl] = jnp.where(low, bot[0], bot[1]) + skip[:, sl] * V[H:, sl]
            return carry

        lax.fori_loop(0, seqs, sequence, 0)

    def pass_state(g):
        @pl.when(at.z > 0)
        def _():
            chain(g).wait_recv()

        @pl.when(at.z < S - 1)
        def _():
            for s in range(seqs):
                hout[g, s] = (dlast[g, s, 0:1] * hin[g, s].astype(f32) + loc[g, s]).astype(bf16)
            chain(g).start()

    def y_copy(i):
        a = lax.rem(i, 2)
        return pltpu.make_async_copy(yst.at[a], oy.at[lax.div(i, seqs), lax.rem(i, seqs)], ysem.at[a])

    def gate_chunk(g, k):
        slot = lax.rem(g, 2)

        @pl.when(g >= 2)
        def _():
            pltpu.make_async_copy(zst.at[slot], oz.at[g - 2], zsem.at[slot]).wait()

        zst[slot] = project(wi[k], HALO)
        pltpu.make_async_copy(zst.at[slot], oz.at[g], zsem.at[slot]).start()

        def sequence(s, carry):
            z = zst[slot, s]
            h2 = jnp.concatenate([hin[g, s], hin[g, s]], axis=0)
            carried = dot(reads2[s], h2) * jnp.exp(spread(turned(ld[0, s], g), g))
            y = ybuf[g, s] + carried
            i = g * seqs + s

            @pl.when(i >= 2)
            def _():
                y_copy(i - 2).wait()

            yst[lax.rem(i, 2)] = y
            y_copy(i).start()
            gated = y * (z * sigmoid(z))
            ybuf[g, s] = gated
            ssq[s] += jnp.broadcast_to(jnp.sum(gated * gated, axis=1, keepdims=True), (T, 128))
            return carry

        lax.fori_loop(0, seqs, sequence, 0)

        @pl.when(g == GROUPS - 1)
        def _():
            for c in normed_copies():
                c.wait()
            cot_copy().start()

    def cot_copy():
        return pltpu.make_async_copy(cot, normed.at[:, pl.ds(0, T)], cotsem.at[0])

    def live(s):
        pos = lax.broadcasted_iota(jnp.int32, (T, 1), 0) + at.z * T
        return jnp.where(pos < lengths[s], 1.0, 0.0)

    def normalise():
        for s in range(seqs):
            r = lax.rsqrt(ssq[s, :, 0:1] * (1.0 / DI) + EPS)
            for g in range(GROUPS):
                nyb[g, s * T : (s + 1) * T] = (ybuf[g, s] * r * gain[g, 6:7]).astype(bf16)
                ybuf[g, s] = jnp.zeros((T, CW), f32)
        pltpu.make_async_copy(nyb, ony, esem.at[seqs]).start()
        pltpu.make_async_copy(hin, ohin, esem.at[seqs + 1]).start()
        pltpu.make_async_copy(ssq, ossq, esem.at[seqs + 5]).start()
        cot_copy().wait()
        for s in range(seqs):
            normed[s, 0:T] = (live(s) * normed[s, 0:T].astype(f32)).astype(bf16)

    def out_chunk(c, carry):
        branch = dot(nyb[0], wo[c, :CW])
        for g in range(1, GROUPS):
            branch = branch + dot(nyb[g], wo[c, g * CW : (g + 1) * CW])
        branch = branch.reshape(seqs, T, CW)
        lane = pl.ds(pl.multiple_of(c * CW, 128), CW)
        masked = normed[:, 0:T, lane].reshape(rows, CW)
        for s in range(seqs):
            out[s, :, lane] = (tok[s, :, lane].astype(f32) + live(s) * branch[s]).astype(bf16)

        def upstream(g, carry):
            part = wo[c, pl.ds(pl.multiple_of(g * CW, 16), CW)]
            ybuf[g] += dot(masked, part, NT).reshape(seqs, T, CW)
            return carry

        lax.fori_loop(0, GROUPS, upstream, 0)

        @pl.when(c == NO - 1)
        def _():
            pltpu.make_async_copy(ybuf, odny, esem.at[0]).start()
            for s in range(seqs):
                t = jnp.zeros((T, 1), f32)
                for g in range(GROUPS):
                    t = t + jnp.sum(ybuf[g, s] * nyb[g, s * T : (s + 1) * T].astype(f32), axis=1, keepdims=True)
                tsum[s] = jnp.broadcast_to(t, (T, 128))
            pltpu.make_async_copy(tsum, otsum, esem.at[1]).start()

        return carry

    def keep(k, start):
        def f(src, dst):
            cp = pltpu.make_async_copy(src, dst, osem.at[k])
            cp.start() if start else cp.wait()

        @pl.when(in_i(k))
        def _():
            f(wi.at[chunk_i(k)], owin.at[chunk_i(k)])

    HOP = 3 if S <= 4 else 1
    last = at.m * LAG + 1

    def tick(t, carry):
        ga.send_z(t + AHEAD)
        for j in range(at.m + 1):
            ga.stage(t - j * LAG, j)
        k = t - last
        ga.arrived(k)
        keep(k, True)
        pl.when(k == 0)(unpack)
        pl.when(k == 1)(first_chunk)
        pl.when((k >= 2) & (k < MID))(lambda: values_chunk(k - 2, k - 1))
        g = k - 3 - HOP * at.z
        pl.when((g >= 0) & (g < GROUPS))(lambda: pass_state(g))
        pl.when((k >= GATE) & (k < LATE))(lambda: gate_chunk(k - GATE, k - GATE + 1 + GROUPS))

        pl.when(k == LATE)(normalise)
        late = jnp.clip(k - LATE, -1, NO - NO // 2 - 1)
        begin = jnp.where(late > 0, late + NO // 2, 0)
        end = jnp.where(late >= 0, late + NO // 2 + 1, 0)
        lax.fori_loop(begin, end, out_chunk, 0)

        return carry

    lax.fori_loop(0, n + last, tick, 0)

    def finish(k, carry):
        ga.sent(k)
        keep(k, False)
        return carry

    lax.fori_loop(0, n, finish, 0)

    @pl.when(at.z < S - 1)
    def _():
        halo_copy().wait_send()

        def f(g, carry):
            chain(g).wait_send()
            return carry

        lax.fori_loop(0, GROUPS, f, 0)

    for k in (GROUPS - 1, GROUPS):
        pltpu.make_async_copy(pcs.at[k % 2], opc.at[k], pcsem.at[k % 2]).wait()
    for g in (GROUPS - 2, GROUPS - 1):
        pltpu.make_async_copy(zst.at[g % 2], oz.at[g], zsem.at[g % 2]).wait()
    for c in prepared():
        c.wait()
    pltpu.make_async_copy(ybuf, odny, esem.at[0]).wait()
    pltpu.make_async_copy(tsum, otsum, esem.at[1]).wait()
    for i in (seqs * GROUPS - 2, seqs * GROUPS - 1):
        y_copy(i).wait()
    pltpu.make_async_copy(nyb, ony, esem.at[seqs]).wait()
    pltpu.make_async_copy(hin, ohin, esem.at[seqs + 1]).wait()
    pltpu.make_async_copy(convp, oconv, esem.at[seqs + 2]).wait()
    pltpu.make_async_copy(gain, ogain, esem.at[seqs + 3]).wait()
    pltpu.make_async_copy(ngain, ong, esem.at[seqs + 4]).wait()
    pltpu.make_async_copy(ssq, ossq, esem.at[seqs + 5]).wait()


def forward(S, dp, lengths, tok, win, wout, small, cot):
    PL = dp // 2
    nd = S * dp
    seqs, T, _ = tok.shape
    n = 1 + NI + NO
    rows = seqs * T
    sds = jax.ShapeDtypeStruct
    dma = pltpu.SemaphoreType.DMA
    V = pltpu.VMEM

    vm = pl.BlockSpec(memory_space=pltpu.VMEM)
    hb = pl.BlockSpec(memory_space=pl.ANY)
    wi_s, wo_s = (NI, D, CW), (NO, DI, CW)
    RI, RO = -(-(D // nd) // 16) * 16, -(-(DI // nd) // 16) * 16
    win = jnp.pad(win, ((0, RI - D // nd), (0, 0)))
    wout = jnp.pad(wout, ((0, RO - DI // nd), (0, 0)))
    zi_s = (NI, S, RI, CW) if RI * nd > D else (8, 128)
    zo_s = (NO, S, RO, CW) if RO * nd > DI else (8, 128)
    return pl.pallas_call(
        functools.partial(forward_kernel, S, PL),
        out_shape=[
            sds((seqs, T, D), bf16), sds(wi_s, bf16), sds((D // CW, rows, CW), bf16),
            sds((1 + GROUPS, seqs, HALO + T, CW), bf16), sds((seqs, T, 128), f32),
            sds((GROUPS, seqs, T, CW), f32), sds((GROUPS, seqs, T, CW), f32),
            sds((GROUPS, seqs, STATE, CW), bf16), sds((GROUPS, rows, CW), bf16),
            sds((1 + GROUPS, 8, CW), f32), sds((GROUPS, 8, CW), f32),
            sds((seqs, T, 128), f32), sds((8, D), f32), sds((GROUPS, seqs, T, CW), f32), sds((seqs, T, 128), f32),
            sds((2, seqs, T, 128), f32), sds((seqs, GROUPS, 8, T), f32), sds((seqs, T, T), f32),
            sds((seqs, T, 2 * STATE), bf16), sds((seqs, STATE, T), f32),
        ],
        in_specs=[pl.BlockSpec(memory_space=pltpu.SMEM)] + [vm] * 9 + [hb] * 2,
        out_specs=[vm] + [hb] * 19,
        scratch_shapes=[
            V(wi_s, bf16), V(wo_s, bf16), V((nd * 16, 128), bf16), V(zi_s, bf16), V(zo_s, bf16), V((seqs, HALO, D), bf16),
            V((seqs, HALO + T, D), bf16), V((GROUPS, seqs, T, CW), f32), V((GROUPS, rows, CW), bf16),
            V((GROUPS, seqs, STATE, CW), f32), V((GROUPS, seqs, STATE, CW), bf16),
            V((GROUPS, seqs, STATE, CW), bf16), V((GROUPS, seqs, 8, CW), f32), V((seqs, T, T), f32),
            V((seqs, STATE, T), f32), V((seqs, T, 2 * STATE), bf16), V((seqs, T, 2 * STATE), bf16),
            V((seqs, STATE, T), f32), V((2, seqs, T, 128), f32),
            V((seqs, GROUPS, 8, T), f32), V((1 + GROUPS, 8, CW), f32), V((GROUPS, 8, CW), f32), V((8, D), f32),
            V((seqs, T, 128), f32), V((seqs, T, 128), f32), V((8, 128), f32), V((2, seqs, HALO + T, CW), bf16),
            V((2, seqs, T, CW), f32), V((2, T, CW), f32),
            dma((NO,)), dma((n,)), dma((2,)), dma((2, GROUPS)), dma((2,)), dma((2,)), dma((2,)), dma((seqs + 11,)), dma((D // CW, seqs)), dma((1,)),
            dma((n, S - 1)), dma((n, S - 1)), dma((n, 2 * PL - 2)), dma((n, 2 * PL - 2)), dma((n, 2 * PL)), dma((n, 2 * PL)),
        ],
        name="forward",
        compiler_params=pltpu.CompilerParams(collective_id=0, has_side_effects=True, vmem_limit_bytes=63 << 20),
    )(lengths, tok, win, *small, wout, cot)


class Scatter:
    def __init__(self, at, R, bufs, sems):
        self.at, self.R, self.SR = at, R, at.S * R
        self.acc, self.cS, self.cR, self.xS, self.xR, self.zS, self.zR, self.zown = bufs
        self.cs, self.cr, self.xs, self.xr, self.zs, self.zr = sems
        self.NA, self.NS, self.NB = self.acc.shape[0], self.xS.shape[0], self.xR.shape[0]
        self.NC, self.MC = self.cR.shape[0], self.cS.shape[0]
        self.NZ, self.MZ = self.zR.shape[0], self.zS.shape[0]
        self.kind = self.xS.dtype

    def ccopy(self, k):
        at, i, o = self.at, lax.rem(k, self.MC), lax.rem(k, self.NC)
        return remote(self.cS.at[i], self.cR.at[o], self.cs.at[i], self.cr.at[o], (at.sib, at.z))

    def xcopy(self, k, j, i, h):
        at, n = self.at, 2**j - 1 + i
        a, b = lax.rem(k, self.NS), lax.rem(k, self.NB)
        return remote(self.xS.at[a, h, n], self.xR.at[b, h, n], self.xs.at[a, h, n], self.xr.at[b, h, n], at.across(j, h))

    def zcopy(self, k, o):
        at = self.at
        a, b = lax.rem(k, self.MZ), lax.rem(k, self.NZ)
        return remote(self.zS.at[a, lax.rem(at.z + o, at.S)], self.zR.at[b, o - 1], self.zs.at[a, o - 1],
                      self.zr.at[b, o - 1], at.along(o))

    def ready(self, k, slots, wait):
        if isinstance(k, int):
            if k >= slots:
                wait()
        else:
            pl.when(k >= slots)(wait)

    def produce(self, k, sibling, own):
        self.ready(k, self.MC, lambda: self.ccopy(k - self.MC).wait_send())
        a, n = lax.rem(k, self.MC), lax.rem(k, self.NA)
        sibling(self.cS.at[a])
        self.ccopy(k).start()
        own(self.acc.at[n])

    def send_x(self, k, j):
        at, n, a, half = self.at, lax.rem(k, self.NA), lax.rem(k, self.NS), self.SR // 2
        for h in range(2):
            for i in range(2**j):
                self.ready(k, self.NS, lambda: self.xcopy(k - self.NS, j, i, h).wait_send())
                q = flip(at.held(h, j)[i], at.weight(j, h))
                self.xS[a, h, 2**j - 1 + i] = self.acc[n, q, h * half : (h + 1) * half].astype(self.kind)
                self.xcopy(k, j, i, h).start()

    def stage_c(self, k):
        self.ccopy(k).wait_recv()
        n, o = lax.rem(k, self.NA), lax.rem(k, self.NC)
        for q in range(self.at.PL):
            self.acc[n, q] += self.cR[o, q]
        self.send_x(k, self.at.m - 1)

    def stage_x(self, k, j):
        at, n, b, half = self.at, lax.rem(k, self.NA), lax.rem(k, self.NB), self.SR // 2
        for h in range(2):
            for i in range(2**j):
                self.xcopy(k, j, i, h).wait_recv()
                q = at.held(h, j)[i]
                self.acc[n, q, h * half : (h + 1) * half] += self.xR[b, h, 2**j - 1 + i].astype(f32)
        if j > 0:
            self.send_x(k, j - 1)
            return
        a = lax.rem(k, self.MZ)
        for o in range(1, at.S):
            self.ready(k, self.MZ, lambda: self.zcopy(k - self.MZ, o).wait_send())
        v = self.acc[n, at.p]
        padded = self.zS.shape[2]
        if padded == self.R:
            self.zS[a] = v.astype(self.kind).reshape(at.S, self.R, v.shape[1])
        else:
            spread_rows = dot(picks(self.SR, self.R, padded), v.astype(bf16), ((0,), (0,)))
            self.zS[a] = spread_rows.astype(self.kind).reshape(at.S, padded, v.shape[1])
        for o in range(1, at.S):
            self.zcopy(k, o).start()
        if padded == self.R:
            own = self.acc[n, at.p, pl.ds(pl.multiple_of(at.z * self.R, 8), self.R)]
        else:
            i = lax.broadcasted_iota(jnp.int32, (padded, self.SR), 0)
            j = lax.broadcasted_iota(jnp.int32, (padded, self.SR), 1)
            mine = (i < self.R) & (j == i + at.z * self.R)
            own = dot(jnp.where(mine, 1.0, 0.0), v, precision=HIGH)
        self.zown[a] = own

    def stage_z(self, k):
        b = lax.rem(k, self.NZ)
        total = self.zown[lax.rem(k, self.MZ)]
        for o in range(1, self.at.S):
            self.zcopy(k, o).wait_recv()
            total = total + self.zR[b, o - 1].astype(f32)
        return total

    def drain(self, n):
        for k in range(max(0, n - self.MC), n):
            self.ccopy(k).wait_send()
        for k in range(max(0, n - self.NS), n):
            for h in range(2):
                for j in range(self.at.m):
                    for i in range(2**j):
                        self.xcopy(k, j, i, h).wait_send()
        for k in range(max(0, n - self.MZ), n):
            for o in range(1, self.at.S):
                self.zcopy(k, o).wait_send()


def scatter_scratch(S, PL, R, padded, width, kind, many, lag, zlag):
    m = PL.bit_length() - 1
    SR = S * R
    NS, NB, NC, NA, MZ, NZ = (lag + 1, 2 * lag, 2, 1 + m * lag, zlag + 1, 2 * zlag) if many else (1,) * 6
    V, dma = pltpu.VMEM, pltpu.SemaphoreType.DMA
    bufs = [
        V((NA, PL, SR, width), f32), V((1, PL, SR, width), f32), V((NC, PL, SR, width), f32),
        V((NS, 2, PL - 1, SR // 2, width), kind), V((NB, 2, PL - 1, SR // 2, width), kind),
        V((MZ, S, padded, width), kind), V((NZ, S - 1, padded, width), kind), V((MZ, padded, width), f32),
    ]
    sems = [dma((1,)), dma((NC,)), dma((NS, 2, PL - 1)), dma((NB, 2, PL - 1)), dma((MZ, S - 1)), dma((NZ, S - 1))]
    return bufs, sems


def pair(cols, q):
    T = cols.shape[0]
    low = lax.broadcasted_iota(jnp.int32, (T, 128), 1) < HDIM
    first = jnp.broadcast_to(cols[:, 2 * q : 2 * q + 1], (T, 128))
    second = jnp.broadcast_to(cols[:, 2 * q + 1 : 2 * q + 2], (T, 128))
    return jnp.where(low, first, second)


def pair_sums(v, q):
    hi = v.astype(bf16)
    rest = v - hi.astype(f32)
    mid = rest.astype(bf16)
    low = (rest - mid.astype(f32)).astype(bf16)
    ch = lax.broadcasted_iota(jnp.int32, (128, 128), 0)
    hd = lax.broadcasted_iota(jnp.int32, (128, 128), 1) - 2 * q
    ones = jnp.where((ch >= hd * HDIM) & (ch < hd * HDIM + HDIM), 1.0, 0.0).astype(bf16)
    return dot(jnp.concatenate([hi, mid, low], axis=1), jnp.concatenate([ones, ones, ones], axis=0))


def turned_back(x, g):
    return pltpu.roll(x, GH * g, 1)


def backward_kernel(S, PL, RLAG, ZLAG, lengths, decay, bias, skips, ngain, gain, convp, raw, ssq, tsum, ld, ldT, gram, keys2, readsT,
                    tok, cot, hin, norm_in, ny, win, zin, yin, dyin, pcin,
                    tgrad, ghead, gin, gout, gsm,
                    masked, lhsT, dyb, dzb, loc, dsin, dsout, dn, dgram, dkeys, dreads,
                    dld, dst, cvec, gvec, hvec, nxt, dcv, fin, heads, pc0, wib, zb, yb, db, hb, pcb,
                    wisem, zsem, ysem, dsem, hinsem, pcsem, setsem, finsem, chsem, hasem, *rest):
    at = Place(S, PL)
    seqs, T, _ = raw.shape
    rows = seqs * T
    nd = S * PL * 2
    R = D // nd
    SR = S * R
    H = T // 2
    NQ = 2 * GROUPS + 1 + 2 * NO
    big = Scatter(at, R, rest[:8], rest[8:14])
    tiny = Scatter(at, 16, rest[14:22], rest[22:28])
    sg = rest[28]
    HOP = 2 if S <= 4 else 1
    TB = 2 + HOP * (S - 1)

    def wi_copy(i):
        a = lax.rem(i, 2)
        k = 9 + i - 16 * lax.div(i, 8) + 7 * lax.div(i, 16)
        return pltpu.make_async_copy(win.at[k], wib.at[a], wisem.at[a])

    def item(i):
        return lax.rem(lax.div(i, seqs), GROUPS), lax.rem(i, seqs)

    def y_copy(i):
        a = lax.rem(i, 2)
        return pltpu.make_async_copy(yin.at[item(i)], yb.at[a], ysem.at[a])

    def zy_copies(i):
        a = lax.rem(i, 2)
        return (pltpu.make_async_copy(zin.at[item(i)], zb.at[a], zsem.at[a]),
                pltpu.make_async_copy(dyin.at[item(i)], db.at[a], dsem.at[a]), y_copy(i))

    def b_copies(g):
        a = lax.rem(g, 2)
        return (pltpu.make_async_copy(hin.at[g], hb.at[a], hinsem.at[a]),
                pltpu.make_async_copy(pcin.at[g + 1], pcb.at[a], pcsem.at[a]))

    def begin(copies, when=True):
        if when is True:
            for c in copies:
                c.start()
        else:
            @pl.when(when)
            def _():
                for c in copies:
                    c.start()

    NCH = D // CW
    setup = [pltpu.make_async_copy(cot, tgrad, setsem.at[0]), pltpu.make_async_copy(ny, dzb, setsem.at[1])]
    setup.append(pltpu.make_async_copy(pcin.at[0], pc0, setsem.at[2 + NCH]))
    setup += [pltpu.make_async_copy(norm_in.at[c], wib.at[c // 3, pl.ds(c % 3 * rows, rows)], setsem.at[2 + c])
              for c in range(NCH)]
    begin([*setup, *zy_copies(0), *b_copies(0)])
    set_heads(heads, decay, bias, skips)
    at.barrier()
    for c in setup:
        c.wait()

    for s in range(seqs):
        live = jnp.where(lax.broadcasted_iota(jnp.int32, (T, 1), 0) + at.z * T < lengths[s], 1.0, 0.0)
        masked[s * T : (s + 1) * T] = (live * tgrad[s].astype(f32)).astype(bf16)
    perm = lax.broadcasted_iota(jnp.int32, (2 * SR, 2 * SR), 0)
    perm_j = lax.broadcasted_iota(jnp.int32, (2 * SR, 2 * SR), 1)
    take = jnp.zeros(perm.shape, jnp.bool_)
    for h in range(2):
        for b in range(S):
            inside = (perm >= h * SR + b * R) & (perm < h * SR + b * R + R)
            take = take | (inside & (perm_j - (2 * b + h) * R == perm - (h * SR + b * R)))
    take = jnp.where(take, 1.0, 0.0).astype(bf16)
    same = jnp.where(lax.broadcasted_iota(jnp.int32, (SR, SR), 0) == lax.broadcasted_iota(jnp.int32, (SR, SR), 1),
                     1.0, 0.0).astype(bf16)
    for q in range(PL):
        for cls in range(2):
            cc = 1 - at.c if cls == 0 else at.c
            slab = 2 * q + cls
            for s in range(seqs):
                tl = slice(s * T, (s + 1) * T)
                lane = slab * 2 * SR
                r = dot(take, dzb[lane // CW, tl, lane % CW : lane % CW + 2 * SR], NT).astype(bf16)
                lhsT[0, cc, q * SR : (q + 1) * SR, tl] = r[:SR]
                lhsT[1, cc, q * SR : (q + 1) * SR, tl] = r[SR:]

    def turn_normed():
        for q in range(PL):
            for cls in range(2):
                cc = 1 - at.c if cls == 0 else at.c
                lane, c = (2 * q + cls) * SR % CW, (2 * q + cls) * SR // CW
                for s in range(seqs):
                    part = wib[c // 3, c % 3 * rows + s * T : c % 3 * rows + (s + 1) * T, lane : lane + SR]
                    lhsT[2, cc, q * SR : (q + 1) * SR, s * T : (s + 1) * T] = dot(same, part, NT).astype(bf16)
        begin([wi_copy(0)])


    for ref in (dn, dgram, dkeys, dreads, dld, dst, cvec, gvec, hvec, sg):
        ref[...] = jnp.zeros_like(ref)

    @pl.when(at.z == S - 1)
    def _():
        dsin[...] = jnp.zeros_like(dsin)
        nxt[...] = jnp.zeros_like(nxt)

    def rms(s):
        return lax.rsqrt(ssq[s, :, 0:1] * (1.0 / DI) + EPS)

    def through_gate(g, carry):
        def sequence(s, carry):
            i = g * seqs + s
            a = lax.rem(i, 2)
            for c in zy_copies(i):
                c.wait()
            begin(zy_copies(i + 1)[:2], i + 1 < seqs * GROUPS)
            begin([y_copy(i + 1)])
            r = rms(s)
            z, y, dn_y = zb[a], yb[a], db[a]
            sg_ = sigmoid(z)
            gate = z * sg_
            w = (y * gate) * r
            gvec[g, 6:7] += jnp.sum(dn_y * w, axis=0, keepdims=True)
            dw = r * (dn_y * gain[g, 6:7] - w * (tsum[s, :, 0:1] * (1.0 / DI)))
            dzb[g, pl.ds(pl.multiple_of(s * T, 16), T)] = (dw * y * (sg_ * (1.0 + z * (1.0 - sg_)))).astype(bf16)
            dy = dw * gate
            dyb[g, s] = dy
            loc[g, s] = dot(readsT[s], dy * jnp.exp(spread(turned(ld[0, s], g), g)), precision=HIGH)
            return carry

        lax.fori_loop(0, seqs, sequence, 0)
        return 0

    def chain(g):
        return remote(dsout.at[g], dsin.at[g], chsem.at[0, g], chsem.at[1, g], at.along(S - 1))

    def pass_state(g):
        @pl.when(at.z < S - 1)
        def _():
            chain(g).wait_recv()

        @pl.when(at.z > 0)
        def _():
            for s in range(seqs):
                last = jnp.exp(spread(turned(ld[0, s, T - 8 :], g), g))[7:8]
                dsout[g, s] = (last * dsin[g, s].astype(f32) + loc[g, s]).astype(bf16)
            chain(g).start()

    def edge(g):
        return remote(dyb.at[g, :, pl.ds(0, 8)], nxt.at[g], hasem.at[0, g], hasem.at[1, g], at.along(S - 1))

    def conv_sums(g, x, dm, lanes):
        x = x[:, :lanes]
        for k in range(CONV):
            shifted = x[HALO:] if k == CONV - 1 else pltpu.roll(x, CONV - 1 - k, 0)[HALO:]
            cvec[g, k : k + 1, :lanes] += jnp.sum(dm * shifted, axis=0, keepdims=True)
        cvec[g, CONV : CONV + 1, :lanes] += jnp.sum(dm, axis=0, keepdims=True)

    def recurrence(i, carry):
        g, s = lax.div(i, seqs), lax.rem(i, seqs)
        a = lax.rem(g, 2)

        @pl.when(s == 0)
        def _():
            for c in b_copies(g):
                c.wait()
            begin(b_copies(g + 1), g + 1 < GROUPS)

        y_copy(i).wait()
        begin([y_copy(i + 1)], i + 1 < seqs * GROUPS)

        cp = convp[g + 1]
        low = lax.broadcasted_iota(jnp.int32, (T, 128), 1) < HDIM
        is_last = lax.broadcasted_iota(jnp.int32, (T, 128), 0) == T - 1
        skips = turned(jnp.broadcast_to(heads[2:3], (8, 128)), g)
        ldc, ldr, stc = turned(ld[0, s], g), ldT[s, g], turned(ld[1, s], g)
        dgt, dgb = jnp.zeros((H, H), f32), jnp.zeros((H, T), f32)
        sums, dk, dr = jnp.zeros((2 * T, 128), f32), jnp.zeros((T, STATE), f32), jnp.zeros((T, STATE), f32)
        for q in range(GH // 2):
            sl = slice(q * 128, q * 128 + 128)
            skip = pair(skips, q)[0:1]
            x = pcb[a, s, :, sl].astype(f32)
            mixed = convolve(x, cp[:, sl])
            sg_ = sigmoid(mixed)
            V = mixed * sg_
            lde, st = pair(ldc, q), pair(stc, q)
            last = lde[T - 1 : T]
            tail = jnp.exp(last - lde)
            X = V * st
            dS, hq = dsin[g, s, :, sl], hb[a, s, :, sl]
            dXt = tail * dot(keys2[s], jnp.concatenate([dS, dS], axis=0))
            dY = dyb[g, s, :, sl]
            xh = X.astype(bf16)
            x2 = jnp.concatenate([xh, xh], axis=1)
            dyp = jnp.concatenate(halves(dY), axis=1)
            two = []
            for h in (2 * q, 2 * q + 1):
                ft = fade(ldc, ldr, h, 0, H, H)
                fb = fade(ldc, ldr, h, H, H, T)
                mt = (gram[s, :H, :H] * ft).astype(bf16)
                mb = (gram[s, H:, :] * fb).astype(bf16)
                r0 = dot(jnp.concatenate([mt, mb[:, :H]], axis=0), dyp, TN)
                r1 = dot(mb[:, H:], dyp[H:], TN)
                r = jnp.concatenate([r0, r1], axis=0)
                two.append(r[:, :128] + r[:, 128:])
                mine = low if h == 2 * q else jnp.logical_not(low)
                dyh = jnp.concatenate(halves(jnp.where(mine, dY, 0.0)), axis=1)
                dgt = dgt + ft * dot(dyh[:H], x2[:H], NT)
                dgb = dgb + fb * dot(dyh[H:], x2, NT)
            dX = jnp.where(low, two[0], two[1]) + dXt
            dV = st * dX + skip * dY
            gvec[g, 7:8, sl] += jnp.sum(dY * V, axis=0, keepdims=True)
            q1 = dY * (yb[lax.rem(i, 2), :, sl] - skip * V) - X * dX
            at_end = jnp.sum(X * dXt, axis=0, keepdims=True) + jnp.exp(last) * jnp.sum(
                hq.astype(f32) * dS.astype(f32), axis=0, keepdims=True)
            q1 = q1 + jnp.where(is_last, at_end, 0.0)
            sums = sums + pair_sums(jnp.concatenate([q1, dX * V], axis=0), q)
            dk = dk + dot(jnp.concatenate(halves(tail * X), axis=1), jnp.concatenate([dS, dS], axis=1), NT)
            dr = dr + dot(jnp.concatenate(halves(dY * jnp.exp(lde)), axis=1), jnp.concatenate([hq, hq], axis=1), NT)
            dm = dV * (sg_ * (1.0 + mixed * (1.0 - sg_)))
            dyb[g, s, :, sl] = dm
            for k in range(CONV):
                shifted = x[HALO:] if k == CONV - 1 else pltpu.roll(x, CONV - 1 - k, 0)[HALO:]
                cvec[g + 1, k : k + 1, sl] += jnp.sum(dm * shifted, axis=0, keepdims=True)
            cvec[g + 1, CONV : CONV + 1, sl] += jnp.sum(dm, axis=0, keepdims=True)
        dgram[s, :H, :H] += dgt
        dgram[s, H:, :] += dgb
        dld[s] += turned_back(sums[:T], g)
        dst[s] += turned_back(sums[T:], g)
        dkeys[s] += dk
        dreads[s] += dr

        @pl.when((at.z > 0) & (s == seqs - 1))
        def _():
            edge(g).start()

        return carry

    def unconvolve(dm, after, cp):
        ext = jnp.concatenate([dm, after], axis=0)
        n = ext.shape[0]
        out = cp[3:4] * dm
        for k in range(CONV - 1):
            out = out + cp[k : k + 1] * pltpu.roll(ext, n - (CONV - 1 - k), 0)[: dm.shape[0]]
        return out

    def heads_chunk():
        tri = lax.broadcasted_iota(jnp.int32, (T, T), 1) >= lax.broadcasted_iota(jnp.int32, (T, T), 0)
        tri = jnp.where(tri, 1.0, 0.0)
        cp = convp[0]
        for s in range(seqs):
            x = pc0[s].astype(f32)
            mixed = convolve(x, cp)[:, : 2 * STATE]
            sg_ = sigmoid(mixed)
            act = mixed * sg_
            keys, reads = act[:, :STATE], act[:, STATE:]
            dr = dreads[s] + dot(dgram[s], keys, precision=HIGH)
            dk = dkeys[s] + dot(dgram[s], reads, TN, HIGH)
            dm = jnp.concatenate([dk, dr], axis=1) * (sg_ * (1.0 + mixed * (1.0 - sg_)))
            conv_sums(0, x, dm, 2 * STATE)
            da = dot(tri, dld[s], precision=HIGH)
            draw = (dst[s] + da * heads[1:2]) * sigmoid(raw[s] + heads[0:1])
            hvec[0:1] += jnp.sum(da * ld[1, s], axis=0, keepdims=True) * heads[1:2]
            hvec[1:2] += jnp.sum(draw, axis=0, keepdims=True)
            zb[s] = jnp.concatenate([dm, draw], axis=1)

        @pl.when(at.z > 0)
        def _():
            kr_edge().start()

    def kr_edge():
        return remote(zb.at[:, pl.ds(0, 8)], nxt.at[GROUPS], hasem.at[0, GROUPS], hasem.at[1, GROUPS], at.along(S - 1))

    def terms(k):
        rhs = dcv[...]
        lhs = lhsT.at[jnp.minimum(lax.div(k, NO), 2)]

        def product(cc, ref):
            for lo in range(0, PL * SR, 384):
                ref[lo // SR : (lo + 384) // SR] = dot(lhs[cc, lo : lo + 384], rhs).reshape(384 // SR, SR, CW)

        def sibling(ref):
            product(0, ref)

        def own(ref):
            product(1, ref)

        big.produce(k, sibling, own)

    def back_in(i, d):
        wi_copy(i).wait()
        begin([wi_copy(i + 1)], i + 1 < 2 * GROUPS + 1)
        for lane in range(0, D, 512):
            dn[:, lane : lane + 512] += dot(d, wib[lax.rem(i, 2), lane : lane + 512], NT)

    def out_terms(k):
        c = lax.rem(k, NO)
        dcv[...] = masked[:, pl.ds(pl.multiple_of(c * CW, 128), CW)]

    def gate_terms(k):
        dcv[...] = dzb[k - 2 * NO]

    def value_terms(k):
        g = k - 2 * NO - GROUPS

        @pl.when(at.z < S - 1)
        def _():
            edge(g).wait_recv()

        cp = convp[g + 1]
        for s in range(seqs):
            dcv[s * T : (s + 1) * T] = unconvolve(dyb[g, s], nxt[g, s], cp).astype(bf16)

    def first_terms(k):
        @pl.when(at.z < S - 1)
        def _():
            kr_edge().wait_recv()

        cp = convp[0]
        for s in range(seqs):
            v = zb[s]
            c = unconvolve(v, nxt[GROUPS, s], cp)
            is_conv = lax.broadcasted_iota(jnp.int32, (T, CW), 1) < 2 * STATE
            dcv[s * T : (s + 1) * T] = jnp.where(is_conv, c, v).astype(bf16)

    def place(vec, count, first):
        lo, hi = first // count, min(nd - 1, (first + CW - 1) // count)
        who = (lax.broadcasted_iota(jnp.int32, (hi - lo + 1, 1, CW), 0) + lo) * count
        ch = lax.broadcasted_iota(jnp.int32, (hi - lo + 1, 1, CW), 2) + first
        wide = jnp.where((ch >= who) & (ch < who + count), vec[None], 0.0).reshape(-1, CW)
        cols = columns(count, first)
        sg[lo : hi + 1, 0:8] += dot(wide, cols, NT, HIGH).reshape(hi - lo + 1, 8, 128)

    def place_group(g):
        row = lax.broadcasted_iota(jnp.int32, (8, CW), 0)
        place(cvec[1 + g], CONV_CH // nd, g * CW)
        place(jnp.where(row == 6, gvec[g], 0.0), DI // nd, g * CW)
        per_head = pair_sums(gvec[g, :, :128], 0)
        for q in range(1, GH // 2):
            per_head = per_head + pair_sums(gvec[g, :, q * 128 : q * 128 + 128], q)
        hvec[2:3] += turned_back(per_head, g)[7:8]

    def ending():
        tok_copy().wait()
        ng = jnp.zeros((1, D), f32)
        for s in range(seqs):
            for i in range(0, T, 64):
                u = masked[s * T + i : s * T + i + 64].astype(f32)
                r = lax.rsqrt(jnp.sum(u * u, axis=1, keepdims=True) * (1.0 / D) + EPS)
                dnv = dn[s * T + i : s * T + i + 64]
                ng = ng + jnp.sum(dnv * u * r, axis=0, keepdims=True)
                v = dnv * ngain[0:1]
                mean = jnp.sum(v * u, axis=1, keepdims=True) * (1.0 / D)
                tgrad[s, i : i + 64] = (tgrad[s, i : i + 64].astype(f32) + r * v - u * (r * r * r * mean)).astype(bf16)
        row = lax.broadcasted_iota(jnp.int32, (8, CW), 0)
        place(cvec[0], CONV_CH // nd, DI)
        for g in range(D // CW):
            place(jnp.where(row == 5, ng[:, g * CW : (g + 1) * CW], 0.0), D // nd, g * CW)
        sg[:, 8:16] = jnp.broadcast_to(hvec[...][None], (nd, 8, 128))

        def sibling(ref):
            for q in range(PL):
                ref[q] = sg[pl.ds((2 * q + 1 - at.c) * S, S)].reshape(S * 16, 128)

        def own(ref):
            for q in range(PL):
                ref[q] = sg[pl.ds((2 * q + at.c) * S, S)].reshape(S * 16, 128)

        tiny.produce(0, sibling, own)

    def tok_copy():
        return pltpu.make_async_copy(tok, masked, setsem.at[0])

    def fin_copy(k, gate):
        a = lax.rem(k, 2)
        if gate:
            return pltpu.make_async_copy(fin.at[a], gin.at[:, pl.ds(pl.multiple_of((k - 2 * NO) * CW, 128), CW)], finsem.at[a])
        return pltpu.make_async_copy(
            fin.at[a], gout.at[lax.div(k, NO), :, pl.ds(pl.multiple_of(lax.rem(k, NO) * CW, 128), CW)], finsem.at[a])

    def each_fin(k, f):
        pl.when(k < 2 * NO)(lambda: f(fin_copy(k, False)))
        pl.when(k >= 2 * NO)(lambda: f(fin_copy(k, True)))

    def finish(k):
        @pl.when(k >= 2)
        def _():
            each_fin(k - 2, lambda c: c.wait())

        fin[lax.rem(k, 2)] = big.stage_z(k)
        each_fin(k, lambda c: c.start())

    m = at.m

    def inside(k):
        return (k >= 0) & (k < NQ)

    def tick(t, carry):
        pl.when(inside(t - 1 - m * RLAG - ZLAG))(lambda: finish(t - 1 - m * RLAG - ZLAG))
        for j in range(m):
            k = t - 1 - (m - j) * RLAG
            pl.when(inside(k))(lambda: big.stage_x(k, j))
        pl.when(inside(t - 1))(lambda: big.stage_c(t - 1))
        pl.when(t < 2 * NO)(lambda: out_terms(t))
        pl.when((t >= 2 * NO) & (t < 2 * NO + GROUPS))(lambda: gate_terms(t))
        pl.when((t >= 2 * NO + GROUPS) & (t < NQ - 1))(lambda: value_terms(t))
        pl.when(t == NQ - 1)(lambda: first_terms(t))
        pl.when(t < NQ)(lambda: terms(t))
        pl.when((t >= 2 * NO + GROUPS) & (t < NQ))(lambda: back_in(t - 2 * NO, dcv[...]))

        pl.when(t == 1)(turn_normed)

        @pl.when(t < GROUPS // 2)
        def _():
            lax.fori_loop(2 * t, 2 * t + 2, through_gate, 0)

        @pl.when((t >= GROUPS // 2) & (t < GROUPS))
        def _():
            def both(g, carry):
                back_in(g, dzb[g])
                return carry

            lax.fori_loop(2 * t - GROUPS, 2 * t - GROUPS + 2, both, 0)

        step = t - 1 - HOP * (S - 1 - at.z)
        passed = lax.div(2 * step + 2, 3)
        pl.when((step >= 0) & (lax.rem(step, 3) < 2) & (passed < GROUPS))(lambda: pass_state(passed))
        def parts_before(t):
            return lax.div(jnp.clip(t - TB, 0, NQ - 2 - TB) * seqs * GROUPS + NQ - 3 - TB, NQ - 2 - TB)

        lax.fori_loop(parts_before(t), parts_before(t + 1), recurrence, 0)
        pl.when(t == 2 * NO)(lambda: tok_copy().start())
        pl.when(t == NQ - 2)(heads_chunk)
        for g in range(GROUPS):
            pl.when(t == 2 * NO + GROUPS + g)(lambda: place_group(g))
        pl.when(t == NQ)(ending)
        pl.when(t == NQ + 1)(lambda: tiny.stage_c(0))
        for j in range(m):
            pl.when(t == NQ + 1 + m - j)(lambda: tiny.stage_x(0, j))
        return carry

    lax.fori_loop(0, NQ + 1 + max(1 + m, m * RLAG + ZLAG), tick, 0)
    total = tiny.stage_z(0)
    gsm[...] = total[:8]
    ghead[...] = total[8:]
    tiny.drain(1)
    big.drain(NQ)
    for k in (NQ - 2, NQ - 1):
        fin_copy(k, True).wait()

    def sent(g, carry):
        chain(g).wait_send()
        edge(g).wait_send()
        return carry

    @pl.when(at.z > 0)
    def _():
        lax.fori_loop(0, GROUPS, sent, 0)
        kr_edge().wait_send()


def backward(S, dp, lengths, tok, cot, small, saved):
    (owin, onormed, opc, oraw, oz, oy, ohin, ony, oconv, ogain, ossq, ong, odny, otsum, old, oldT, ogram, okeys2,
     oreadsT) = saved
    PL = dp // 2
    RLAG, ZLAG = (2, 3) if PL <= 4 else (1, 1)
    nd = S * dp
    R = D // nd
    Rp = -(-R // 16) * 16
    SR = S * R
    seqs, T, _ = tok.shape
    rows = seqs * T
    sds = jax.ShapeDtypeStruct
    dma = pltpu.SemaphoreType.DMA
    V = pltpu.VMEM
    vm = pl.BlockSpec(memory_space=pltpu.VMEM)
    hb = pl.BlockSpec(memory_space=pl.ANY)
    bufs, sems = scatter_scratch(S, PL, R, Rp, CW, bf16, True, RLAG, ZLAG)
    tbufs, tsems = scatter_scratch(S, PL, 16, 16, 128, f32, False, 1, 1)
    return pl.pallas_call(
        functools.partial(backward_kernel, S, PL, RLAG, ZLAG),
        out_shape=[sds((seqs, T, D), bf16), sds((8, 128), f32), sds((Rp, NI * CW), f32), sds((2, Rp, D), f32), sds((8, 128), f32)],
        in_specs=[pl.BlockSpec(memory_space=pltpu.SMEM)] + [vm] * 14 + [hb] * 10,
        out_specs=[vm, vm, hb, hb, vm],
        scratch_shapes=[
            V((rows, D), bf16), V((3, 2, PL * SR, rows), bf16),
            V((GROUPS, seqs, T, CW), f32), V((GROUPS, rows, CW), bf16), V((GROUPS, seqs, STATE, CW), f32),
            V((GROUPS, seqs, STATE, CW), bf16), V((GROUPS, seqs, STATE, CW), bf16), V((rows, D), f32),
            V((seqs, T, T), f32), V((seqs, T, STATE), f32), V((seqs, T, STATE), f32),
            V((seqs, T, 128), f32), V((seqs, T, 128), f32),
            V((1 + GROUPS, 8, CW), f32), V((GROUPS, 8, CW), f32), V((8, 128), f32),
            V((1 + GROUPS, seqs, 8, CW), f32), V((rows, CW), bf16),
            V((2, Rp, CW), f32), V((8, 128), f32), V((seqs, HALO + T, CW), bf16),
            V((2, D, CW), bf16), V((2, T, CW), f32), V((2, T, CW), f32), V((2, T, CW), f32),
            V((2, seqs, STATE, CW), bf16), V((2, seqs, HALO + T, CW), bf16),
            dma((2,)), dma((2,)), dma((2,)), dma((2,)), dma((2,)), dma((2,)), dma((3 + D // CW,)), dma((2,)), dma((2, GROUPS)), dma((2, GROUPS + 1)),
            *bufs, *sems, *tbufs, *tsems, V((nd, 16, 128), f32),
        ],
        name="backward",
        compiler_params=pltpu.CompilerParams(collective_id=1, has_side_effects=True, vmem_limit_bytes=127 << 19),
    )(lengths, *small[4:], ong, ogain, oconv, oraw, ossq, otsum, old, oldT, ogram, okeys2, oreadsT,
      tok.reshape(rows, D), cot, ohin, onormed, ony, owin, oz, oy, odny, opc)


def deliver_kernel(out, tgrad, gout, gin, gsm, ghead, *results):
    for src, dst in zip((out, tgrad, gout), results):
        dst[...] = src[...]
    results[3][...] = gin[:, :PROJ]
    cw, cb, ng, gg, decay, bias, skip = results[4:]
    cw[...] = gsm[0:CONV, : cw.shape[1]]
    for ref, r in ((cb, 4), (ng, 5), (gg, 6)):
        ref[...] = gsm[r : r + 1, : ref.shape[1]]
    for ref, r in ((decay, 0), (bias, 1), (skip, 2)):
        ref[...] = ghead[r : r + 1, : ref.shape[1]]


def deliver(nd, *arrays):
    sds = jax.ShapeDtypeStruct
    vm = pl.BlockSpec(memory_space=pltpu.VMEM)
    widths = (CONV_CH // nd, D // nd, DI // nd, HEADS, HEADS, HEADS)
    return pl.pallas_call(
        deliver_kernel,
        out_shape=[sds(a.shape, a.dtype) for a in arrays[:3]] + [sds((arrays[3].shape[0], PROJ), f32)] + [sds((CONV, CONV_CH // nd), f32)] + [sds((1, w), f32) for w in widths],
        in_specs=[vm] * 6,
        out_specs=[vm] * 11,
        name="deliver",
        compiler_params=pltpu.CompilerParams(vmem_limit_bytes=32 << 20),
    )(*arrays)


def body(tokens, lengths, in_weight, conv_weight, conv_bias, decay_log, step_bias, skip_gain, norm_gain, gate_gain,
         out_weight, cotangent):
    S, dp = lax.axis_size("seq"), lax.axis_size("dp")
    nd = S * dp
    row = lambda v: v.reshape(1, -1)
    small = [conv_weight.T, *map(row, (conv_bias, norm_gain, gate_gain, decay_log, step_bias, skip_gain))]
    out, *saved = forward(S, dp, lengths, tokens, in_weight, out_weight, small, cotangent)
    tgrad, ghead, gin, gout, gsm = backward(S, dp, lengths, tokens, cotangent, small, saved)
    R = D // nd
    if gin.shape[0] > R:
        gin, gout = gin[:R], gout[:, :R]
    out, tgrad, gout, gin, cw, *rows = deliver(nd, out, tgrad, gout, gin, gsm, ghead)
    cb, ng, gg, decay, bias, skip = (r.reshape(-1) for r in rows)
    return out, tgrad, gin, cw.T, cb, decay, bias, skip, ng, gg, gout.reshape(2 * R, D)


def solution(mesh):
    rows, own = P(AXES, None), P(AXES)
    toks = P("dp", "seq", None)
    return jax.shard_map(
        body, mesh=mesh,
        in_specs=(toks, P("dp"), rows, rows, own, P(), P(), P(), own, own, rows, toks),
        out_specs=(toks, toks, rows, rows, own, P(), P(), P(), own, own, rows),
        check_vma=False,
    )
```

```python
import functools
import jax
import jax.numpy as jnp
from jax import lax
from jax.experimental import pallas as pl
from jax.experimental.pallas import tpu as pltpu
from jax.sharding import PartitionSpec as P

D = 1536
DI = 3072
HEADS = 48
HDIM = 64
STATE = 128
CONV = 4
PROJ = 6448
CONV_CH = 3328
CW = 384
GROUPS = DI // CW
GH = CW // HDIM
NI = 1 + 2 * GROUPS
NO = D // CW
EARLY = 2
MID = 2 + GROUPS
GATE = MID + EARLY
LATE = GATE + GROUPS
HALO = 16
EPS = 1e-05
MESH = pl.DeviceIdType.MESH
HIGH = lax.Precision.HIGHEST
f32 = jnp.float32
bf16 = jnp.bfloat16
AXES = ("dp", "seq")
LAG = 2
SLACK = 1


def flip(p, w):
    return p + w * (1 - 2 * lax.rem(lax.div(p, w), 2))


class Place:
    def __init__(self, S, PL):
        self.S, self.PL, self.m = S, PL, PL.bit_length() - 1
        self.d = lax.axis_index("dp")
        self.z = lax.axis_index("seq")
        self.p = lax.div(self.d, 2)
        self.c = lax.rem(self.d, 2)
        self.sib = self.d + 1 - 2 * self.c

    def weight(self, j, h):
        return 2 ** ((j + h) % self.m)

    def held(self, h, j):
        out = [self.p]
        for i in range(j):
            out = out + [flip(q, self.weight(i, h)) for q in out]
        return out

    def across(self, j, h):
        return (2 * flip(self.p, self.weight(j, h)) + self.c, self.z)

    def along(self, o):
        return (self.d, lax.rem(self.z + o, self.S))

    def behind(self, o):
        return lax.rem(self.z - o + self.S, self.S)

    def barrier(self):
        peers = [self.along(o) for o in range(1, self.S)]
        peers += [self.across(j, 0) for j in range(self.m)]
        peers += [(self.sib, self.z)]
        bar = pltpu.get_barrier_semaphore()
        for q in peers:
            pl.semaphore_signal(bar, inc=1, device_id=q, device_id_type=MESH)
        pl.semaphore_wait(bar, len(peers))


def remote(src, dst, ss, rs, to):
    return pltpu.make_async_remote_copy(
        src_ref=src, dst_ref=dst, send_sem=ss, recv_sem=rs, device_id=to, device_id_type=MESH
    )


def picks(rows, R, padded):
    i = lax.broadcasted_iota(jnp.int32, (rows, rows // R * padded), 0)
    j = lax.broadcasted_iota(jnp.int32, (rows, rows // R * padded), 1)
    out = jnp.zeros(i.shape, jnp.bool_)
    for b in range(rows // R):
        inside = (i >= b * R) & (i < b * R + R)
        out = out | (inside & (j - b * padded == i - b * R))
    return jnp.where(out, 1.0, 0.0).astype(bf16)


class Gather:
    def __init__(self, at, sems, arrays):
        self.at = at
        self.zs, self.zr, self.xs, self.xr, self.cs, self.cr = sems
        self.arrays = arrays

    def each(self, k, f):
        for among, fn, land, R in self.arrays:
            if isinstance(k, int):
                if among(k):
                    f(fn(k), R, land and land(k))
            else:
                @pl.when(among(k))
                def _():
                    f(fn(k), R, land and land(k))

    def zcopy(self, ref, R, land, k, way, h):
        at = self.at
        src = at.z - h if way == 0 else at.z + h
        blk = ref.at[pl.ds((at.d * at.S + src) * R, R)] if land is None else land.at[src]
        to = (at.d, at.z + 1 if way == 0 else at.z - 1)
        n = min(h, at.S - 2)
        return remote(blk, blk, self.zs.at[k, way, n], self.zr.at[k, way, n], to)

    def zarrival(self, ref, R, land, k, way, h):
        at = self.at
        src = at.z - h if way == 0 else at.z + h
        blk = ref.at[pl.ds((at.d * at.S + src) * R, R)] if land is None else land.at[src]
        return remote(blk, blk, self.zs.at[k, way, 0], self.zr.at[k, way, h - 1], at.along(1))

    def holds(self, way, h):
        return self.at.z >= h if way == 0 else self.at.z + h < self.at.S

    def goes_on(self, way):
        return self.at.z < self.at.S - 1 if way == 0 else self.at.z > 0

    def half(self, ref, R, q, c, h):
        n = self.at.S * R // 2
        return ref.at[pl.ds((q * 2 + c) * self.at.S * R + h * n, n)]

    def xcopy(self, ref, R, k, j, i, h, recv=False):
        at = self.at
        q = at.held(h, j)[i]
        if recv:
            q = flip(q, at.weight(j, h))
        blk = self.half(ref, R, q, at.c, h)
        n = (2**j - 1 + i) * 2 + h
        return remote(blk, blk, self.xs.at[k, n], self.xr.at[k, n], at.across(j, h))

    def ccopy(self, ref, R, k, n, h, recv=False):
        at = self.at
        q = at.held(h, at.m)[n]
        blk = self.half(ref, R, q, 1 - at.c if recv else at.c, h)
        return remote(blk, blk, self.cs.at[k, n * 2 + h], self.cr.at[k, n * 2 + h], (at.sib, at.z))

    def send_z(self, k):
        def f(ref, R, land):
            for way in range(2):
                pl.when(self.goes_on(way))(lambda: self.zcopy(ref, R, land, k, way, 0).start())

        self.each(k, f)

    def hop(self, k, h):
        def f(ref, R, land):
            for way in range(2):
                pl.when(self.holds(way, h))(lambda: self.zarrival(ref, R, land, k, way, h).wait_recv())
                if h < self.at.S - 1:
                    pl.when(self.holds(way, h) & self.goes_on(way))(lambda: self.zcopy(ref, R, land, k, way, h).start())

        self.each(k, f)

    def stage(self, k, j):
        def f(ref, R, land):
            if j == 0:
                if land is not None:
                    rows = self.at.S * R
                    own = ref.at[pl.ds(pl.multiple_of(self.at.d * rows, 16), rows)]
                    own[...] = dot(picks(rows, R, land.shape[1]), land[...].reshape(-1, land.shape[2])).astype(bf16)
            else:
                for h in range(2):
                    for i in range(2 ** (j - 1)):
                        self.xcopy(ref, R, k, j - 1, i, h, True).wait_recv()
            if j < self.at.m:
                for h in range(2):
                    for i in range(2**j):
                        self.xcopy(ref, R, k, j, i, h).start()
            for h in range(2):
                for n in range(0 if j == 0 else 2 ** (j - 1), 2**j):
                    self.ccopy(ref, R, k, n, h).start()

        self.each(k, f)

    def arrived(self, k):
        def f(ref, R, land):
            for n in range(self.at.PL):
                for h in range(2):
                    self.ccopy(ref, R, k, n, h, True).wait_recv()

        self.each(k, f)

    def sent(self, k):
        def f(ref, R, land):
            for way in range(2):
                for h in range(self.at.S - 1):
                    pl.when(self.holds(way, h) & self.goes_on(way))(
                        lambda: self.zcopy(ref, R, land, k, way, h).wait_send())
            for h in range(2):
                for j in range(self.at.m):
                    for i in range(2**j):
                        self.xcopy(ref, R, k, j, i, h).wait_send()
                for n in range(self.at.PL):
                    self.ccopy(ref, R, k, n, h).wait_send()

        self.each(k, f)


def lanes128(r):
    return jnp.concatenate([r, jnp.zeros((r.shape[0], 128 - r.shape[1]), r.dtype)], axis=1)


def set_heads(heads, decay, bias, skips):
    rows = [bias[...], -jnp.exp(decay[...]), skips[...]]
    heads[...] = jnp.concatenate([lanes128(r) for r in rows] + [jnp.zeros((5, 128), f32)], axis=0)


def sigmoid(v):
    return 1.0 / (1.0 + jnp.exp(-v))


NT = ((1,), (1,))
TN = ((0,), (0,))


def dot(a, b, dims=((1,), (0,)), precision=None):
    return lax.dot_general(a, b, (dims, ((), ())), precision=precision, preferred_element_type=f32)


def halves(v):
    hi = v.astype(bf16)
    return hi, (v - hi.astype(f32)).astype(bf16)


def spread(cols, g6):
    T = cols.shape[0]
    low = lax.broadcasted_iota(jnp.int32, (T, 128), 1) < HDIM
    return jnp.concatenate(
        [
            jnp.where(
                low,
                jnp.broadcast_to(cols[:, 2 * q : 2 * q + 1], (T, 128)),
                jnp.broadcast_to(cols[:, 2 * q + 1 : 2 * q + 2], (T, 128)),
            )
            for q in range(GH // 2)
        ],
        axis=1,
    )


def turned(x, g):
    return pltpu.roll(x, lax.rem(128 - GH * g, 128), 1)


def convolve(x, cp):
    T = x.shape[0] - HALO
    mixed = cp[4:5] + cp[3:4] * x[HALO:]
    for k in range(CONV - 1):
        mixed = mixed + cp[k : k + 1] * pltpu.roll(x, CONV - 1 - k, 0)[HALO:]
    return mixed


def columns(count, first):
    ch = (lax.broadcasted_iota(jnp.int32, (1, CW), 1) + first).astype(f32)
    place = ch - count * jnp.floor((ch + 0.5) / count)
    return jnp.where(lax.broadcasted_iota(jnp.int32, (128, CW), 0).astype(f32) == place, 1.0, 0.0)


def prepare(s, raw, x, heads, cp, ld, ldT, gram):
    T = raw.shape[0]
    steps = jax.nn.softplus(raw + heads[0:1])
    tri = lax.broadcasted_iota(jnp.int32, (T, T), 0) >= lax.broadcasted_iota(jnp.int32, (T, T), 1)
    log_decay = dot(jnp.where(tri, 1.0, 0.0), steps * heads[1:2], precision=HIGH)
    ld[0, s] = log_decay
    ld[1, s] = steps
    turned_ld = log_decay.T
    for g in range(GROUPS):
        ldT[s, g, 0:GH] = turned_ld[g * GH : (g + 1) * GH]
    mixed = convolve(x, cp)[:, : 2 * STATE]
    act = mixed * sigmoid(mixed)
    keys, reads = act[:, :STATE], act[:, STATE:]
    gram[s] = dot(reads, keys, ((1,), (1,)), HIGH)
    return keys, reads, mixed


def fade(ldc, ldr, h, lo, n, m):
    gap = ldc[lo : lo + n, h : h + 1] - ldr[h : h + 1, :m]
    i = lax.broadcasted_iota(jnp.int32, (n, m), 0) + lo
    j = lax.broadcasted_iota(jnp.int32, (n, m), 1)
    return jnp.exp(jnp.where(i >= j, gap, -1e30))


def forward_kernel(S, PL, lengths, tok, win, cw, cb, ng_in, gg_in, decay, bias, skips, wout, cot,
                   out, owin, onormed, opc, oraw, oz, oy, ohin, ony, oconv, ogain, ossq, ong, odny, otsum, old, oldT, ogram, okeys2, oreadsT,
                   wi, wo, sm, zi, zo, halo, normed, ybuf, nyb, loc, hin, hout, dlast, gram, keysT, reads2, keys2, readsT,
                   ld, ldT, convp, gain, ngain, ssq, tsum, heads, pcs, zst, yst,
                   lsem, osem, hsem, ssem, pcsem, zsem, ysem, esem, nsem, cotsem, *sems):
    at = Place(S, PL)
    me = at.d * S + at.z
    seqs, T, _ = tok.shape
    rows = seqs * T
    n = 1 + NI + NO
    nd = S * PL * 2
    RI, RO = D // nd, DI // nd
    packed_i, packed_o = RI % 16 > 0, RO % 16 > 0

    def in_i(k):
        return (k >= 1) & (k < LATE) & ((k < MID) | (k >= GATE))

    def in_o(k):
        return ((k >= MID) & (k < GATE)) | ((k >= LATE) & (k < n))

    def chunk_i(k):
        return k - 1 - EARLY * lax.div(k, GATE)

    def chunk_o(k):
        return k - MID - GROUPS * lax.div(k, LATE)

    ga = Gather(at, sems, [
        (lambda k: k == 0, lambda k: sm, None, 16),
        (in_i, lambda k: wi.at[chunk_i(k)], (lambda k: zi.at[chunk_i(k)]) if packed_i else None, RI),
        (in_o, lambda k: wo.at[chunk_o(k)], (lambda k: zo.at[chunk_o(k)]) if packed_o else None, RO),
    ])

    def local(c):
        return pltpu.make_async_copy(
            wout.at[:, pl.ds(c * CW, CW)], zo.at[c, at.z] if packed_o else wo.at[c, pl.ds(me * RO, RO)], lsem.at[c])

    for c in range(NO):
        local(c).start()
    for j in range(NI):
        lane = 2 * DI if j == 0 else DI + (j - 1) * CW if j <= GROUPS else (j - 1 - GROUPS) * CW
        part = win[:, lane:] if j == 0 else win[:, lane : lane + CW]
        if j == 0:
            part = jnp.concatenate([part, jnp.zeros((part.shape[0], CW - part.shape[1]), bf16)], axis=1)
        if packed_i:
            zi[j, at.z] = part
        else:
            wi[j, pl.ds(pl.multiple_of(me * RI, 16), RI)] = part
    own = [lanes128(r[...].astype(f32)) for r in (cw, cb, ng_in, gg_in)] + [jnp.zeros((9, 128), f32)]
    sm[pl.ds(pl.multiple_of(me * 16, 16), 16)] = jnp.concatenate(own, axis=0).astype(bf16)
    set_heads(heads, decay, bias, skips)
    at.barrier()
    for c in range(NO):
        local(c).wait()

    def halo_copy():
        return remote(tok.at[:, pl.ds(T - HALO, HALO)], halo, hsem.at[0], hsem.at[1], at.along(1))

    @pl.when(at.z < S - 1)
    def _():
        halo_copy().start()

    @pl.when(at.z == 0)
    def _():
        halo[...] = jnp.zeros_like(halo)
        hin[...] = jnp.zeros_like(hin)

    @pl.when(at.z > 0)
    def _():
        halo_copy().wait_recv()

    ssq[...] = jnp.zeros_like(ssq)

    def chain(g):
        return remote(hout.at[g], hin.at[g], ssem.at[0, g], ssem.at[1, g], at.along(1))

    def normed_copies():
        return [pltpu.make_async_copy(normed.at[s, pl.ds(HALO, T), pl.ds(c * CW, CW)],
                                      onormed.at[c, pl.ds(s * T, T)], nsem.at[c, s])
                for c in range(D // CW) for s in range(seqs)]

    def unpack():
        gathered = sm[...]

        def rows_of(count, first):
            wide = dot(gathered, columns(count, first).astype(bf16)).reshape(nd, 16, CW)
            who = lax.broadcasted_iota(jnp.int32, (nd, 1, CW), 0) * count
            at_lane = lax.broadcasted_iota(jnp.int32, (nd, 1, CW), 2) + first
            wide = jnp.where((at_lane >= who) & (at_lane < who + count), wide, 0.0)
            return jnp.sum(wide, axis=0)[:8]

        def group(g, carry):
            convp[1 + g] = rows_of(CONV_CH // nd, g * CW)
            gain[g] = rows_of(DI // nd, g * CW)
            return carry

        lax.fori_loop(0, GROUPS, group, 0)
        convp[0] = rows_of(CONV_CH // nd, DI)
        ng = jnp.concatenate([rows_of(D // nd, g * CW)[5:6] for g in range(D // CW)], axis=1)
        ngain[...] = jnp.broadcast_to(ng, (8, D))
        pltpu.make_async_copy(ngain, ong, esem.at[4 + seqs]).start()
        for s in range(seqs):
            u = halo[s].astype(f32)
            r = lax.rsqrt(jnp.sum(u * u, axis=1, keepdims=True) * (1.0 / D) + EPS)
            normed[s, 0:HALO] = (u * r * ng).astype(bf16)
            for i in range(0, T, 64):
                u = tok[s, i : i + 64].astype(f32)
                r = lax.rsqrt(jnp.sum(u * u, axis=1, keepdims=True) * (1.0 / D) + EPS)
                normed[s, HALO + i : HALO + i + 64] = (u * r * ng).astype(bf16)
        for c in normed_copies():
            c.start()
        pltpu.make_async_copy(convp, oconv, esem.at[2 + seqs]).start()
        pltpu.make_async_copy(gain, ogain, esem.at[3 + seqs]).start()

    def project(w, first):
        x = normed[...] if first == 0 else normed[:, first:]
        return dot(x.reshape(seqs * x.shape[1], D), w).reshape(seqs, x.shape[1], CW)

    def keep_pc(pc, k, slot):
        pcs[slot] = pc
        pltpu.make_async_copy(pcs.at[slot], opc.at[k], pcsem.at[slot]).start()

    def prepared():
        pairs = ((ld, old), (ldT, oldT), (gram, ogram), (keys2, okeys2), (readsT, oreadsT))
        return [pltpu.make_async_copy(a, b, esem.at[seqs + 6 + i]) for i, (a, b) in enumerate(pairs)]

    def first_chunk():
        proj = project(wi[0], 0)
        pc = proj.astype(bf16)
        keep_pc(pc, 0, 0)
        raw = proj[:, HALO:, 2 * STATE :]
        zst[0, :, :, :128] = raw
        pltpu.make_async_copy(zst.at[0, :, :, pl.ds(0, 128)], oraw, zsem.at[0]).start()
        for s in range(seqs):
            keys, reads = prepare(s, raw[s], pc[s].astype(f32), heads, convp[0], ld, ldT, gram)[:2]
            keysT[s] = keys.T
            readsT[s] = reads.T
            reads2[s] = jnp.concatenate(halves(reads), axis=1)
            keys2[s] = jnp.concatenate(halves(keys), axis=1)
        for c in prepared():
            c.start()
        pltpu.make_async_copy(zst.at[0, :, :, pl.ds(0, 128)], oraw, zsem.at[0]).wait()

    def values_chunk(g, k):
        slot = lax.rem(k, 2)

        @pl.when(k >= 2)
        def _():
            pltpu.make_async_copy(pcs.at[slot], opc.at[k - 2], pcsem.at[slot]).wait()

        pc = project(wi[k], 0).astype(bf16)
        keep_pc(pc, k, slot)
        cp = convp[k]
        low = lax.broadcasted_iota(jnp.int32, (T // 2, 128), 1) < HDIM
        skip = spread(turned(jnp.broadcast_to(heads[2:3], (8, 128)), g), 0)[0:1]

        def sequence(s, carry):
            mixed = convolve(pcs[slot, s].astype(f32), cp)
            V = mixed * sigmoid(mixed)
            ldc = turned(ld[0, s], g)
            ldr = ldT[s, g]
            X = V * spread(turned(ld[1, s], g), g)
            lde = spread(ldc, g)
            last = lde[T - 1 : T]
            dlast[g, s] = jnp.broadcast_to(jnp.exp(last), (8, CW))
            loc[g, s] = dot(keysT[s], X * jnp.exp(last - lde), precision=HIGH)
            hi, lo = halves(X)
            H = T // 2
            for q in range(GH // 2):
                sl = slice(q * 128, q * 128 + 128)
                xs = jnp.concatenate([hi[:, sl], lo[:, sl]], axis=1)
                top, bot = [], []
                for h in (2 * q, 2 * q + 1):
                    mt, mt_low = halves(gram[s, :H, :H] * fade(ldc, ldr, h, 0, H, H))
                    mb, mb_low = halves(gram[s, H:, :] * fade(ldc, ldr, h, H, H, T))
                    r = dot(mt, xs[:H])
                    top.append(r[:, :128] + r[:, 128:] + dot(mt_low, xs[:H, :128]))
                    r = dot(mb, xs)
                    bot.append(r[:, :128] + r[:, 128:] + dot(mb_low, xs[:, :128]))
                ybuf[g, s, :H, sl] = jnp.where(low, top[0], top[1]) + skip[:, sl] * V[:H, sl]
                ybuf[g, s, H:, sl] = jnp.where(low, bot[0], bot[1]) + skip[:, sl] * V[H:, sl]
            return carry

        lax.fori_loop(0, seqs, sequence, 0)

    def pass_state(g):
        @pl.when(at.z > 0)
        def _():
            chain(g).wait_recv()

        @pl.when(at.z < S - 1)
        def _():
            for s in range(seqs):
                hout[g, s] = (dlast[g, s, 0:1] * hin[g, s].astype(f32) + loc[g, s]).astype(bf16)
            chain(g).start()

    def y_copy(i):
        a = lax.rem(i, 2)
        return pltpu.make_async_copy(yst.at[a], oy.at[lax.div(i, seqs), lax.rem(i, seqs)], ysem.at[a])

    def gate_chunk(g, k):
        slot = lax.rem(g, 2)

        @pl.when(g >= 2)
        def _():
            pltpu.make_async_copy(zst.at[slot], oz.at[g - 2], zsem.at[slot]).wait()

        zst[slot] = project(wi[k], HALO)
        pltpu.make_async_copy(zst.at[slot], oz.at[g], zsem.at[slot]).start()

        def sequence(s, carry):
            z = zst[slot, s]
            h2 = jnp.concatenate([hin[g, s], hin[g, s]], axis=0)
            carried = dot(reads2[s], h2) * jnp.exp(spread(turned(ld[0, s], g), g))
            y = ybuf[g, s] + carried
            i = g * seqs + s

            @pl.when(i >= 2)
            def _():
                y_copy(i - 2).wait()

            yst[lax.rem(i, 2)] = y
            y_copy(i).start()
            gated = y * (z * sigmoid(z))
            ybuf[g, s] = gated
            ssq[s] += jnp.broadcast_to(jnp.sum(gated * gated, axis=1, keepdims=True), (T, 128))
            return carry

        lax.fori_loop(0, seqs, sequence, 0)

        @pl.when(g == GROUPS - 1)
        def _():
            for c in normed_copies():
                c.wait()
            cot_copy().start()

    def cot_copy():
        return pltpu.make_async_copy(cot, normed.at[:, pl.ds(0, T)], cotsem.at[0])

    def live(s):
        pos = lax.broadcasted_iota(jnp.int32, (T, 1), 0) + at.z * T
        return jnp.where(pos < lengths[s], 1.0, 0.0)

    def normalise():
        for s in range(seqs):
            r = lax.rsqrt(ssq[s, :, 0:1] * (1.0 / DI) + EPS)
            for g in range(GROUPS):
                nyb[g, s * T : (s + 1) * T] = (ybuf[g, s] * r * gain[g, 6:7]).astype(bf16)
                ybuf[g, s] = jnp.zeros((T, CW), f32)
        pltpu.make_async_copy(nyb, ony, esem.at[seqs]).start()
        pltpu.make_async_copy(hin, ohin, esem.at[seqs + 1]).start()
        pltpu.make_async_copy(ssq, ossq, esem.at[seqs + 5]).start()
        cot_copy().wait()
        for s in range(seqs):
            normed[s, 0:T] = (live(s) * normed[s, 0:T].astype(f32)).astype(bf16)

    def out_chunk(c, carry):
        branch = jnp.zeros((rows, CW), f32)
        for g in range(0, GROUPS, 2):
            two = jnp.concatenate([nyb[g], nyb[g + 1]], axis=1)
            branch = branch + dot(two, wo[c, g * CW : (g + 2) * CW])
        branch = branch.reshape(seqs, T, CW)
        lane = pl.ds(pl.multiple_of(c * CW, 128), CW)
        masked = normed[:, 0:T, lane].reshape(rows, CW)
        for s in range(seqs):
            out[s, :, lane] = (tok[s, :, lane].astype(f32) + live(s) * branch[s]).astype(bf16)

        def upstream(g, carry):
            part = wo[c, pl.ds(pl.multiple_of(g * 2 * CW, 16), 2 * CW)]
            for s in range(seqs):
                both = dot(masked[s * T : (s + 1) * T], part, NT)
                ybuf[2 * g, s] += both[:, :CW]
                ybuf[2 * g + 1, s] += both[:, CW:]
            return carry

        lax.fori_loop(0, GROUPS // 2, upstream, 0)

        @pl.when(c == NO - 1)
        def _():
            pltpu.make_async_copy(ybuf, odny, esem.at[0]).start()
            for s in range(seqs):
                t = jnp.zeros((T, 1), f32)
                for g in range(GROUPS):
                    t = t + jnp.sum(ybuf[g, s] * nyb[g, s * T : (s + 1) * T].astype(f32), axis=1, keepdims=True)
                tsum[s] = jnp.broadcast_to(t, (T, 128))
            pltpu.make_async_copy(tsum, otsum, esem.at[1]).start()

        return carry

    def keep(k, start):
        def f(src, dst):
            cp = pltpu.make_async_copy(src, dst, osem.at[k])
            cp.start() if start else cp.wait()

        @pl.when(in_i(k))
        def _():
            f(wi.at[chunk_i(k)], owin.at[chunk_i(k)])

    HOP = (GATE - 3) // (S - 1)
    last = at.m * LAG + 1

    def tick(t, carry):
        ga.send_z(t + S + SLACK)
        for h in range(1, S):
            ga.hop(t + S - h, h)
        for j in range(at.m + 1):
            ga.stage(t - j * LAG, j)
        k = t - last
        ga.arrived(k)
        keep(k, True)
        pl.when(k == 0)(unpack)
        pl.when(k == 1)(first_chunk)
        pl.when((k >= 2) & (k < MID))(lambda: values_chunk(k - 2, k - 1))
        g = k - 3 - HOP * at.z - lax.div(at.z, S - 1) * (GATE - 3 - HOP * (S - 1))
        pl.when((g >= 0) & (g < GROUPS))(lambda: pass_state(g))
        pl.when((k >= GATE) & (k < LATE))(lambda: gate_chunk(k - GATE, k - GATE + 1 + GROUPS))

        pl.when(k == LATE)(normalise)
        late = jnp.clip(k - LATE, -1, NO - EARLY - 1)
        begin = jnp.where(late > 0, late + EARLY, 0)
        end = jnp.where(late >= 0, late + EARLY + 1, 0)
        lax.fori_loop(begin, end, out_chunk, 0)

        return carry

    lax.fori_loop(-S - SLACK, n + last, tick, 0)

    def finish(k, carry):
        ga.sent(k)
        keep(k, False)
        return carry

    lax.fori_loop(0, n, finish, 0)

    @pl.when(at.z < S - 1)
    def _():
        halo_copy().wait_send()

        def f(g, carry):
            chain(g).wait_send()
            return carry

        lax.fori_loop(0, GROUPS, f, 0)

    for k in (GROUPS - 1, GROUPS):
        pltpu.make_async_copy(pcs.at[k % 2], opc.at[k], pcsem.at[k % 2]).wait()
    for g in (GROUPS - 2, GROUPS - 1):
        pltpu.make_async_copy(zst.at[g % 2], oz.at[g], zsem.at[g % 2]).wait()
    for c in prepared():
        c.wait()
    pltpu.make_async_copy(ybuf, odny, esem.at[0]).wait()
    pltpu.make_async_copy(tsum, otsum, esem.at[1]).wait()
    for i in (seqs * GROUPS - 2, seqs * GROUPS - 1):
        y_copy(i).wait()
    pltpu.make_async_copy(nyb, ony, esem.at[seqs]).wait()
    pltpu.make_async_copy(hin, ohin, esem.at[seqs + 1]).wait()
    pltpu.make_async_copy(convp, oconv, esem.at[seqs + 2]).wait()
    pltpu.make_async_copy(gain, ogain, esem.at[seqs + 3]).wait()
    pltpu.make_async_copy(ngain, ong, esem.at[seqs + 4]).wait()
    pltpu.make_async_copy(ssq, ossq, esem.at[seqs + 5]).wait()


def forward(S, dp, lengths, tok, win, wout, small, cot):
    PL = dp // 2
    nd = S * dp
    seqs, T, _ = tok.shape
    n = 1 + NI + NO
    rows = seqs * T
    sds = jax.ShapeDtypeStruct
    dma = pltpu.SemaphoreType.DMA
    V = pltpu.VMEM

    vm = pl.BlockSpec(memory_space=pltpu.VMEM)
    hb = pl.BlockSpec(memory_space=pl.ANY)
    wi_s, wo_s = (NI, D, CW), (NO, DI, CW)
    RI, RO = -(-(D // nd) // 16) * 16, -(-(DI // nd) // 16) * 16
    win = jnp.pad(win, ((0, RI - D // nd), (0, 0)))
    wout = jnp.pad(wout, ((0, RO - DI // nd), (0, 0)))
    zi_s = (NI, S, RI, CW) if RI * nd > D else (8, 128)
    zo_s = (NO, S, RO, CW) if RO * nd > DI else (8, 128)
    return pl.pallas_call(
        functools.partial(forward_kernel, S, PL),
        out_shape=[
            sds((seqs, T, D), bf16), sds(wi_s, bf16), sds((D // CW, rows, CW), bf16),
            sds((1 + GROUPS, seqs, HALO + T, CW), bf16), sds((seqs, T, 128), f32),
            sds((GROUPS, seqs, T, CW), f32), sds((GROUPS, seqs, T, CW), f32),
            sds((GROUPS, seqs, STATE, CW), bf16), sds((GROUPS, rows, CW), bf16),
            sds((1 + GROUPS, 8, CW), f32), sds((GROUPS, 8, CW), f32),
            sds((seqs, T, 128), f32), sds((8, D), f32), sds((GROUPS, seqs, T, CW), f32), sds((seqs, T, 128), f32),
            sds((2, seqs, T, 128), f32), sds((seqs, GROUPS, 8, T), f32), sds((seqs, T, T), f32),
            sds((seqs, T, 2 * STATE), bf16), sds((seqs, STATE, T), f32),
        ],
        in_specs=[pl.BlockSpec(memory_space=pltpu.SMEM)] + [vm] * 9 + [hb] * 2,
        out_specs=[vm] + [hb] * 19,
        scratch_shapes=[
            V(wi_s, bf16), V(wo_s, bf16), V((nd * 16, 128), bf16), V(zi_s, bf16), V(zo_s, bf16), V((seqs, HALO, D), bf16),
            V((seqs, HALO + T, D), bf16), V((GROUPS, seqs, T, CW), f32), V((GROUPS, rows, CW), bf16),
            V((GROUPS, seqs, STATE, CW), f32), V((GROUPS, seqs, STATE, CW), bf16),
            V((GROUPS, seqs, STATE, CW), bf16), V((GROUPS, seqs, 8, CW), f32), V((seqs, T, T), f32),
            V((seqs, STATE, T), f32), V((seqs, T, 2 * STATE), bf16), V((seqs, T, 2 * STATE), bf16),
            V((seqs, STATE, T), f32), V((2, seqs, T, 128), f32),
            V((seqs, GROUPS, 8, T), f32), V((1 + GROUPS, 8, CW), f32), V((GROUPS, 8, CW), f32), V((8, D), f32),
            V((seqs, T, 128), f32), V((seqs, T, 128), f32), V((8, 128), f32), V((2, seqs, HALO + T, CW), bf16),
            V((2, seqs, T, CW), f32), V((2, T, CW), f32),
            dma((NO,)), dma((n,)), dma((2,)), dma((2, GROUPS)), dma((2,)), dma((2,)), dma((2,)), dma((seqs + 11,)), dma((D // CW, seqs)), dma((1,)),
            dma((n, 2, S - 1)), dma((n, 2, S - 1)), dma((n, 2 * PL - 2)), dma((n, 2 * PL - 2)), dma((n, 2 * PL)), dma((n, 2 * PL)),
        ],
        name="forward",
        compiler_params=pltpu.CompilerParams(collective_id=0, has_side_effects=True, vmem_limit_bytes=63 << 20),
    )(lengths, tok, win, *small, wout, cot)


class Scatter:
    def __init__(self, at, R, bufs, sems):
        self.at, self.R, self.SR = at, R, at.S * R
        self.acc, self.cS, self.cR, self.xS, self.xR, self.zS, self.zR, self.zown = bufs
        self.cs, self.cr, self.xs, self.xr, self.zs, self.zr = sems
        self.NA, self.NS, self.NB = self.acc.shape[0], self.xS.shape[0], self.xR.shape[0]
        self.NC, self.MC = self.cR.shape[0], self.cS.shape[0]
        self.NZ, self.MZ = self.zR.shape[0], self.zS.shape[0]
        self.kind = self.xS.dtype

    def ccopy(self, k):
        at, i, o = self.at, lax.rem(k, self.MC), lax.rem(k, self.NC)
        return remote(self.cS.at[i], self.cR.at[o], self.cs.at[i], self.cr.at[o], (at.sib, at.z))

    def xcopy(self, k, j, i, h):
        at, n = self.at, 2**j - 1 + i
        a, b = lax.rem(k, self.NS), lax.rem(k, self.NB)
        return remote(self.xS.at[a, h, n], self.xR.at[b, h, n], self.xs.at[a, h, n], self.xr.at[b, h, n], at.across(j, h))

    def zcopy(self, k, o):
        at = self.at
        a, b = lax.rem(k, self.MZ), lax.rem(k, self.NZ)
        return remote(self.zS.at[a, lax.rem(at.z + o, at.S)], self.zR.at[b, o - 1], self.zs.at[a, o - 1],
                      self.zr.at[b, o - 1], at.along(o))

    def ready(self, k, slots, wait):
        if isinstance(k, int):
            if k >= slots:
                wait()
        else:
            pl.when(k >= slots)(wait)

    def produce(self, k, sibling, own):
        self.ready(k, self.MC, lambda: self.ccopy(k - self.MC).wait_send())
        a, n = lax.rem(k, self.MC), lax.rem(k, self.NA)
        sibling(self.cS.at[a])
        self.ccopy(k).start()
        own(self.acc.at[n])

    def send_x(self, k, j):
        at, n, a, half = self.at, lax.rem(k, self.NA), lax.rem(k, self.NS), self.SR // 2
        for h in range(2):
            for i in range(2**j):
                self.ready(k, self.NS, lambda: self.xcopy(k - self.NS, j, i, h).wait_send())
                q = flip(at.held(h, j)[i], at.weight(j, h))
                self.xS[a, h, 2**j - 1 + i] = self.acc[n, q, h * half : (h + 1) * half].astype(self.kind)
                self.xcopy(k, j, i, h).start()

    def stage_c(self, k):
        self.ccopy(k).wait_recv()
        n, o = lax.rem(k, self.NA), lax.rem(k, self.NC)
        for q in range(self.at.PL):
            self.acc[n, q] += self.cR[o, q]
        self.send_x(k, self.at.m - 1)

    def stage_x(self, k, j):
        at, n, b, half = self.at, lax.rem(k, self.NA), lax.rem(k, self.NB), self.SR // 2
        for h in range(2):
            for i in range(2**j):
                self.xcopy(k, j, i, h).wait_recv()
                q = at.held(h, j)[i]
                self.acc[n, q, h * half : (h + 1) * half] += self.xR[b, h, 2**j - 1 + i].astype(f32)
        if j > 0:
            self.send_x(k, j - 1)
            return
        a = lax.rem(k, self.MZ)
        for o in range(1, at.S):
            self.ready(k, self.MZ, lambda: self.zcopy(k - self.MZ, o).wait_send())
        v = self.acc[n, at.p]
        padded = self.zS.shape[2]
        if padded == self.R:
            self.zS[a] = v.astype(self.kind).reshape(at.S, self.R, v.shape[1])
        else:
            spread_rows = dot(picks(self.SR, self.R, padded), v.astype(bf16), ((0,), (0,)))
            self.zS[a] = spread_rows.astype(self.kind).reshape(at.S, padded, v.shape[1])
        for o in range(1, at.S):
            self.zcopy(k, o).start()
        if padded == self.R:
            own = self.acc[n, at.p, pl.ds(pl.multiple_of(at.z * self.R, 8), self.R)]
        else:
            i = lax.broadcasted_iota(jnp.int32, (padded, self.SR), 0)
            j = lax.broadcasted_iota(jnp.int32, (padded, self.SR), 1)
            mine = (i < self.R) & (j == i + at.z * self.R)
            own = dot(jnp.where(mine, 1.0, 0.0), v, precision=HIGH)
        self.zown[a] = own

    def stage_z(self, k):
        b = lax.rem(k, self.NZ)
        total = self.zown[lax.rem(k, self.MZ)]
        for o in range(1, self.at.S):
            self.zcopy(k, o).wait_recv()
            total = total + self.zR[b, o - 1].astype(f32)
        return total

    def drain(self, n):
        for k in range(max(0, n - self.MC), n):
            self.ccopy(k).wait_send()
        for k in range(max(0, n - self.NS), n):
            for h in range(2):
                for j in range(self.at.m):
                    for i in range(2**j):
                        self.xcopy(k, j, i, h).wait_send()
        for k in range(max(0, n - self.MZ), n):
            for o in range(1, self.at.S):
                self.zcopy(k, o).wait_send()


def scatter_scratch(S, PL, R, padded, width, kind, many, lag, zlag):
    m = PL.bit_length() - 1
    SR = S * R
    NS, NB, NC, NA, MZ, NZ = (lag + 1, 2 * lag, 2, 1 + m * lag, zlag + 1, 2 * zlag) if many else (1,) * 6
    V, dma = pltpu.VMEM, pltpu.SemaphoreType.DMA
    bufs = [
        V((NA, PL, SR, width), f32), V((1, PL, SR, width), f32), V((NC, PL, SR, width), f32),
        V((NS, 2, PL - 1, SR // 2, width), kind), V((NB, 2, PL - 1, SR // 2, width), kind),
        V((MZ, S, padded, width), kind), V((NZ, S - 1, padded, width), kind), V((MZ, padded, width), f32),
    ]
    sems = [dma((1,)), dma((NC,)), dma((NS, 2, PL - 1)), dma((NB, 2, PL - 1)), dma((MZ, S - 1)), dma((NZ, S - 1))]
    return bufs, sems


def pair(cols, q):
    T = cols.shape[0]
    low = lax.broadcasted_iota(jnp.int32, (T, 128), 1) < HDIM
    first = jnp.broadcast_to(cols[:, 2 * q : 2 * q + 1], (T, 128))
    second = jnp.broadcast_to(cols[:, 2 * q + 1 : 2 * q + 2], (T, 128))
    return jnp.where(low, first, second)


def pair_sums(v, q):
    hi = v.astype(bf16)
    rest = v - hi.astype(f32)
    mid = rest.astype(bf16)
    low = (rest - mid.astype(f32)).astype(bf16)
    ch = lax.broadcasted_iota(jnp.int32, (128, 128), 0)
    hd = lax.broadcasted_iota(jnp.int32, (128, 128), 1) - 2 * q
    ones = jnp.where((ch >= hd * HDIM) & (ch < hd * HDIM + HDIM), 1.0, 0.0).astype(bf16)
    return dot(jnp.concatenate([hi, mid, low], axis=1), jnp.concatenate([ones, ones, ones], axis=0))


def turned_back(x, g):
    return pltpu.roll(x, GH * g, 1)


def backward_kernel(S, PL, RLAG, ZLAG, lengths, decay, bias, skips, ngain, gain, convp, raw, ssq, tsum, ld, ldT, gram, keys2, readsT,
                    tok, cot, hin, norm_in, ny, win, zin, yin, dyin, pcin,
                    tgrad, ghead, gin, gout, gsm,
                    masked, lhsT, dyb, dzb, loc, dsin, dsout, dn, dgram, dkeys, dreads,
                    dld, dst, cvec, gvec, hvec, nxt, dcv, fin, heads, pc0, wib, zb, yb, db, hb, pcb,
                    wisem, zsem, ysem, dsem, hinsem, pcsem, setsem, finsem, chsem, hasem, *rest):
    at = Place(S, PL)
    seqs, T, _ = raw.shape
    rows = seqs * T
    nd = S * PL * 2
    R = D // nd
    SR = S * R
    H = T // 2
    NQ = 2 * GROUPS + 1 + 2 * NO
    big = Scatter(at, R, rest[:8], rest[8:14])
    tiny = Scatter(at, 16, rest[14:22], rest[22:28])
    sg = rest[28]
    HOP = 2 if S <= 4 else 1
    TB = 2 + HOP * (S - 1)

    def wi_copy(i):
        a = lax.rem(i, 2)
        k = 9 + i - 16 * lax.div(i, 8) + 7 * lax.div(i, 16)
        return pltpu.make_async_copy(win.at[k], wib.at[a], wisem.at[a])

    def item(i):
        return lax.rem(lax.div(i, seqs), GROUPS), lax.rem(i, seqs)

    def y_copy(i):
        a = lax.rem(i, 2)
        return pltpu.make_async_copy(yin.at[item(i)], yb.at[a], ysem.at[a])

    def zy_copies(i):
        a = lax.rem(i, 2)
        return (pltpu.make_async_copy(zin.at[item(i)], zb.at[a], zsem.at[a]),
                pltpu.make_async_copy(dyin.at[item(i)], db.at[a], dsem.at[a]), y_copy(i))

    def b_copies(g):
        a = lax.rem(g, 2)
        return (pltpu.make_async_copy(hin.at[g], hb.at[a], hinsem.at[a]),
                pltpu.make_async_copy(pcin.at[g + 1], pcb.at[a], pcsem.at[a]))

    def begin(copies, when=True):
        if when is True:
            for c in copies:
                c.start()
        else:
            @pl.when(when)
            def _():
                for c in copies:
                    c.start()

    NCH = D // CW
    setup = [pltpu.make_async_copy(cot, tgrad, setsem.at[0]), pltpu.make_async_copy(ny, dzb, setsem.at[1])]
    setup.append(pltpu.make_async_copy(pcin.at[0], pc0, setsem.at[2 + NCH]))
    setup += [pltpu.make_async_copy(norm_in.at[c], wib.at[c // 3, pl.ds(c % 3 * rows, rows)], setsem.at[2 + c])
              for c in range(NCH)]
    begin([*setup, *zy_copies(0), *b_copies(0)])
    set_heads(heads, decay, bias, skips)
    at.barrier()
    for c in setup:
        c.wait()

    for s in range(seqs):
        live = jnp.where(lax.broadcasted_iota(jnp.int32, (T, 1), 0) + at.z * T < lengths[s], 1.0, 0.0)
        masked[s * T : (s + 1) * T] = (live * tgrad[s].astype(f32)).astype(bf16)
    perm = lax.broadcasted_iota(jnp.int32, (2 * SR, 2 * SR), 0)
    perm_j = lax.broadcasted_iota(jnp.int32, (2 * SR, 2 * SR), 1)
    take = jnp.zeros(perm.shape, jnp.bool_)
    for h in range(2):
        for b in range(S):
            inside = (perm >= h * SR + b * R) & (perm < h * SR + b * R + R)
            take = take | (inside & (perm_j - (2 * b + h) * R == perm - (h * SR + b * R)))
    take = jnp.where(take, 1.0, 0.0).astype(bf16)
    same = jnp.where(lax.broadcasted_iota(jnp.int32, (SR, SR), 0) == lax.broadcasted_iota(jnp.int32, (SR, SR), 1),
                     1.0, 0.0).astype(bf16)
    for q in range(PL):
        for cls in range(2):
            cc = 1 - at.c if cls == 0 else at.c
            slab = 2 * q + cls
            for s in range(seqs):
                tl = slice(s * T, (s + 1) * T)
                lane = slab * 2 * SR
                r = dot(take, dzb[lane // CW, tl, lane % CW : lane % CW + 2 * SR], NT).astype(bf16)
                lhsT[0, cc, q * SR : (q + 1) * SR, tl] = r[:SR]
                lhsT[1, cc, q * SR : (q + 1) * SR, tl] = r[SR:]

    def turn_normed():
        for q in range(PL):
            for cls in range(2):
                cc = 1 - at.c if cls == 0 else at.c
                lane, c = (2 * q + cls) * SR % CW, (2 * q + cls) * SR // CW
                for s in range(seqs):
                    part = wib[c // 3, c % 3 * rows + s * T : c % 3 * rows + (s + 1) * T, lane : lane + SR]
                    lhsT[2, cc, q * SR : (q + 1) * SR, s * T : (s + 1) * T] = dot(same, part, NT).astype(bf16)
        begin([wi_copy(0)])


    for ref in (dn, dgram, dkeys, dreads, dld, dst, cvec, gvec, hvec, sg):
        ref[...] = jnp.zeros_like(ref)

    @pl.when(at.z == S - 1)
    def _():
        dsin[...] = jnp.zeros_like(dsin)
        nxt[...] = jnp.zeros_like(nxt)

    def rms(s):
        return lax.rsqrt(ssq[s, :, 0:1] * (1.0 / DI) + EPS)

    def through_gate(g, carry):
        def sequence(s, carry):
            i = g * seqs + s
            a = lax.rem(i, 2)
            for c in zy_copies(i):
                c.wait()
            begin(zy_copies(i + 1)[:2], i + 1 < seqs * GROUPS)
            begin([y_copy(i + 1)])
            r = rms(s)
            z, y, dn_y = zb[a], yb[a], db[a]
            sg_ = sigmoid(z)
            gate = z * sg_
            w = (y * gate) * r
            gvec[g, 6:7] += jnp.sum(dn_y * w, axis=0, keepdims=True)
            dw = r * (dn_y * gain[g, 6:7] - w * (tsum[s, :, 0:1] * (1.0 / DI)))
            dzb[g, pl.ds(pl.multiple_of(s * T, 16), T)] = (dw * y * (sg_ * (1.0 + z * (1.0 - sg_)))).astype(bf16)
            dy = dw * gate
            dyb[g, s] = dy
            loc[g, s] = dot(readsT[s], dy * jnp.exp(spread(turned(ld[0, s], g), g)), precision=HIGH)
            return carry

        lax.fori_loop(0, seqs, sequence, 0)
        return 0

    def chain(g):
        return remote(dsout.at[g], dsin.at[g], chsem.at[0, g], chsem.at[1, g], at.along(S - 1))

    def pass_state(g):
        @pl.when(at.z < S - 1)
        def _():
            chain(g).wait_recv()

        @pl.when(at.z > 0)
        def _():
            for s in range(seqs):
                last = jnp.exp(spread(turned(ld[0, s, T - 8 :], g), g))[7:8]
                dsout[g, s] = (last * dsin[g, s].astype(f32) + loc[g, s]).astype(bf16)
            chain(g).start()

    def edge(g):
        return remote(dyb.at[g, :, pl.ds(0, 8)], nxt.at[g], hasem.at[0, g], hasem.at[1, g], at.along(S - 1))

    def conv_sums(g, x, dm, lanes):
        x = x[:, :lanes]
        for k in range(CONV):
            shifted = x[HALO:] if k == CONV - 1 else pltpu.roll(x, CONV - 1 - k, 0)[HALO:]
            cvec[g, k : k + 1, :lanes] += jnp.sum(dm * shifted, axis=0, keepdims=True)
        cvec[g, CONV : CONV + 1, :lanes] += jnp.sum(dm, axis=0, keepdims=True)

    def recurrence(i, carry):
        g, s = lax.div(i, seqs), lax.rem(i, seqs)
        a = lax.rem(g, 2)

        @pl.when(s == 0)
        def _():
            for c in b_copies(g):
                c.wait()
            begin(b_copies(g + 1), g + 1 < GROUPS)

        y_copy(i).wait()
        begin([y_copy(i + 1)], i + 1 < seqs * GROUPS)

        cp = convp[g + 1]
        low = lax.broadcasted_iota(jnp.int32, (T, 128), 1) < HDIM
        is_last = lax.broadcasted_iota(jnp.int32, (T, 128), 0) == T - 1
        skips = turned(jnp.broadcast_to(heads[2:3], (8, 128)), g)
        ldc, ldr, stc = turned(ld[0, s], g), ldT[s, g], turned(ld[1, s], g)
        dgt, dgb = jnp.zeros((H, H), f32), jnp.zeros((H, T), f32)
        sums, dk, dr = jnp.zeros((2 * T, 128), f32), jnp.zeros((T, STATE), f32), jnp.zeros((T, STATE), f32)
        for q in range(GH // 2):
            sl = slice(q * 128, q * 128 + 128)
            skip = pair(skips, q)[0:1]
            x = pcb[a, s, :, sl].astype(f32)
            mixed = convolve(x, cp[:, sl])
            sg_ = sigmoid(mixed)
            V = mixed * sg_
            lde, st = pair(ldc, q), pair(stc, q)
            last = lde[T - 1 : T]
            tail = jnp.exp(last - lde)
            X = V * st
            dS, hq = dsin[g, s, :, sl], hb[a, s, :, sl]
            dXt = tail * dot(keys2[s], jnp.concatenate([dS, dS], axis=0))
            dY = dyb[g, s, :, sl]
            xh = X.astype(bf16)
            x2 = jnp.concatenate([xh, xh], axis=1)
            dyp = jnp.concatenate(halves(dY), axis=1)
            two = []
            for h in (2 * q, 2 * q + 1):
                ft = fade(ldc, ldr, h, 0, H, H)
                fb = fade(ldc, ldr, h, H, H, T)
                mt, mt_low = halves(gram[s, :H, :H] * ft)
                mb, mb_low = halves(gram[s, H:, :] * fb)
                r0 = dot(jnp.concatenate([mt, mb[:, :H]], axis=0), dyp, TN)
                r1 = dot(mb[:, H:], dyp[H:], TN)
                r = jnp.concatenate([r0, r1], axis=0)
                low0 = dot(jnp.concatenate([mt_low, mb_low[:, :H]], axis=0), dyp[:, :128], TN)
                low1 = dot(mb_low[:, H:], dyp[H:, :128], TN)
                two.append(r[:, :128] + r[:, 128:] + jnp.concatenate([low0, low1], axis=0))
                mine = low if h == 2 * q else jnp.logical_not(low)
                dyh = jnp.concatenate(halves(jnp.where(mine, dY, 0.0)), axis=1)
                dgt = dgt + ft * dot(dyh[:H], x2[:H], NT)
                dgb = dgb + fb * dot(dyh[H:], x2, NT)
            dX = jnp.where(low, two[0], two[1]) + dXt
            dV = st * dX + skip * dY
            gvec[g, 7:8, sl] += jnp.sum(dY * V, axis=0, keepdims=True)
            q1 = dY * (yb[lax.rem(i, 2), :, sl] - skip * V) - X * dX
            at_end = jnp.sum(X * dXt, axis=0, keepdims=True) + jnp.exp(last) * jnp.sum(
                hq.astype(f32) * dS.astype(f32), axis=0, keepdims=True)
            q1 = q1 + jnp.where(is_last, at_end, 0.0)
            sums = sums + pair_sums(jnp.concatenate([q1, dX * V], axis=0), q)
            dk = dk + dot(jnp.concatenate(halves(tail * X), axis=1), jnp.concatenate([dS, dS], axis=1), NT)
            dr = dr + dot(jnp.concatenate(halves(dY * jnp.exp(lde)), axis=1), jnp.concatenate([hq, hq], axis=1), NT)
            dm = dV * (sg_ * (1.0 + mixed * (1.0 - sg_)))
            dyb[g, s, :, sl] = dm
            for k in range(CONV):
                shifted = x[HALO:] if k == CONV - 1 else pltpu.roll(x, CONV - 1 - k, 0)[HALO:]
                cvec[g + 1, k : k + 1, sl] += jnp.sum(dm * shifted, axis=0, keepdims=True)
            cvec[g + 1, CONV : CONV + 1, sl] += jnp.sum(dm, axis=0, keepdims=True)
        dgram[s, :H, :H] += dgt
        dgram[s, H:, :] += dgb
        dld[s] += turned_back(sums[:T], g)
        dst[s] += turned_back(sums[T:], g)
        dkeys[s] += dk
        dreads[s] += dr

        @pl.when((at.z > 0) & (s == seqs - 1))
        def _():
            edge(g).start()

        return carry

    def unconvolve(dm, after, cp):
        ext = jnp.concatenate([dm, after], axis=0)
        n = ext.shape[0]
        out = cp[3:4] * dm
        for k in range(CONV - 1):
            out = out + cp[k : k + 1] * pltpu.roll(ext, n - (CONV - 1 - k), 0)[: dm.shape[0]]
        return out

    def heads_chunk():
        tri = lax.broadcasted_iota(jnp.int32, (T, T), 1) >= lax.broadcasted_iota(jnp.int32, (T, T), 0)
        tri = jnp.where(tri, 1.0, 0.0)
        cp = convp[0]
        for s in range(seqs):
            x = pc0[s].astype(f32)
            mixed = convolve(x, cp)[:, : 2 * STATE]
            sg_ = sigmoid(mixed)
            act = mixed * sg_
            keys, reads = act[:, :STATE], act[:, STATE:]
            dr = dreads[s] + dot(dgram[s], keys, precision=HIGH)
            dk = dkeys[s] + dot(dgram[s], reads, TN, HIGH)
            dm = jnp.concatenate([dk, dr], axis=1) * (sg_ * (1.0 + mixed * (1.0 - sg_)))
            conv_sums(0, x, dm, 2 * STATE)
            da = dot(tri, dld[s], precision=HIGH)
            draw = (dst[s] + da * heads[1:2]) * sigmoid(raw[s] + heads[0:1])
            hvec[0:1] += jnp.sum(da * ld[1, s], axis=0, keepdims=True) * heads[1:2]
            hvec[1:2] += jnp.sum(draw, axis=0, keepdims=True)
            zb[s] = jnp.concatenate([dm, draw], axis=1)

        @pl.when(at.z > 0)
        def _():
            kr_edge().start()

    def kr_edge():
        return remote(zb.at[:, pl.ds(0, 8)], nxt.at[GROUPS], hasem.at[0, GROUPS], hasem.at[1, GROUPS], at.along(S - 1))

    def terms(k):
        rhs = dcv[...]
        lhs = lhsT.at[jnp.minimum(lax.div(k, NO), 2)]

        def product(cc, ref):
            for lo in range(0, PL * SR, 384):
                ref[lo // SR : (lo + 384) // SR] = dot(lhs[cc, lo : lo + 384], rhs).reshape(384 // SR, SR, CW)

        def sibling(ref):
            product(0, ref)

        def own(ref):
            product(1, ref)

        big.produce(k, sibling, own)

    def back_in(i, d):
        wi_copy(i).wait()
        begin([wi_copy(i + 1)], i + 1 < 2 * GROUPS + 1)
        for lane in range(0, D, 512):
            dn[:, lane : lane + 512] += dot(d, wib[lax.rem(i, 2), lane : lane + 512], NT)

    def out_terms(k):
        c = lax.rem(k, NO)
        dcv[...] = masked[:, pl.ds(pl.multiple_of(c * CW, 128), CW)]

    def gate_terms(k):
        dcv[...] = dzb[k - 2 * NO]

    def value_terms(k):
        g = k - 2 * NO - GROUPS

        @pl.when(at.z < S - 1)
        def _():
            edge(g).wait_recv()

        cp = convp[g + 1]
        for s in range(seqs):
            dcv[s * T : (s + 1) * T] = unconvolve(dyb[g, s], nxt[g, s], cp).astype(bf16)

    def first_terms(k):
        @pl.when(at.z < S - 1)
        def _():
            kr_edge().wait_recv()

        cp = convp[0]
        for s in range(seqs):
            v = zb[s]
            c = unconvolve(v, nxt[GROUPS, s], cp)
            is_conv = lax.broadcasted_iota(jnp.int32, (T, CW), 1) < 2 * STATE
            dcv[s * T : (s + 1) * T] = jnp.where(is_conv, c, v).astype(bf16)

    def place(vec, count, first):
        lo, hi = first // count, min(nd - 1, (first + CW - 1) // count)
        who = (lax.broadcasted_iota(jnp.int32, (hi - lo + 1, 1, CW), 0) + lo) * count
        ch = lax.broadcasted_iota(jnp.int32, (hi - lo + 1, 1, CW), 2) + first
        wide = jnp.where((ch >= who) & (ch < who + count), vec[None], 0.0).reshape(-1, CW)
        cols = columns(count, first)
        sg[lo : hi + 1, 0:8] += dot(wide, cols, NT, HIGH).reshape(hi - lo + 1, 8, 128)

    def place_group(g):
        row = lax.broadcasted_iota(jnp.int32, (8, CW), 0)
        place(cvec[1 + g], CONV_CH // nd, g * CW)
        place(jnp.where(row == 6, gvec[g], 0.0), DI // nd, g * CW)
        per_head = pair_sums(gvec[g, :, :128], 0)
        for q in range(1, GH // 2):
            per_head = per_head + pair_sums(gvec[g, :, q * 128 : q * 128 + 128], q)
        hvec[2:3] += turned_back(per_head, g)[7:8]

    def ending():
        tok_copy().wait()
        ng = jnp.zeros((1, D), f32)
        for s in range(seqs):
            for i in range(0, T, 64):
                u = masked[s * T + i : s * T + i + 64].astype(f32)
                r = lax.rsqrt(jnp.sum(u * u, axis=1, keepdims=True) * (1.0 / D) + EPS)
                dnv = dn[s * T + i : s * T + i + 64]
                ng = ng + jnp.sum(dnv * u * r, axis=0, keepdims=True)
                v = dnv * ngain[0:1]
                mean = jnp.sum(v * u, axis=1, keepdims=True) * (1.0 / D)
                tgrad[s, i : i + 64] = (tgrad[s, i : i + 64].astype(f32) + r * v - u * (r * r * r * mean)).astype(bf16)
        row = lax.broadcasted_iota(jnp.int32, (8, CW), 0)
        place(cvec[0], CONV_CH // nd, DI)
        for g in range(D // CW):
            place(jnp.where(row == 5, ng[:, g * CW : (g + 1) * CW], 0.0), D // nd, g * CW)
        sg[:, 8:16] = jnp.broadcast_to(hvec[...][None], (nd, 8, 128))

        def sibling(ref):
            for q in range(PL):
                ref[q] = sg[pl.ds((2 * q + 1 - at.c) * S, S)].reshape(S * 16, 128)

        def own(ref):
            for q in range(PL):
                ref[q] = sg[pl.ds((2 * q + at.c) * S, S)].reshape(S * 16, 128)

        tiny.produce(0, sibling, own)

    def tok_copy():
        return pltpu.make_async_copy(tok, masked, setsem.at[0])

    def fin_copy(k, gate):
        a = lax.rem(k, 2)
        if gate:
            return pltpu.make_async_copy(fin.at[a], gin.at[:, pl.ds(pl.multiple_of((k - 2 * NO) * CW, 128), CW)], finsem.at[a])
        return pltpu.make_async_copy(
            fin.at[a], gout.at[lax.div(k, NO), :, pl.ds(pl.multiple_of(lax.rem(k, NO) * CW, 128), CW)], finsem.at[a])

    def each_fin(k, f):
        pl.when(k < 2 * NO)(lambda: f(fin_copy(k, False)))
        pl.when(k >= 2 * NO)(lambda: f(fin_copy(k, True)))

    def finish(k):
        @pl.when(k >= 2)
        def _():
            each_fin(k - 2, lambda c: c.wait())

        fin[lax.rem(k, 2)] = big.stage_z(k)
        each_fin(k, lambda c: c.start())

    m = at.m

    def inside(k):
        return (k >= 0) & (k < NQ)

    def tick(t, carry):
        pl.when(inside(t - 1 - m * RLAG - ZLAG))(lambda: finish(t - 1 - m * RLAG - ZLAG))
        for j in range(m):
            k = t - 1 - (m - j) * RLAG
            pl.when(inside(k))(lambda: big.stage_x(k, j))
        pl.when(inside(t - 1))(lambda: big.stage_c(t - 1))
        pl.when(t < 2 * NO)(lambda: out_terms(t))
        pl.when((t >= 2 * NO) & (t < 2 * NO + GROUPS))(lambda: gate_terms(t))
        pl.when((t >= 2 * NO + GROUPS) & (t < NQ - 1))(lambda: value_terms(t))
        pl.when(t == NQ - 1)(lambda: first_terms(t))
        pl.when(t < NQ)(lambda: terms(t))
        pl.when((t >= 2 * NO + GROUPS) & (t < NQ))(lambda: back_in(t - 2 * NO, dcv[...]))

        pl.when(t == 1)(turn_normed)

        @pl.when(t < GROUPS // 2)
        def _():
            lax.fori_loop(2 * t, 2 * t + 2, through_gate, 0)

        @pl.when((t >= GROUPS // 2) & (t < GROUPS))
        def _():
            def both(g, carry):
                back_in(g, dzb[g])
                return carry

            lax.fori_loop(2 * t - GROUPS, 2 * t - GROUPS + 2, both, 0)

        step = t - 1 - HOP * (S - 1 - at.z)
        passed = lax.div(4 * step + 6, 7)
        new = passed * 7 < 4 * step + 4
        pl.when((step >= 0) & new & (passed < GROUPS))(lambda: pass_state(passed))
        def parts_before(t):
            return lax.div(jnp.clip(t - TB, 0, NQ - 2 - TB) * seqs * GROUPS + NQ - 3 - TB, NQ - 2 - TB)

        lax.fori_loop(parts_before(t), parts_before(t + 1), recurrence, 0)
        pl.when(t == 2 * NO)(lambda: tok_copy().start())
        pl.when(t == NQ - 2)(heads_chunk)
        for g in range(GROUPS):
            pl.when(t == 2 * NO + GROUPS + g)(lambda: place_group(g))
        pl.when(t == NQ)(ending)
        pl.when(t == NQ + 1)(lambda: tiny.stage_c(0))
        for j in range(m):
            pl.when(t == NQ + 1 + m - j)(lambda: tiny.stage_x(0, j))
        return carry

    lax.fori_loop(0, NQ + 1 + max(1 + m, m * RLAG + ZLAG), tick, 0)
    total = tiny.stage_z(0)
    gsm[...] = total[:8]
    ghead[...] = total[8:]
    tiny.drain(1)
    big.drain(NQ)
    for k in (NQ - 2, NQ - 1):
        fin_copy(k, True).wait()

    def sent(g, carry):
        chain(g).wait_send()
        edge(g).wait_send()
        return carry

    @pl.when(at.z > 0)
    def _():
        lax.fori_loop(0, GROUPS, sent, 0)
        kr_edge().wait_send()


def backward(S, dp, lengths, tok, cot, small, saved):
    (owin, onormed, opc, oraw, oz, oy, ohin, ony, oconv, ogain, ossq, ong, odny, otsum, old, oldT, ogram, okeys2,
     oreadsT) = saved
    PL = dp // 2
    RLAG, ZLAG = (2, 3) if PL <= 4 else (1, 1)
    nd = S * dp
    R = D // nd
    Rp = -(-R // 16) * 16
    SR = S * R
    seqs, T, _ = tok.shape
    rows = seqs * T
    sds = jax.ShapeDtypeStruct
    dma = pltpu.SemaphoreType.DMA
    V = pltpu.VMEM
    vm = pl.BlockSpec(memory_space=pltpu.VMEM)
    hb = pl.BlockSpec(memory_space=pl.ANY)
    bufs, sems = scatter_scratch(S, PL, R, Rp, CW, bf16, True, RLAG, ZLAG)
    tbufs, tsems = scatter_scratch(S, PL, 16, 16, 128, f32, False, 1, 1)
    return pl.pallas_call(
        functools.partial(backward_kernel, S, PL, RLAG, ZLAG),
        out_shape=[sds((seqs, T, D), bf16), sds((8, 128), f32), sds((Rp, NI * CW), f32), sds((2, Rp, D), f32), sds((8, 128), f32)],
        in_specs=[pl.BlockSpec(memory_space=pltpu.SMEM)] + [vm] * 14 + [hb] * 10,
        out_specs=[vm, vm, hb, hb, vm],
        scratch_shapes=[
            V((rows, D), bf16), V((3, 2, PL * SR, rows), bf16),
            V((GROUPS, seqs, T, CW), f32), V((GROUPS, rows, CW), bf16), V((GROUPS, seqs, STATE, CW), f32),
            V((GROUPS, seqs, STATE, CW), bf16), V((GROUPS, seqs, STATE, CW), bf16), V((rows, D), f32),
            V((seqs, T, T), f32), V((seqs, T, STATE), f32), V((seqs, T, STATE), f32),
            V((seqs, T, 128), f32), V((seqs, T, 128), f32),
            V((1 + GROUPS, 8, CW), f32), V((GROUPS, 8, CW), f32), V((8, 128), f32),
            V((1 + GROUPS, seqs, 8, CW), f32), V((rows, CW), bf16),
            V((2, Rp, CW), f32), V((8, 128), f32), V((seqs, HALO + T, CW), bf16),
            V((2, D, CW), bf16), V((2, T, CW), f32), V((2, T, CW), f32), V((2, T, CW), f32),
            V((2, seqs, STATE, CW), bf16), V((2, seqs, HALO + T, CW), bf16),
            dma((2,)), dma((2,)), dma((2,)), dma((2,)), dma((2,)), dma((2,)), dma((3 + D // CW,)), dma((2,)), dma((2, GROUPS)), dma((2, GROUPS + 1)),
            *bufs, *sems, *tbufs, *tsems, V((nd, 16, 128), f32),
        ],
        name="backward",
        compiler_params=pltpu.CompilerParams(collective_id=1, has_side_effects=True, vmem_limit_bytes=127 << 19),
    )(lengths, *small[4:], ong, ogain, oconv, oraw, ossq, otsum, old, oldT, ogram, okeys2, oreadsT,
      tok.reshape(rows, D), cot, ohin, onormed, ony, owin, oz, oy, odny, opc)


def deliver_kernel(out, tgrad, gout, gin, gsm, ghead, *results):
    for src, dst in zip((out, tgrad, gout), results):
        dst[...] = src[...]
    results[3][...] = gin[:, :PROJ]
    cw, cb, ng, gg, decay, bias, skip = results[4:]
    cw[...] = gsm[0:CONV, : cw.shape[1]]
    for ref, r in ((cb, 4), (ng, 5), (gg, 6)):
        ref[...] = gsm[r : r + 1, : ref.shape[1]]
    for ref, r in ((decay, 0), (bias, 1), (skip, 2)):
        ref[...] = ghead[r : r + 1, : ref.shape[1]]


def deliver(nd, *arrays):
    sds = jax.ShapeDtypeStruct
    vm = pl.BlockSpec(memory_space=pltpu.VMEM)
    widths = (CONV_CH // nd, D // nd, DI // nd, HEADS, HEADS, HEADS)
    return pl.pallas_call(
        deliver_kernel,
        out_shape=[sds(a.shape, a.dtype) for a in arrays[:3]] + [sds((arrays[3].shape[0], PROJ), f32)] + [sds((CONV, CONV_CH // nd), f32)] + [sds((1, w), f32) for w in widths],
        in_specs=[vm] * 6,
        out_specs=[vm] * 11,
        name="deliver",
        compiler_params=pltpu.CompilerParams(vmem_limit_bytes=32 << 20),
    )(*arrays)


def body(tokens, lengths, in_weight, conv_weight, conv_bias, decay_log, step_bias, skip_gain, norm_gain, gate_gain,
         out_weight, cotangent):
    S, dp = lax.axis_size("seq"), lax.axis_size("dp")
    nd = S * dp
    row = lambda v: v.reshape(1, -1)
    small = [conv_weight.T, *map(row, (conv_bias, norm_gain, gate_gain, decay_log, step_bias, skip_gain))]
    out, *saved = forward(S, dp, lengths, tokens, in_weight, out_weight, small, cotangent)
    tgrad, ghead, gin, gout, gsm = backward(S, dp, lengths, tokens, cotangent, small, saved)
    R = D // nd
    if gin.shape[0] > R:
        gin, gout = gin[:R], gout[:, :R]
    out, tgrad, gout, gin, cw, *rows = deliver(nd, out, tgrad, gout, gin, gsm, ghead)
    cb, ng, gg, decay, bias, skip = (r.reshape(-1) for r in rows)
    return out, tgrad, gin, cw.T, cb, decay, bias, skip, ng, gg, gout.reshape(2 * R, D)


def solution(mesh):
    rows, own = P(AXES, None), P(AXES)
    toks = P("dp", "seq", None)
    return jax.shard_map(
        body, mesh=mesh,
        in_specs=(toks, P("dp"), rows, rows, own, P(), P(), P(), own, own, rows, toks),
        out_specs=(toks, toks, rows, rows, own, P(), P(), P(), own, own, rows),
        check_vma=False,
    )
```

```python
import functools
import jax
import jax.numpy as jnp
from jax import lax
from jax.experimental import pallas as pl
from jax.experimental.pallas import tpu as pltpu
from jax.sharding import PartitionSpec as P

D = 1536
DI = 3072
HEADS = 48
HDIM = 64
STATE = 128
CONV = 4
PROJ = 6448
CONV_CH = 3328
CW = 384
GROUPS = DI // CW
GH = CW // HDIM
NI = 1 + 2 * GROUPS
NO = D // CW
EARLY = 2
MID = 2 + GROUPS
GATE = MID + EARLY
LATE = GATE + GROUPS
HALO = 16
EPS = 1e-05
MESH = pl.DeviceIdType.MESH
HIGH = lax.Precision.HIGHEST
f32 = jnp.float32
bf16 = jnp.bfloat16
AXES = ("dp", "seq")
LAG = 2
SLACK = 1


def flip(p, w):
    return p + w * (1 - 2 * lax.rem(lax.div(p, w), 2))


class Place:
    def __init__(self, S, PL):
        self.S, self.PL, self.m = S, PL, PL.bit_length() - 1
        self.d = lax.axis_index("dp")
        self.z = lax.axis_index("seq")
        self.p = lax.div(self.d, 2)
        self.c = lax.rem(self.d, 2)
        self.sib = self.d + 1 - 2 * self.c

    def weight(self, j, h):
        return 2 ** ((j + h) % self.m)

    def held(self, h, j):
        out = [self.p]
        for i in range(j):
            out = out + [flip(q, self.weight(i, h)) for q in out]
        return out

    def across(self, j, h):
        return (2 * flip(self.p, self.weight(j, h)) + self.c, self.z)

    def along(self, o):
        return (self.d, lax.rem(self.z + o, self.S))

    def behind(self, o):
        return lax.rem(self.z - o + self.S, self.S)

    def barrier(self):
        peers = [self.along(o) for o in range(1, self.S)]
        peers += [self.across(j, 0) for j in range(self.m)]
        peers += [(self.sib, self.z)]
        bar = pltpu.get_barrier_semaphore()
        for q in peers:
            pl.semaphore_signal(bar, inc=1, device_id=q, device_id_type=MESH)
        pl.semaphore_wait(bar, len(peers))


def remote(src, dst, ss, rs, to):
    return pltpu.make_async_remote_copy(
        src_ref=src, dst_ref=dst, send_sem=ss, recv_sem=rs, device_id=to, device_id_type=MESH
    )


def picks(rows, R, padded):
    i = lax.broadcasted_iota(jnp.int32, (rows, rows // R * padded), 0)
    j = lax.broadcasted_iota(jnp.int32, (rows, rows // R * padded), 1)
    out = jnp.zeros(i.shape, jnp.bool_)
    for b in range(rows // R):
        inside = (i >= b * R) & (i < b * R + R)
        out = out | (inside & (j - b * padded == i - b * R))
    return jnp.where(out, 1.0, 0.0).astype(bf16)


class Gather:
    def __init__(self, at, sems, arrays):
        self.at = at
        self.zs, self.zr, self.xs, self.xr, self.cs, self.cr = sems
        self.arrays = arrays

    def each(self, k, f):
        for among, fn, land, R in self.arrays:
            if isinstance(k, int):
                if among(k):
                    f(fn(k), R, land and land(k))
            else:
                @pl.when(among(k))
                def _():
                    f(fn(k), R, land and land(k))

    def zcopy(self, ref, R, land, k, way, h):
        at = self.at
        src = at.z - h if way == 0 else at.z + h
        blk = ref.at[pl.ds((at.d * at.S + src) * R, R)] if land is None else land.at[src]
        to = (at.d, at.z + 1 if way == 0 else at.z - 1)
        n = min(h, at.S - 2)
        return remote(blk, blk, self.zs.at[k, way, n], self.zr.at[k, way, n], to)

    def zarrival(self, ref, R, land, k, way, h):
        at = self.at
        src = at.z - h if way == 0 else at.z + h
        blk = ref.at[pl.ds((at.d * at.S + src) * R, R)] if land is None else land.at[src]
        return remote(blk, blk, self.zs.at[k, way, 0], self.zr.at[k, way, h - 1], at.along(1))

    def holds(self, way, h):
        return self.at.z >= h if way == 0 else self.at.z + h < self.at.S

    def goes_on(self, way):
        return self.at.z < self.at.S - 1 if way == 0 else self.at.z > 0

    def half(self, ref, R, q, c, h):
        n = self.at.S * R // 2
        return ref.at[pl.ds((q * 2 + c) * self.at.S * R + h * n, n)]

    def xcopy(self, ref, R, k, j, i, h, recv=False):
        at = self.at
        q = at.held(h, j)[i]
        if recv:
            q = flip(q, at.weight(j, h))
        blk = self.half(ref, R, q, at.c, h)
        n = (2**j - 1 + i) * 2 + h
        return remote(blk, blk, self.xs.at[k, n], self.xr.at[k, n], at.across(j, h))

    def ccopy(self, ref, R, k, n, h, recv=False):
        at = self.at
        q = at.held(h, at.m)[n]
        blk = self.half(ref, R, q, 1 - at.c if recv else at.c, h)
        return remote(blk, blk, self.cs.at[k, n * 2 + h], self.cr.at[k, n * 2 + h], (at.sib, at.z))

    def send_z(self, k):
        def f(ref, R, land):
            for way in range(2):
                pl.when(self.goes_on(way))(lambda: self.zcopy(ref, R, land, k, way, 0).start())

        self.each(k, f)

    def hop(self, k, h):
        def f(ref, R, land):
            for way in range(2):
                pl.when(self.holds(way, h))(lambda: self.zarrival(ref, R, land, k, way, h).wait_recv())
                if h < self.at.S - 1:
                    pl.when(self.holds(way, h) & self.goes_on(way))(lambda: self.zcopy(ref, R, land, k, way, h).start())

        self.each(k, f)

    def stage(self, k, j):
        def f(ref, R, land):
            if j == 0:
                if land is not None:
                    rows = self.at.S * R
                    own = ref.at[pl.ds(pl.multiple_of(self.at.d * rows, 16), rows)]
                    own[...] = dot(picks(rows, R, land.shape[1]), land[...].reshape(-1, land.shape[2])).astype(bf16)
            else:
                for h in range(2):
                    for i in range(2 ** (j - 1)):
                        self.xcopy(ref, R, k, j - 1, i, h, True).wait_recv()
            if j < self.at.m:
                for h in range(2):
                    for i in range(2**j):
                        self.xcopy(ref, R, k, j, i, h).start()
            for h in range(2):
                for n in range(0 if j == 0 else 2 ** (j - 1), 2**j):
                    self.ccopy(ref, R, k, n, h).start()

        self.each(k, f)

    def arrived(self, k):
        def f(ref, R, land):
            for n in range(self.at.PL):
                for h in range(2):
                    self.ccopy(ref, R, k, n, h, True).wait_recv()

        self.each(k, f)

    def sent(self, k):
        def f(ref, R, land):
            for way in range(2):
                for h in range(self.at.S - 1):
                    pl.when(self.holds(way, h) & self.goes_on(way))(
                        lambda: self.zcopy(ref, R, land, k, way, h).wait_send())
            for h in range(2):
                for j in range(self.at.m):
                    for i in range(2**j):
                        self.xcopy(ref, R, k, j, i, h).wait_send()
                for n in range(self.at.PL):
                    self.ccopy(ref, R, k, n, h).wait_send()

        self.each(k, f)


def lanes128(r):
    return jnp.concatenate([r, jnp.zeros((r.shape[0], 128 - r.shape[1]), r.dtype)], axis=1)


def set_heads(heads, decay, bias, skips):
    rows = [bias[...], -jnp.exp(decay[...]), skips[...]]
    heads[...] = jnp.concatenate([lanes128(r) for r in rows] + [jnp.zeros((5, 128), f32)], axis=0)


def sigmoid(v):
    return 1.0 / (1.0 + jnp.exp(-v))


NT = ((1,), (1,))
TN = ((0,), (0,))


def dot(a, b, dims=((1,), (0,)), precision=None):
    return lax.dot_general(a, b, (dims, ((), ())), precision=precision, preferred_element_type=f32)


def halves(v):
    hi = v.astype(bf16)
    return hi, (v - hi.astype(f32)).astype(bf16)


def spread(cols, g6):
    T = cols.shape[0]
    low = lax.broadcasted_iota(jnp.int32, (T, 128), 1) < HDIM
    return jnp.concatenate(
        [
            jnp.where(
                low,
                jnp.broadcast_to(cols[:, 2 * q : 2 * q + 1], (T, 128)),
                jnp.broadcast_to(cols[:, 2 * q + 1 : 2 * q + 2], (T, 128)),
            )
            for q in range(GH // 2)
        ],
        axis=1,
    )


def turned(x, g):
    return pltpu.roll(x, lax.rem(128 - GH * g, 128), 1)


def convolve(x, cp):
    T = x.shape[0] - HALO
    mixed = cp[4:5] + cp[3:4] * x[HALO:]
    for k in range(CONV - 1):
        mixed = mixed + cp[k : k + 1] * pltpu.roll(x, CONV - 1 - k, 0)[HALO:]
    return mixed


def columns(count, first):
    ch = (lax.broadcasted_iota(jnp.int32, (1, CW), 1) + first).astype(f32)
    place = ch - count * jnp.floor((ch + 0.5) / count)
    return jnp.where(lax.broadcasted_iota(jnp.int32, (128, CW), 0).astype(f32) == place, 1.0, 0.0)


def prepare(s, raw, x, heads, cp, ld, ldT, gram):
    T = raw.shape[0]
    steps = jax.nn.softplus(raw + heads[0:1])
    tri = lax.broadcasted_iota(jnp.int32, (T, T), 0) >= lax.broadcasted_iota(jnp.int32, (T, T), 1)
    log_decay = dot(jnp.where(tri, 1.0, 0.0), steps * heads[1:2], precision=HIGH)
    ld[0, s] = log_decay
    ld[1, s] = steps
    turned_ld = log_decay.T
    for g in range(GROUPS):
        ldT[s, g, 0:GH] = turned_ld[g * GH : (g + 1) * GH]
    mixed = convolve(x, cp)[:, : 2 * STATE]
    act = mixed * sigmoid(mixed)
    keys, reads = act[:, :STATE], act[:, STATE:]
    gram[s] = dot(reads, keys, ((1,), (1,)), HIGH)
    return keys, reads, mixed


def fade(ldc, ldr, h, lo, n, m):
    gap = ldc[lo : lo + n, h : h + 1] - ldr[h : h + 1, :m]
    i = lax.broadcasted_iota(jnp.int32, (n, m), 0) + lo
    j = lax.broadcasted_iota(jnp.int32, (n, m), 1)
    return jnp.exp(jnp.where(i >= j, gap, -1e30))


def forward_kernel(S, PL, lengths, tok, win, cw, cb, ng_in, gg_in, decay, bias, skips, wout, cot,
                   out, owin, onormed, opc, oraw, oz, oy, ohin, ony, oconv, ogain, ossq, ong, odny, otsum, old, oldT, ogram, okeys2, oreadsT,
                   wi, wo, sm, zi, zo, halo, normed, ybuf, nyb, loc, hin, hout, dlast, gram, keysT, reads2, keys2, readsT,
                   ld, ldT, convp, gain, ngain, ssq, tsum, heads, pcs, zst, yst,
                   lsem, osem, hsem, ssem, pcsem, zsem, ysem, esem, nsem, cotsem, *sems):
    at = Place(S, PL)
    me = at.d * S + at.z
    seqs, T, _ = tok.shape
    rows = seqs * T
    n = 1 + NI + NO
    nd = S * PL * 2
    RI, RO = D // nd, DI // nd
    packed_i, packed_o = RI % 16 > 0, RO % 16 > 0

    def in_i(k):
        return (k >= 1) & (k < LATE) & ((k < MID) | (k >= GATE))

    def in_o(k):
        return ((k >= MID) & (k < GATE)) | ((k >= LATE) & (k < n))

    def chunk_i(k):
        return k - 1 - EARLY * lax.div(k, GATE)

    def chunk_o(k):
        return k - MID - GROUPS * lax.div(k, LATE)

    ga = Gather(at, sems, [
        (lambda k: k == 0, lambda k: sm, None, 16),
        (in_i, lambda k: wi.at[chunk_i(k)], (lambda k: zi.at[chunk_i(k)]) if packed_i else None, RI),
        (in_o, lambda k: wo.at[chunk_o(k)], (lambda k: zo.at[chunk_o(k)]) if packed_o else None, RO),
    ])

    def local(c):
        return pltpu.make_async_copy(
            wout.at[:, pl.ds(c * CW, CW)], zo.at[c, at.z] if packed_o else wo.at[c, pl.ds(me * RO, RO)], lsem.at[c])

    for c in range(NO):
        local(c).start()
    for j in range(NI):
        lane = 2 * DI if j == 0 else DI + (j - 1) * CW if j <= GROUPS else (j - 1 - GROUPS) * CW
        part = win[:, lane:] if j == 0 else win[:, lane : lane + CW]
        if j == 0:
            part = jnp.concatenate([part, jnp.zeros((part.shape[0], CW - part.shape[1]), bf16)], axis=1)
        if packed_i:
            zi[j, at.z] = part
        else:
            wi[j, pl.ds(pl.multiple_of(me * RI, 16), RI)] = part
    own = [lanes128(r[...].astype(f32)) for r in (cw, cb, ng_in, gg_in)] + [jnp.zeros((9, 128), f32)]
    sm[pl.ds(pl.multiple_of(me * 16, 16), 16)] = jnp.concatenate(own, axis=0).astype(bf16)
    set_heads(heads, decay, bias, skips)
    at.barrier()
    for c in range(NO):
        local(c).wait()

    def halo_copy():
        return remote(tok.at[:, pl.ds(T - HALO, HALO)], halo, hsem.at[0], hsem.at[1], at.along(1))

    @pl.when(at.z < S - 1)
    def _():
        halo_copy().start()

    @pl.when(at.z == 0)
    def _():
        halo[...] = jnp.zeros_like(halo)
        hin[...] = jnp.zeros_like(hin)

    @pl.when(at.z > 0)
    def _():
        halo_copy().wait_recv()

    ssq[...] = jnp.zeros_like(ssq)

    def chain(g):
        return remote(hout.at[g], hin.at[g], ssem.at[0, g], ssem.at[1, g], at.along(1))

    def normed_copies():
        return [pltpu.make_async_copy(normed.at[s, pl.ds(HALO, T), pl.ds(c * CW, CW)],
                                      onormed.at[c, pl.ds(s * T, T)], nsem.at[c, s])
                for c in range(D // CW) for s in range(seqs)]

    def unpack():
        gathered = sm[...]

        def rows_of(count, first):
            wide = dot(gathered, columns(count, first).astype(bf16)).reshape(nd, 16, CW)
            who = lax.broadcasted_iota(jnp.int32, (nd, 1, CW), 0) * count
            at_lane = lax.broadcasted_iota(jnp.int32, (nd, 1, CW), 2) + first
            wide = jnp.where((at_lane >= who) & (at_lane < who + count), wide, 0.0)
            return jnp.sum(wide, axis=0)[:8]

        def group(g, carry):
            convp[1 + g] = rows_of(CONV_CH // nd, g * CW)
            gain[g] = rows_of(DI // nd, g * CW)
            return carry

        lax.fori_loop(0, GROUPS, group, 0)
        convp[0] = rows_of(CONV_CH // nd, DI)
        ng = jnp.concatenate([rows_of(D // nd, g * CW)[5:6] for g in range(D // CW)], axis=1)
        ngain[...] = jnp.broadcast_to(ng, (8, D))
        pltpu.make_async_copy(ngain, ong, esem.at[4 + seqs]).start()
        for s in range(seqs):
            u = halo[s].astype(f32)
            r = lax.rsqrt(jnp.sum(u * u, axis=1, keepdims=True) * (1.0 / D) + EPS)
            normed[s, 0:HALO] = (u * r * ng).astype(bf16)
            for i in range(0, T, 64):
                u = tok[s, i : i + 64].astype(f32)
                r = lax.rsqrt(jnp.sum(u * u, axis=1, keepdims=True) * (1.0 / D) + EPS)
                normed[s, HALO + i : HALO + i + 64] = (u * r * ng).astype(bf16)
        for c in normed_copies():
            c.start()
        pltpu.make_async_copy(convp, oconv, esem.at[2 + seqs]).start()
        pltpu.make_async_copy(gain, ogain, esem.at[3 + seqs]).start()

    def project(w, first):
        x = normed[...] if first == 0 else normed[:, first:]
        return dot(x.reshape(seqs * x.shape[1], D), w).reshape(seqs, x.shape[1], CW)

    def keep_pc(pc, k, slot):
        pcs[slot] = pc
        pltpu.make_async_copy(pcs.at[slot], opc.at[k], pcsem.at[slot]).start()

    def prepared():
        pairs = ((ld, old), (ldT, oldT), (gram, ogram), (keys2, okeys2), (readsT, oreadsT))
        return [pltpu.make_async_copy(a, b, esem.at[seqs + 6 + i]) for i, (a, b) in enumerate(pairs)]

    def first_chunk():
        proj = project(wi[0], 0)
        pc = proj.astype(bf16)
        keep_pc(pc, 0, 0)
        raw = proj[:, HALO:, 2 * STATE :]
        zst[0, :, :, :128] = raw
        pltpu.make_async_copy(zst.at[0, :, :, pl.ds(0, 128)], oraw, zsem.at[0]).start()
        for s in range(seqs):
            keys, reads = prepare(s, raw[s], pc[s].astype(f32), heads, convp[0], ld, ldT, gram)[:2]
            keysT[s] = keys.T
            readsT[s] = reads.T
            reads2[s] = jnp.concatenate(halves(reads), axis=1)
            keys2[s] = jnp.concatenate(halves(keys), axis=1)
        for c in prepared():
            c.start()
        pltpu.make_async_copy(zst.at[0, :, :, pl.ds(0, 128)], oraw, zsem.at[0]).wait()

    def values_chunk(g, k):
        slot = lax.rem(k, 2)

        @pl.when(k >= 2)
        def _():
            pltpu.make_async_copy(pcs.at[slot], opc.at[k - 2], pcsem.at[slot]).wait()

        pc = project(wi[k], 0).astype(bf16)
        keep_pc(pc, k, slot)
        cp = convp[k]
        low = lax.broadcasted_iota(jnp.int32, (T // 2, 128), 1) < HDIM
        skip = spread(turned(jnp.broadcast_to(heads[2:3], (8, 128)), g), 0)[0:1]

        def sequence(s, carry):
            mixed = convolve(pcs[slot, s].astype(f32), cp)
            V = mixed * sigmoid(mixed)
            ldc = turned(ld[0, s], g)
            ldr = ldT[s, g]
            X = V * spread(turned(ld[1, s], g), g)
            lde = spread(ldc, g)
            last = lde[T - 1 : T]
            dlast[g, s] = jnp.broadcast_to(jnp.exp(last), (8, CW))
            loc[g, s] = dot(keysT[s], X * jnp.exp(last - lde), precision=HIGH)
            hi, lo = halves(X)
            H = T // 2
            for q in range(GH // 2):
                sl = slice(q * 128, q * 128 + 128)
                xs = jnp.concatenate([hi[:, sl], lo[:, sl]], axis=1)
                top, bot = [], []
                for h in (2 * q, 2 * q + 1):
                    mt, mt_low = halves(gram[s, :H, :H] * fade(ldc, ldr, h, 0, H, H))
                    mb, mb_low = halves(gram[s, H:, :] * fade(ldc, ldr, h, H, H, T))
                    r = dot(mt, xs[:H])
                    top.append(r[:, :128] + r[:, 128:] + dot(mt_low, xs[:H, :128]))
                    r = dot(mb, xs)
                    bot.append(r[:, :128] + r[:, 128:] + dot(mb_low, xs[:, :128]))
                ybuf[g, s, :H, sl] = jnp.where(low, top[0], top[1]) + skip[:, sl] * V[:H, sl]
                ybuf[g, s, H:, sl] = jnp.where(low, bot[0], bot[1]) + skip[:, sl] * V[H:, sl]
            return carry

        lax.fori_loop(0, seqs, sequence, 0)

    def pass_state(g):
        @pl.when(at.z > 0)
        def _():
            chain(g).wait_recv()

        @pl.when(at.z < S - 1)
        def _():
            for s in range(seqs):
                hout[g, s] = (dlast[g, s, 0:1] * hin[g, s].astype(f32) + loc[g, s]).astype(bf16)
            chain(g).start()

    def y_copy(i):
        a = lax.rem(i, 2)
        return pltpu.make_async_copy(yst.at[a], oy.at[lax.div(i, seqs), lax.rem(i, seqs)], ysem.at[a])

    def gate_chunk(g, k):
        slot = lax.rem(g, 2)

        @pl.when(g >= 2)
        def _():
            pltpu.make_async_copy(zst.at[slot], oz.at[g - 2], zsem.at[slot]).wait()

        zst[slot] = project(wi[k], HALO)
        pltpu.make_async_copy(zst.at[slot], oz.at[g], zsem.at[slot]).start()

        def sequence(s, carry):
            z = zst[slot, s]
            h2 = jnp.concatenate([hin[g, s], hin[g, s]], axis=0)
            carried = dot(reads2[s], h2) * jnp.exp(spread(turned(ld[0, s], g), g))
            y = ybuf[g, s] + carried
            i = g * seqs + s

            @pl.when(i >= 2)
            def _():
                y_copy(i - 2).wait()

            yst[lax.rem(i, 2)] = y
            y_copy(i).start()
            gated = y * (z * sigmoid(z))
            ybuf[g, s] = gated
            ssq[s] += jnp.broadcast_to(jnp.sum(gated * gated, axis=1, keepdims=True), (T, 128))
            return carry

        lax.fori_loop(0, seqs, sequence, 0)

        @pl.when(g == GROUPS - 1)
        def _():
            for c in normed_copies():
                c.wait()
            cot_copy().start()

    def cot_copy():
        return pltpu.make_async_copy(cot, normed.at[:, pl.ds(0, T)], cotsem.at[0])

    def live(s):
        pos = lax.broadcasted_iota(jnp.int32, (T, 1), 0) + at.z * T
        return jnp.where(pos < lengths[s], 1.0, 0.0)

    def normalise():
        for s in range(seqs):
            r = lax.rsqrt(ssq[s, :, 0:1] * (1.0 / DI) + EPS)
            for g in range(GROUPS):
                nyb[g, s * T : (s + 1) * T] = (ybuf[g, s] * r * gain[g, 6:7]).astype(bf16)
                ybuf[g, s] = jnp.zeros((T, CW), f32)
        pltpu.make_async_copy(nyb, ony, esem.at[seqs]).start()
        pltpu.make_async_copy(hin, ohin, esem.at[seqs + 1]).start()
        pltpu.make_async_copy(ssq, ossq, esem.at[seqs + 5]).start()
        cot_copy().wait()
        for s in range(seqs):
            normed[s, 0:T] = (live(s) * normed[s, 0:T].astype(f32)).astype(bf16)

    def out_chunk(c, carry):
        branch = jnp.zeros((rows, CW), f32)
        for g in range(0, GROUPS, 2):
            two = jnp.concatenate([nyb[g], nyb[g + 1]], axis=1)
            branch = branch + dot(two, wo[c, g * CW : (g + 2) * CW])
        branch = branch.reshape(seqs, T, CW)
        lane = pl.ds(pl.multiple_of(c * CW, 128), CW)
        masked = normed[:, 0:T, lane].reshape(rows, CW)
        for s in range(seqs):
            out[s, :, lane] = (tok[s, :, lane].astype(f32) + live(s) * branch[s]).astype(bf16)

        def upstream(g, carry):
            part = wo[c, pl.ds(pl.multiple_of(g * 2 * CW, 16), 2 * CW)]
            for s in range(seqs):
                both = dot(masked[s * T : (s + 1) * T], part, NT)
                ybuf[2 * g, s] += both[:, :CW]
                ybuf[2 * g + 1, s] += both[:, CW:]

            @pl.when(c == NO - 1)
            def _():
                two = pl.ds(2 * g, 2)
                pltpu.make_async_copy(ybuf.at[two], odny.at[two], esem.at[0]).start()

            return carry

        lax.fori_loop(0, GROUPS // 2, upstream, 0)

        @pl.when(c == NO - 1)
        def _():
            for s in range(seqs):
                t = jnp.zeros((T, 1), f32)
                for g in range(GROUPS):
                    t = t + jnp.sum(ybuf[g, s] * nyb[g, s * T : (s + 1) * T].astype(f32), axis=1, keepdims=True)
                tsum[s] = jnp.broadcast_to(t, (T, 128))
            pltpu.make_async_copy(tsum, otsum, esem.at[1]).start()

        return carry

    def keep(k, start):
        def f(src, dst):
            cp = pltpu.make_async_copy(src, dst, osem.at[k])
            cp.start() if start else cp.wait()

        @pl.when(in_i(k))
        def _():
            f(wi.at[chunk_i(k)], owin.at[chunk_i(k)])

    HOP = (GATE - 3) // (S - 1)
    last = at.m * LAG + 1

    def tick(t, carry):
        ga.send_z(t + S + SLACK)
        for h in range(1, S):
            ga.hop(t + S - h, h)
        for j in range(at.m + 1):
            ga.stage(t - j * LAG, j)
        k = t - last
        ga.arrived(k)
        keep(k, True)
        pl.when(k == 0)(unpack)
        pl.when(k == 1)(first_chunk)
        pl.when((k >= 2) & (k < MID))(lambda: values_chunk(k - 2, k - 1))
        g = k - 3 - HOP * at.z - lax.div(at.z, S - 1) * (GATE - 3 - HOP * (S - 1))
        pl.when((g >= 0) & (g < GROUPS))(lambda: pass_state(g))
        pl.when((k >= GATE) & (k < LATE))(lambda: gate_chunk(k - GATE, k - GATE + 1 + GROUPS))

        pl.when(k == LATE)(normalise)
        late = jnp.clip(k - LATE, -1, NO - EARLY - 1)
        begin = jnp.where(late > 0, late + EARLY, 0)
        end = jnp.where(late >= 0, late + EARLY + 1, 0)
        lax.fori_loop(begin, end, out_chunk, 0)

        return carry

    lax.fori_loop(-S - SLACK, n + last, tick, 0)

    def finish(k, carry):
        ga.sent(k)
        keep(k, False)
        return carry

    lax.fori_loop(0, n, finish, 0)

    @pl.when(at.z < S - 1)
    def _():
        halo_copy().wait_send()

        def f(g, carry):
            chain(g).wait_send()
            return carry

        lax.fori_loop(0, GROUPS, f, 0)

    for k in (GROUPS - 1, GROUPS):
        pltpu.make_async_copy(pcs.at[k % 2], opc.at[k], pcsem.at[k % 2]).wait()
    for g in (GROUPS - 2, GROUPS - 1):
        pltpu.make_async_copy(zst.at[g % 2], oz.at[g], zsem.at[g % 2]).wait()
    for c in prepared():
        c.wait()
    pltpu.make_async_copy(ybuf, odny, esem.at[0]).wait()
    pltpu.make_async_copy(tsum, otsum, esem.at[1]).wait()
    for i in (seqs * GROUPS - 2, seqs * GROUPS - 1):
        y_copy(i).wait()
    pltpu.make_async_copy(nyb, ony, esem.at[seqs]).wait()
    pltpu.make_async_copy(hin, ohin, esem.at[seqs + 1]).wait()
    pltpu.make_async_copy(convp, oconv, esem.at[seqs + 2]).wait()
    pltpu.make_async_copy(gain, ogain, esem.at[seqs + 3]).wait()
    pltpu.make_async_copy(ngain, ong, esem.at[seqs + 4]).wait()
    pltpu.make_async_copy(ssq, ossq, esem.at[seqs + 5]).wait()


def forward(S, dp, lengths, tok, win, wout, small, cot):
    PL = dp // 2
    nd = S * dp
    seqs, T, _ = tok.shape
    n = 1 + NI + NO
    rows = seqs * T
    sds = jax.ShapeDtypeStruct
    dma = pltpu.SemaphoreType.DMA
    V = pltpu.VMEM

    vm = pl.BlockSpec(memory_space=pltpu.VMEM)
    hb = pl.BlockSpec(memory_space=pl.ANY)
    wi_s, wo_s = (NI, D, CW), (NO, DI, CW)
    RI, RO = -(-(D // nd) // 16) * 16, -(-(DI // nd) // 16) * 16
    win = jnp.pad(win, ((0, RI - D // nd), (0, 0)))
    wout = jnp.pad(wout, ((0, RO - DI // nd), (0, 0)))
    zi_s = (NI, S, RI, CW) if RI * nd > D else (8, 128)
    zo_s = (NO, S, RO, CW) if RO * nd > DI else (8, 128)
    return pl.pallas_call(
        functools.partial(forward_kernel, S, PL),
        out_shape=[
            sds((seqs, T, D), bf16), sds(wi_s, bf16), sds((D // CW, rows, CW), bf16),
            sds((1 + GROUPS, seqs, HALO + T, CW), bf16), sds((seqs, T, 128), f32),
            sds((GROUPS, seqs, T, CW), f32), sds((GROUPS, seqs, T, CW), f32),
            sds((GROUPS, seqs, STATE, CW), bf16), sds((GROUPS, rows, CW), bf16),
            sds((1 + GROUPS, 8, CW), f32), sds((GROUPS, 8, CW), f32),
            sds((seqs, T, 128), f32), sds((8, D), f32), sds((GROUPS, seqs, T, CW), f32), sds((seqs, T, 128), f32),
            sds((2, seqs, T, 128), f32), sds((seqs, GROUPS, 8, T), f32), sds((seqs, T, T), f32),
            sds((seqs, T, 2 * STATE), bf16), sds((seqs, STATE, T), f32),
        ],
        in_specs=[pl.BlockSpec(memory_space=pltpu.SMEM)] + [vm] * 9 + [hb] * 2,
        out_specs=[vm] + [hb] * 19,
        scratch_shapes=[
            V(wi_s, bf16), V(wo_s, bf16), V((nd * 16, 128), bf16), V(zi_s, bf16), V(zo_s, bf16), V((seqs, HALO, D), bf16),
            V((seqs, HALO + T, D), bf16), V((GROUPS, seqs, T, CW), f32), V((GROUPS, rows, CW), bf16),
            V((GROUPS, seqs, STATE, CW), f32), V((GROUPS, seqs, STATE, CW), bf16),
            V((GROUPS, seqs, STATE, CW), bf16), V((GROUPS, seqs, 8, CW), f32), V((seqs, T, T), f32),
            V((seqs, STATE, T), f32), V((seqs, T, 2 * STATE), bf16), V((seqs, T, 2 * STATE), bf16),
            V((seqs, STATE, T), f32), V((2, seqs, T, 128), f32),
            V((seqs, GROUPS, 8, T), f32), V((1 + GROUPS, 8, CW), f32), V((GROUPS, 8, CW), f32), V((8, D), f32),
            V((seqs, T, 128), f32), V((seqs, T, 128), f32), V((8, 128), f32), V((2, seqs, HALO + T, CW), bf16),
            V((2, seqs, T, CW), f32), V((2, T, CW), f32),
            dma((NO,)), dma((n,)), dma((2,)), dma((2, GROUPS)), dma((2,)), dma((2,)), dma((2,)), dma((seqs + 11,)), dma((D // CW, seqs)), dma((1,)),
            dma((n, 2, S - 1)), dma((n, 2, S - 1)), dma((n, 2 * PL - 2)), dma((n, 2 * PL - 2)), dma((n, 2 * PL)), dma((n, 2 * PL)),
        ],
        name="forward",
        compiler_params=pltpu.CompilerParams(collective_id=0, has_side_effects=True, vmem_limit_bytes=63 << 20),
    )(lengths, tok, win, *small, wout, cot)


class Scatter:
    def __init__(self, at, R, bufs, sems):
        self.at, self.R, self.SR = at, R, at.S * R
        self.acc, self.cS, self.cR, self.xS, self.xR, self.zS, self.zR, self.zown = bufs
        self.cs, self.cr, self.xs, self.xr, self.zs, self.zr = sems
        self.NA, self.NS, self.NB = self.acc.shape[0], self.xS.shape[0], self.xR.shape[0]
        self.NC, self.MC = self.cR.shape[0], self.cS.shape[0]
        self.NZ, self.MZ = self.zR.shape[0], self.zS.shape[0]
        self.kind = self.xS.dtype

    def ccopy(self, k):
        at, i, o = self.at, lax.rem(k, self.MC), lax.rem(k, self.NC)
        return remote(self.cS.at[i], self.cR.at[o], self.cs.at[i], self.cr.at[o], (at.sib, at.z))

    def xcopy(self, k, j, i, h):
        at, n = self.at, 2**j - 1 + i
        a, b = lax.rem(k, self.NS), lax.rem(k, self.NB)
        return remote(self.xS.at[a, h, n], self.xR.at[b, h, n], self.xs.at[a, h, n], self.xr.at[b, h, n], at.across(j, h))

    def zcopy(self, k, o):
        at = self.at
        a, b = lax.rem(k, self.MZ), lax.rem(k, self.NZ)
        return remote(self.zS.at[a, lax.rem(at.z + o, at.S)], self.zR.at[b, o - 1], self.zs.at[a, o - 1],
                      self.zr.at[b, o - 1], at.along(o))

    def ready(self, k, slots, wait):
        if isinstance(k, int):
            if k >= slots:
                wait()
        else:
            pl.when(k >= slots)(wait)

    def produce(self, k, sibling, own):
        self.ready(k, self.MC, lambda: self.ccopy(k - self.MC).wait_send())
        a, n = lax.rem(k, self.MC), lax.rem(k, self.NA)
        sibling(self.cS.at[a])
        self.ccopy(k).start()
        own(self.acc.at[n])

    def send_x(self, k, j):
        at, n, a, half = self.at, lax.rem(k, self.NA), lax.rem(k, self.NS), self.SR // 2
        for h in range(2):
            for i in range(2**j):
                self.ready(k, self.NS, lambda: self.xcopy(k - self.NS, j, i, h).wait_send())
                q = flip(at.held(h, j)[i], at.weight(j, h))
                self.xS[a, h, 2**j - 1 + i] = self.acc[n, q, h * half : (h + 1) * half].astype(self.kind)
                self.xcopy(k, j, i, h).start()

    def stage_c(self, k):
        self.ccopy(k).wait_recv()
        n, o = lax.rem(k, self.NA), lax.rem(k, self.NC)
        for q in range(self.at.PL):
            self.acc[n, q] += self.cR[o, q]
        self.send_x(k, self.at.m - 1)

    def stage_x(self, k, j):
        at, n, b, half = self.at, lax.rem(k, self.NA), lax.rem(k, self.NB), self.SR // 2
        for h in range(2):
            for i in range(2**j):
                self.xcopy(k, j, i, h).wait_recv()
                q = at.held(h, j)[i]
                self.acc[n, q, h * half : (h + 1) * half] += self.xR[b, h, 2**j - 1 + i].astype(f32)
        if j > 0:
            self.send_x(k, j - 1)
            return
        a = lax.rem(k, self.MZ)
        for o in range(1, at.S):
            self.ready(k, self.MZ, lambda: self.zcopy(k - self.MZ, o).wait_send())
        v = self.acc[n, at.p]
        padded = self.zS.shape[2]
        if padded == self.R:
            self.zS[a] = v.astype(self.kind).reshape(at.S, self.R, v.shape[1])
        else:
            spread_rows = dot(picks(self.SR, self.R, padded), v.astype(bf16), ((0,), (0,)))
            self.zS[a] = spread_rows.astype(self.kind).reshape(at.S, padded, v.shape[1])
        for o in range(1, at.S):
            self.zcopy(k, o).start()
        if padded == self.R:
            own = self.acc[n, at.p, pl.ds(pl.multiple_of(at.z * self.R, 8), self.R)]
        else:
            i = lax.broadcasted_iota(jnp.int32, (padded, self.SR), 0)
            j = lax.broadcasted_iota(jnp.int32, (padded, self.SR), 1)
            mine = (i < self.R) & (j == i + at.z * self.R)
            own = dot(jnp.where(mine, 1.0, 0.0), v, precision=HIGH)
        self.zown[a] = own

    def stage_z(self, k):
        b = lax.rem(k, self.NZ)
        total = self.zown[lax.rem(k, self.MZ)]
        for o in range(1, self.at.S):
            self.zcopy(k, o).wait_recv()
            total = total + self.zR[b, o - 1].astype(f32)
        return total

    def drain(self, n):
        for k in range(max(0, n - self.MC), n):
            self.ccopy(k).wait_send()
        for k in range(max(0, n - self.NS), n):
            for h in range(2):
                for j in range(self.at.m):
                    for i in range(2**j):
                        self.xcopy(k, j, i, h).wait_send()
        for k in range(max(0, n - self.MZ), n):
            for o in range(1, self.at.S):
                self.zcopy(k, o).wait_send()


def scatter_scratch(S, PL, R, padded, width, kind, many, lag, zlag):
    m = PL.bit_length() - 1
    SR = S * R
    NS, NB, NC, NA, MZ, NZ = (lag + 1, 2 * lag, 2, 1 + m * lag, zlag + 1, 2 * zlag) if many else (1,) * 6
    V, dma = pltpu.VMEM, pltpu.SemaphoreType.DMA
    bufs = [
        V((NA, PL, SR, width), f32), V((1, PL, SR, width), f32), V((NC, PL, SR, width), f32),
        V((NS, 2, PL - 1, SR // 2, width), kind), V((NB, 2, PL - 1, SR // 2, width), kind),
        V((MZ, S, padded, width), kind), V((NZ, S - 1, padded, width), kind), V((MZ, padded, width), f32),
    ]
    sems = [dma((1,)), dma((NC,)), dma((NS, 2, PL - 1)), dma((NB, 2, PL - 1)), dma((MZ, S - 1)), dma((NZ, S - 1))]
    return bufs, sems


def pair(cols, q):
    T = cols.shape[0]
    low = lax.broadcasted_iota(jnp.int32, (T, 128), 1) < HDIM
    first = jnp.broadcast_to(cols[:, 2 * q : 2 * q + 1], (T, 128))
    second = jnp.broadcast_to(cols[:, 2 * q + 1 : 2 * q + 2], (T, 128))
    return jnp.where(low, first, second)


def pair_sums(v, q):
    hi = v.astype(bf16)
    rest = v - hi.astype(f32)
    mid = rest.astype(bf16)
    low = (rest - mid.astype(f32)).astype(bf16)
    ch = lax.broadcasted_iota(jnp.int32, (128, 128), 0)
    hd = lax.broadcasted_iota(jnp.int32, (128, 128), 1) - 2 * q
    ones = jnp.where((ch >= hd * HDIM) & (ch < hd * HDIM + HDIM), 1.0, 0.0).astype(bf16)
    return dot(jnp.concatenate([hi, mid, low], axis=1), jnp.concatenate([ones, ones, ones], axis=0))


def turned_back(x, g):
    return pltpu.roll(x, GH * g, 1)


def backward_kernel(S, PL, RLAG, ZLAG, lengths, decay, bias, skips, ngain, gain, convp, raw, ssq, tsum, ld, ldT, gram, keys2, readsT,
                    tok, cot, hin, norm_in, ny, win, zin, yin, dyin, pcin,
                    tgrad, ghead, gin, gout, gsm,
                    masked, lhsT, dyb, dzb, loc, dsin, dsout, dn, dgram, dkeys, dreads,
                    dld, dst, cvec, gvec, hvec, nxt, dcv, fin, heads, pc0, wib, zb, yb, db, hb, pcb,
                    wisem, zsem, ysem, dsem, hinsem, pcsem, setsem, finsem, chsem, hasem, *rest):
    at = Place(S, PL)
    seqs, T, _ = raw.shape
    rows = seqs * T
    nd = S * PL * 2
    R = D // nd
    SR = S * R
    H = T // 2
    NQ = 2 * GROUPS + 1 + 2 * NO
    big = Scatter(at, R, rest[:8], rest[8:14])
    tiny = Scatter(at, 16, rest[14:22], rest[22:28])
    sg = rest[28]
    HOP = 2 if S <= 4 else 1
    TB = 2 + HOP * (S - 1)

    def wi_copy(i):
        a = lax.rem(i, 2)
        k = 9 + i - 16 * lax.div(i, 8) + 7 * lax.div(i, 16)
        return pltpu.make_async_copy(win.at[k], wib.at[a], wisem.at[a])

    def item(i):
        return lax.rem(lax.div(i, seqs), GROUPS), lax.rem(i, seqs)

    def y_copy(i):
        a = lax.rem(i, 2)
        return pltpu.make_async_copy(yin.at[item(i)], yb.at[a], ysem.at[a])

    def zy_copies(i):
        a = lax.rem(i, 2)
        return (pltpu.make_async_copy(zin.at[item(i)], zb.at[a], zsem.at[a]),
                pltpu.make_async_copy(dyin.at[item(i)], db.at[a], dsem.at[a]), y_copy(i))

    def b_copies(g):
        a = lax.rem(g, 2)
        return (pltpu.make_async_copy(hin.at[g], hb.at[a], hinsem.at[a]),
                pltpu.make_async_copy(pcin.at[g + 1], pcb.at[a], pcsem.at[a]))

    def begin(copies, when=True):
        if when is True:
            for c in copies:
                c.start()
        else:
            @pl.when(when)
            def _():
                for c in copies:
                    c.start()

    NCH = D // CW
    setup = [pltpu.make_async_copy(cot, tgrad, setsem.at[0]), pltpu.make_async_copy(ny, dzb, setsem.at[1])]
    setup.append(pltpu.make_async_copy(pcin.at[0], pc0, setsem.at[2 + NCH]))
    setup += [pltpu.make_async_copy(norm_in.at[c], wib.at[c // 3, pl.ds(c % 3 * rows, rows)], setsem.at[2 + c])
              for c in range(NCH)]
    begin([*setup, *zy_copies(0), *b_copies(0)])
    set_heads(heads, decay, bias, skips)
    at.barrier()
    for c in setup:
        c.wait()

    for s in range(seqs):
        live = jnp.where(lax.broadcasted_iota(jnp.int32, (T, 1), 0) + at.z * T < lengths[s], 1.0, 0.0)
        masked[s * T : (s + 1) * T] = (live * tgrad[s].astype(f32)).astype(bf16)
    perm = lax.broadcasted_iota(jnp.int32, (2 * SR, 2 * SR), 0)
    perm_j = lax.broadcasted_iota(jnp.int32, (2 * SR, 2 * SR), 1)
    take = jnp.zeros(perm.shape, jnp.bool_)
    for h in range(2):
        for b in range(S):
            inside = (perm >= h * SR + b * R) & (perm < h * SR + b * R + R)
            take = take | (inside & (perm_j - (2 * b + h) * R == perm - (h * SR + b * R)))
    take = jnp.where(take, 1.0, 0.0).astype(bf16)
    same = jnp.where(lax.broadcasted_iota(jnp.int32, (SR, SR), 0) == lax.broadcasted_iota(jnp.int32, (SR, SR), 1),
                     1.0, 0.0).astype(bf16)
    for q in range(PL):
        for cls in range(2):
            cc = 1 - at.c if cls == 0 else at.c
            slab = 2 * q + cls
            for s in range(seqs):
                tl = slice(s * T, (s + 1) * T)
                lane = slab * 2 * SR
                r = dot(take, dzb[lane // CW, tl, lane % CW : lane % CW + 2 * SR], NT).astype(bf16)
                lhsT[0, cc, q * SR : (q + 1) * SR, tl] = r[:SR]
                lhsT[1, cc, q * SR : (q + 1) * SR, tl] = r[SR:]

    def turn_normed():
        for q in range(PL):
            for cls in range(2):
                cc = 1 - at.c if cls == 0 else at.c
                lane, c = (2 * q + cls) * SR % CW, (2 * q + cls) * SR // CW
                for s in range(seqs):
                    part = wib[c // 3, c % 3 * rows + s * T : c % 3 * rows + (s + 1) * T, lane : lane + SR]
                    lhsT[2, cc, q * SR : (q + 1) * SR, s * T : (s + 1) * T] = dot(same, part, NT).astype(bf16)
        begin([wi_copy(0)])


    for ref in (dn, dgram, dkeys, dreads, dld, dst, cvec, gvec, hvec, sg):
        ref[...] = jnp.zeros_like(ref)

    @pl.when(at.z == S - 1)
    def _():
        dsin[...] = jnp.zeros_like(dsin)
        nxt[...] = jnp.zeros_like(nxt)

    def rms(s):
        return lax.rsqrt(ssq[s, :, 0:1] * (1.0 / DI) + EPS)

    def through_gate(g, carry):
        def sequence(s, carry):
            i = g * seqs + s
            a = lax.rem(i, 2)
            for c in zy_copies(i):
                c.wait()
            begin(zy_copies(i + 1)[:2], i + 1 < seqs * GROUPS)
            begin([y_copy(i + 1)])
            r = rms(s)
            z, y, dn_y = zb[a], yb[a], db[a]
            sg_ = sigmoid(z)
            gate = z * sg_
            w = (y * gate) * r
            gvec[g, 6:7] += jnp.sum(dn_y * w, axis=0, keepdims=True)
            dw = r * (dn_y * gain[g, 6:7] - w * (tsum[s, :, 0:1] * (1.0 / DI)))
            dzb[g, pl.ds(pl.multiple_of(s * T, 16), T)] = (dw * y * (sg_ * (1.0 + z * (1.0 - sg_)))).astype(bf16)
            dy = dw * gate
            dyb[g, s] = dy
            loc[g, s] = dot(readsT[s], dy * jnp.exp(spread(turned(ld[0, s], g), g)), precision=HIGH)
            return carry

        lax.fori_loop(0, seqs, sequence, 0)
        return 0

    def chain(g):
        return remote(dsout.at[g], dsin.at[g], chsem.at[0, g], chsem.at[1, g], at.along(S - 1))

    def pass_state(g):
        @pl.when(at.z < S - 1)
        def _():
            chain(g).wait_recv()

        @pl.when(at.z > 0)
        def _():
            for s in range(seqs):
                last = jnp.exp(spread(turned(ld[0, s, T - 8 :], g), g))[7:8]
                dsout[g, s] = (last * dsin[g, s].astype(f32) + loc[g, s]).astype(bf16)
            chain(g).start()

    def edge(g):
        return remote(dyb.at[g, :, pl.ds(0, 8)], nxt.at[g], hasem.at[0, g], hasem.at[1, g], at.along(S - 1))

    def conv_sums(g, x, dm, lanes):
        x = x[:, :lanes]
        for k in range(CONV):
            shifted = x[HALO:] if k == CONV - 1 else pltpu.roll(x, CONV - 1 - k, 0)[HALO:]
            cvec[g, k : k + 1, :lanes] += jnp.sum(dm * shifted, axis=0, keepdims=True)
        cvec[g, CONV : CONV + 1, :lanes] += jnp.sum(dm, axis=0, keepdims=True)

    def recurrence(i, carry):
        g, s = lax.div(i, seqs), lax.rem(i, seqs)
        a = lax.rem(g, 2)

        @pl.when(s == 0)
        def _():
            for c in b_copies(g):
                c.wait()
            begin(b_copies(g + 1), g + 1 < GROUPS)

        y_copy(i).wait()
        begin([y_copy(i + 1)], i + 1 < seqs * GROUPS)

        cp = convp[g + 1]
        low = lax.broadcasted_iota(jnp.int32, (T, 128), 1) < HDIM
        is_last = lax.broadcasted_iota(jnp.int32, (T, 128), 0) == T - 1
        skips = turned(jnp.broadcast_to(heads[2:3], (8, 128)), g)
        ldc, ldr, stc = turned(ld[0, s], g), ldT[s, g], turned(ld[1, s], g)
        dgt, dgb = jnp.zeros((H, H), f32), jnp.zeros((H, T), f32)
        sums, dk, dr = jnp.zeros((2 * T, 128), f32), jnp.zeros((T, STATE), f32), jnp.zeros((T, STATE), f32)
        for q in range(GH // 2):
            sl = slice(q * 128, q * 128 + 128)
            skip = pair(skips, q)[0:1]
            x = pcb[a, s, :, sl].astype(f32)
            mixed = convolve(x, cp[:, sl])
            sg_ = sigmoid(mixed)
            V = mixed * sg_
            lde, st = pair(ldc, q), pair(stc, q)
            last = lde[T - 1 : T]
            tail = jnp.exp(last - lde)
            X = V * st
            dS, hq = dsin[g, s, :, sl], hb[a, s, :, sl]
            dXt = tail * dot(keys2[s], jnp.concatenate([dS, dS], axis=0))
            dY = dyb[g, s, :, sl]
            xh = X.astype(bf16)
            x2 = jnp.concatenate([xh, xh], axis=1)
            dyp = jnp.concatenate(halves(dY), axis=1)
            two = []
            for h in (2 * q, 2 * q + 1):
                ft = fade(ldc, ldr, h, 0, H, H)
                fb = fade(ldc, ldr, h, H, H, T)
                mt, mt_low = halves(gram[s, :H, :H] * ft)
                mb, mb_low = halves(gram[s, H:, :] * fb)
                r0 = dot(jnp.concatenate([mt, mb[:, :H]], axis=0), dyp, TN)
                r1 = dot(mb[:, H:], dyp[H:], TN)
                r = jnp.concatenate([r0, r1], axis=0)
                low0 = dot(jnp.concatenate([mt_low, mb_low[:, :H]], axis=0), dyp[:, :128], TN)
                low1 = dot(mb_low[:, H:], dyp[H:, :128], TN)
                two.append(r[:, :128] + r[:, 128:] + jnp.concatenate([low0, low1], axis=0))
                mine = low if h == 2 * q else jnp.logical_not(low)
                dyh = jnp.concatenate(halves(jnp.where(mine, dY, 0.0)), axis=1)
                dgt = dgt + ft * dot(dyh[:H], x2[:H], NT)
                dgb = dgb + fb * dot(dyh[H:], x2, NT)
            dX = jnp.where(low, two[0], two[1]) + dXt
            dV = st * dX + skip * dY
            gvec[g, 7:8, sl] += jnp.sum(dY * V, axis=0, keepdims=True)
            q1 = dY * (yb[lax.rem(i, 2), :, sl] - skip * V) - X * dX
            at_end = jnp.sum(X * dXt, axis=0, keepdims=True) + jnp.exp(last) * jnp.sum(
                hq.astype(f32) * dS.astype(f32), axis=0, keepdims=True)
            q1 = q1 + jnp.where(is_last, at_end, 0.0)
            sums = sums + pair_sums(jnp.concatenate([q1, dX * V], axis=0), q)
            dk = dk + dot(jnp.concatenate(halves(tail * X), axis=1), jnp.concatenate([dS, dS], axis=1), NT)
            dr = dr + dot(jnp.concatenate(halves(dY * jnp.exp(lde)), axis=1), jnp.concatenate([hq, hq], axis=1), NT)
            dm = dV * (sg_ * (1.0 + mixed * (1.0 - sg_)))
            dyb[g, s, :, sl] = dm
            for k in range(CONV):
                shifted = x[HALO:] if k == CONV - 1 else pltpu.roll(x, CONV - 1 - k, 0)[HALO:]
                cvec[g + 1, k : k + 1, sl] += jnp.sum(dm * shifted, axis=0, keepdims=True)
            cvec[g + 1, CONV : CONV + 1, sl] += jnp.sum(dm, axis=0, keepdims=True)
        dgram[s, :H, :H] += dgt
        dgram[s, H:, :] += dgb
        dld[s] += turned_back(sums[:T], g)
        dst[s] += turned_back(sums[T:], g)
        dkeys[s] += dk
        dreads[s] += dr

        @pl.when((at.z > 0) & (s == seqs - 1))
        def _():
            edge(g).start()

        return carry

    def unconvolve(dm, after, cp):
        ext = jnp.concatenate([dm, after], axis=0)
        n = ext.shape[0]
        out = cp[3:4] * dm
        for k in range(CONV - 1):
            out = out + cp[k : k + 1] * pltpu.roll(ext, n - (CONV - 1 - k), 0)[: dm.shape[0]]
        return out

    def heads_chunk():
        tri = lax.broadcasted_iota(jnp.int32, (T, T), 1) >= lax.broadcasted_iota(jnp.int32, (T, T), 0)
        tri = jnp.where(tri, 1.0, 0.0)
        cp = convp[0]
        for s in range(seqs):
            x = pc0[s].astype(f32)
            mixed = convolve(x, cp)[:, : 2 * STATE]
            sg_ = sigmoid(mixed)
            act = mixed * sg_
            keys, reads = act[:, :STATE], act[:, STATE:]
            dr = dreads[s] + dot(dgram[s], keys, precision=HIGH)
            dk = dkeys[s] + dot(dgram[s], reads, TN, HIGH)
            dm = jnp.concatenate([dk, dr], axis=1) * (sg_ * (1.0 + mixed * (1.0 - sg_)))
            conv_sums(0, x, dm, 2 * STATE)
            da = dot(tri, dld[s], precision=HIGH)
            draw = (dst[s] + da * heads[1:2]) * sigmoid(raw[s] + heads[0:1])
            hvec[0:1] += jnp.sum(da * ld[1, s], axis=0, keepdims=True) * heads[1:2]
            hvec[1:2] += jnp.sum(draw, axis=0, keepdims=True)
            zb[s] = jnp.concatenate([dm, draw], axis=1)

        @pl.when(at.z > 0)
        def _():
            kr_edge().start()

    def kr_edge():
        return remote(zb.at[:, pl.ds(0, 8)], nxt.at[GROUPS], hasem.at[0, GROUPS], hasem.at[1, GROUPS], at.along(S - 1))

    def terms(k):
        rhs = dcv[...]
        lhs = lhsT.at[jnp.minimum(lax.div(k, NO), 2)]

        def product(cc, ref):
            for lo in range(0, PL * SR, 384):
                ref[lo // SR : (lo + 384) // SR] = dot(lhs[cc, lo : lo + 384], rhs).reshape(384 // SR, SR, CW)

        def sibling(ref):
            product(0, ref)

        def own(ref):
            product(1, ref)

        big.produce(k, sibling, own)

    def back_in(i, d):
        wi_copy(i).wait()
        begin([wi_copy(i + 1)], i + 1 < 2 * GROUPS + 1)
        for lane in range(0, D, 512):
            dn[:, lane : lane + 512] += dot(d, wib[lax.rem(i, 2), lane : lane + 512], NT)

    def out_terms(k):
        c = lax.rem(k, NO)
        dcv[...] = masked[:, pl.ds(pl.multiple_of(c * CW, 128), CW)]

    def gate_terms(k):
        dcv[...] = dzb[k - 2 * NO]

    def value_terms(k):
        g = k - 2 * NO - GROUPS

        @pl.when(at.z < S - 1)
        def _():
            edge(g).wait_recv()

        cp = convp[g + 1]
        for s in range(seqs):
            dcv[s * T : (s + 1) * T] = unconvolve(dyb[g, s], nxt[g, s], cp).astype(bf16)

    def first_terms(k):
        @pl.when(at.z < S - 1)
        def _():
            kr_edge().wait_recv()

        cp = convp[0]
        for s in range(seqs):
            v = zb[s]
            c = unconvolve(v, nxt[GROUPS, s], cp)
            is_conv = lax.broadcasted_iota(jnp.int32, (T, CW), 1) < 2 * STATE
            dcv[s * T : (s + 1) * T] = jnp.where(is_conv, c, v).astype(bf16)

    def place(vec, count, first):
        lo, hi = first // count, min(nd - 1, (first + CW - 1) // count)
        who = (lax.broadcasted_iota(jnp.int32, (hi - lo + 1, 1, CW), 0) + lo) * count
        ch = lax.broadcasted_iota(jnp.int32, (hi - lo + 1, 1, CW), 2) + first
        wide = jnp.where((ch >= who) & (ch < who + count), vec[None], 0.0).reshape(-1, CW)
        cols = columns(count, first)
        sg[lo : hi + 1, 0:8] += dot(wide, cols, NT, HIGH).reshape(hi - lo + 1, 8, 128)

    def place_group(g):
        row = lax.broadcasted_iota(jnp.int32, (8, CW), 0)
        place(cvec[1 + g], CONV_CH // nd, g * CW)
        place(jnp.where(row == 6, gvec[g], 0.0), DI // nd, g * CW)
        per_head = pair_sums(gvec[g, :, :128], 0)
        for q in range(1, GH // 2):
            per_head = per_head + pair_sums(gvec[g, :, q * 128 : q * 128 + 128], q)
        hvec[2:3] += turned_back(per_head, g)[7:8]

    def ending():
        tok_copy().wait()
        ng = jnp.zeros((1, D), f32)
        for s in range(seqs):
            for i in range(0, T, 64):
                u = masked[s * T + i : s * T + i + 64].astype(f32)
                r = lax.rsqrt(jnp.sum(u * u, axis=1, keepdims=True) * (1.0 / D) + EPS)
                dnv = dn[s * T + i : s * T + i + 64]
                ng = ng + jnp.sum(dnv * u * r, axis=0, keepdims=True)
                v = dnv * ngain[0:1]
                mean = jnp.sum(v * u, axis=1, keepdims=True) * (1.0 / D)
                tgrad[s, i : i + 64] = (tgrad[s, i : i + 64].astype(f32) + r * v - u * (r * r * r * mean)).astype(bf16)
        row = lax.broadcasted_iota(jnp.int32, (8, CW), 0)
        place(cvec[0], CONV_CH // nd, DI)
        for g in range(D // CW):
            place(jnp.where(row == 5, ng[:, g * CW : (g + 1) * CW], 0.0), D // nd, g * CW)
        sg[:, 8:16] = jnp.broadcast_to(hvec[...][None], (nd, 8, 128))

        def sibling(ref):
            for q in range(PL):
                ref[q] = sg[pl.ds((2 * q + 1 - at.c) * S, S)].reshape(S * 16, 128)

        def own(ref):
            for q in range(PL):
                ref[q] = sg[pl.ds((2 * q + at.c) * S, S)].reshape(S * 16, 128)

        tiny.produce(0, sibling, own)

    def tok_copy():
        return pltpu.make_async_copy(tok, masked, setsem.at[0])

    def fin_copy(k, gate):
        a = lax.rem(k, 2)
        if gate:
            return pltpu.make_async_copy(fin.at[a], gin.at[:, pl.ds(pl.multiple_of((k - 2 * NO) * CW, 128), CW)], finsem.at[a])
        return pltpu.make_async_copy(
            fin.at[a], gout.at[lax.div(k, NO), :, pl.ds(pl.multiple_of(lax.rem(k, NO) * CW, 128), CW)], finsem.at[a])

    def each_fin(k, f):
        pl.when(k < 2 * NO)(lambda: f(fin_copy(k, False)))
        pl.when(k >= 2 * NO)(lambda: f(fin_copy(k, True)))

    def finish(k):
        @pl.when(k >= 2)
        def _():
            each_fin(k - 2, lambda c: c.wait())

        fin[lax.rem(k, 2)] = big.stage_z(k)
        each_fin(k, lambda c: c.start())

    m = at.m

    def inside(k):
        return (k >= 0) & (k < NQ)

    def tick(t, carry):
        pl.when(inside(t - 1 - m * RLAG - ZLAG))(lambda: finish(t - 1 - m * RLAG - ZLAG))
        for j in range(m):
            k = t - 1 - (m - j) * RLAG
            pl.when(inside(k))(lambda: big.stage_x(k, j))
        pl.when(inside(t - 1))(lambda: big.stage_c(t - 1))
        pl.when(t < 2 * NO)(lambda: out_terms(t))
        pl.when((t >= 2 * NO) & (t < 2 * NO + GROUPS))(lambda: gate_terms(t))
        pl.when((t >= 2 * NO + GROUPS) & (t < NQ - 1))(lambda: value_terms(t))
        pl.when(t == NQ - 1)(lambda: first_terms(t))
        pl.when(t < NQ)(lambda: terms(t))
        pl.when((t >= 2 * NO + GROUPS) & (t < NQ))(lambda: back_in(t - 2 * NO, dcv[...]))

        pl.when(t == 1)(turn_normed)

        @pl.when(t < GROUPS // 2)
        def _():
            lax.fori_loop(2 * t, 2 * t + 2, through_gate, 0)

        @pl.when((t >= GROUPS // 2) & (t < GROUPS))
        def _():
            def both(g, carry):
                back_in(g, dzb[g])
                return carry

            lax.fori_loop(2 * t - GROUPS, 2 * t - GROUPS + 2, both, 0)

        step = t - 1 - HOP * (S - 1 - at.z)
        passed = lax.div(4 * step + 6, 7)
        new = passed * 7 < 4 * step + 4
        pl.when((step >= 0) & new & (passed < GROUPS))(lambda: pass_state(passed))
        def parts_before(t):
            return lax.div(jnp.clip(t - TB, 0, NQ - 2 - TB) * seqs * GROUPS + NQ - 3 - TB, NQ - 2 - TB)

        lax.fori_loop(parts_before(t), parts_before(t + 1), recurrence, 0)
        pl.when(t == 2 * NO)(lambda: tok_copy().start())
        pl.when(t == NQ - 2)(heads_chunk)
        for g in range(GROUPS):
            pl.when(t == 2 * NO + GROUPS + g)(lambda: place_group(g))
        pl.when(t == NQ)(ending)
        pl.when(t == NQ + 1)(lambda: tiny.stage_c(0))
        for j in range(m):
            pl.when(t == NQ + 1 + m - j)(lambda: tiny.stage_x(0, j))
        return carry

    lax.fori_loop(0, NQ + 1 + max(1 + m, m * RLAG + ZLAG), tick, 0)
    total = tiny.stage_z(0)
    gsm[...] = total[:8]
    ghead[...] = total[8:]
    tiny.drain(1)
    big.drain(NQ)
    for k in (NQ - 2, NQ - 1):
        fin_copy(k, True).wait()

    def sent(g, carry):
        chain(g).wait_send()
        edge(g).wait_send()
        return carry

    @pl.when(at.z > 0)
    def _():
        lax.fori_loop(0, GROUPS, sent, 0)
        kr_edge().wait_send()


def backward(S, dp, lengths, tok, cot, small, saved):
    (owin, onormed, opc, oraw, oz, oy, ohin, ony, oconv, ogain, ossq, ong, odny, otsum, old, oldT, ogram, okeys2,
     oreadsT) = saved
    PL = dp // 2
    RLAG, ZLAG = (2, 3) if PL <= 4 else (1, 1)
    nd = S * dp
    R = D // nd
    Rp = -(-R // 16) * 16
    SR = S * R
    seqs, T, _ = tok.shape
    rows = seqs * T
    sds = jax.ShapeDtypeStruct
    dma = pltpu.SemaphoreType.DMA
    V = pltpu.VMEM
    vm = pl.BlockSpec(memory_space=pltpu.VMEM)
    hb = pl.BlockSpec(memory_space=pl.ANY)
    bufs, sems = scatter_scratch(S, PL, R, Rp, CW, bf16, True, RLAG, ZLAG)
    tbufs, tsems = scatter_scratch(S, PL, 16, 16, 128, f32, False, 1, 1)
    return pl.pallas_call(
        functools.partial(backward_kernel, S, PL, RLAG, ZLAG),
        out_shape=[sds((seqs, T, D), bf16), sds((8, 128), f32), sds((Rp, NI * CW), f32), sds((2, Rp, D), f32), sds((8, 128), f32)],
        in_specs=[pl.BlockSpec(memory_space=pltpu.SMEM)] + [vm] * 14 + [hb] * 10,
        out_specs=[vm, vm, hb, hb, vm],
        scratch_shapes=[
            V((rows, D), bf16), V((3, 2, PL * SR, rows), bf16),
            V((GROUPS, seqs, T, CW), f32), V((GROUPS, rows, CW), bf16), V((GROUPS, seqs, STATE, CW), f32),
            V((GROUPS, seqs, STATE, CW), bf16), V((GROUPS, seqs, STATE, CW), bf16), V((rows, D), f32),
            V((seqs, T, T), f32), V((seqs, T, STATE), f32), V((seqs, T, STATE), f32),
            V((seqs, T, 128), f32), V((seqs, T, 128), f32),
            V((1 + GROUPS, 8, CW), f32), V((GROUPS, 8, CW), f32), V((8, 128), f32),
            V((1 + GROUPS, seqs, 8, CW), f32), V((rows, CW), bf16),
            V((2, Rp, CW), f32), V((8, 128), f32), V((seqs, HALO + T, CW), bf16),
            V((2, D, CW), bf16), V((2, T, CW), f32), V((2, T, CW), f32), V((2, T, CW), f32),
            V((2, seqs, STATE, CW), bf16), V((2, seqs, HALO + T, CW), bf16),
            dma((2,)), dma((2,)), dma((2,)), dma((2,)), dma((2,)), dma((2,)), dma((3 + D // CW,)), dma((2,)), dma((2, GROUPS)), dma((2, GROUPS + 1)),
            *bufs, *sems, *tbufs, *tsems, V((nd, 16, 128), f32),
        ],
        name="backward",
        compiler_params=pltpu.CompilerParams(collective_id=1, has_side_effects=True, vmem_limit_bytes=127 << 19),
    )(lengths, *small[4:], ong, ogain, oconv, oraw, ossq, otsum, old, oldT, ogram, okeys2, oreadsT,
      tok.reshape(rows, D), cot, ohin, onormed, ony, owin, oz, oy, odny, opc)


def deliver_kernel(out, tgrad, gout, gin, gsm, ghead, *results):
    for src, dst in zip((out, tgrad, gout), results):
        dst[...] = src[...]
    results[3][...] = gin[:, :PROJ]
    cw, cb, ng, gg, decay, bias, skip = results[4:]
    cw[...] = gsm[0:CONV, : cw.shape[1]]
    for ref, r in ((cb, 4), (ng, 5), (gg, 6)):
        ref[...] = gsm[r : r + 1, : ref.shape[1]]
    for ref, r in ((decay, 0), (bias, 1), (skip, 2)):
        ref[...] = ghead[r : r + 1, : ref.shape[1]]


def deliver(nd, *arrays):
    sds = jax.ShapeDtypeStruct
    vm = pl.BlockSpec(memory_space=pltpu.VMEM)
    widths = (CONV_CH // nd, D // nd, DI // nd, HEADS, HEADS, HEADS)
    return pl.pallas_call(
        deliver_kernel,
        out_shape=[sds(a.shape, a.dtype) for a in arrays[:3]] + [sds((arrays[3].shape[0], PROJ), f32)] + [sds((CONV, CONV_CH // nd), f32)] + [sds((1, w), f32) for w in widths],
        in_specs=[vm] * 6,
        out_specs=[vm] * 11,
        name="deliver",
        compiler_params=pltpu.CompilerParams(vmem_limit_bytes=32 << 20),
    )(*arrays)


def body(tokens, lengths, in_weight, conv_weight, conv_bias, decay_log, step_bias, skip_gain, norm_gain, gate_gain,
         out_weight, cotangent):
    S, dp = lax.axis_size("seq"), lax.axis_size("dp")
    nd = S * dp
    row = lambda v: v.reshape(1, -1)
    small = [conv_weight.T, *map(row, (conv_bias, norm_gain, gate_gain, decay_log, step_bias, skip_gain))]
    out, *saved = forward(S, dp, lengths, tokens, in_weight, out_weight, small, cotangent)
    tgrad, ghead, gin, gout, gsm = backward(S, dp, lengths, tokens, cotangent, small, saved)
    R = D // nd
    if gin.shape[0] > R:
        gin, gout = gin[:R], gout[:, :R]
    out, tgrad, gout, gin, cw, *rows = deliver(nd, out, tgrad, gout, gin, gsm, ghead)
    cb, ng, gg, decay, bias, skip = (r.reshape(-1) for r in rows)
    return out, tgrad, gin, cw.T, cb, decay, bias, skip, ng, gg, gout.reshape(2 * R, D)


def solution(mesh):
    rows, own = P(AXES, None), P(AXES)
    toks = P("dp", "seq", None)
    return jax.shard_map(
        body, mesh=mesh,
        in_specs=(toks, P("dp"), rows, rows, own, P(), P(), P(), own, own, rows, toks),
        out_specs=(toks, toks, rows, rows, own, P(), P(), P(), own, own, rows),
        check_vma=False,
    )
```
